32 devices in a mesh: dp: 8 (over y, x, core), cont: 4 (over z).
Axes of the slice: x: 2, y: 2, z: 4, core: 2. Of those that a mesh axis runs over, the one named last changes fastest.
Arguments:
- prompt_x: bfloat16 [16, 1024, 512], P('dp', 'cont'), may hold values from -6 to 6
- cont_x: bfloat16 [16, 4, 128, 512], P('dp', 'cont'), may hold values from -6 to 6
- prompt_dy: bfloat16 [16, 1024, 512], P('dp', 'cont'), may hold values from -6 to 6
- cont_dy: bfloat16 [16, 4, 128, 512], P('dp', 'cont'), may hold values from -6 to 6
- teacher: bfloat16 [16, 4, 128, 512], P('dp', 'cont'), may hold values from -6 to 6
- cont_lengths: int32 [16, 4], P('dp', 'cont'), may hold values from 1 to 128, as said below
- loss_scale: float32 [], replicated, may hold values from 131072 to 524288
- norm1_gain: bfloat16 [512], P(('dp', 'cont')), may hold values from 0.5 to 1.5
- norm1_bias: bfloat16 [512], P(('dp', 'cont')), may hold values from -1.5 to 1.5
- w_query: bfloat16 [512, 512], P(('dp', 'cont')), may hold values from -0.375 to 0.375
- w_key: bfloat16 [512, 512], P(('dp', 'cont')), may hold values from -0.25 to 0.25
- w_value: bfloat16 [512, 512], P(('dp', 'cont')), may hold values from -0.25 to 0.25
- w_out: bfloat16 [512, 512], P(('dp', 'cont')), may hold values from -4 to 4
- norm2_gain: bfloat16 [512], P(('dp', 'cont')), may hold values from 0.5 to 1.5
- norm2_bias: bfloat16 [512], P(('dp', 'cont')), may hold values from -1.5 to 1.5
- w_up: bfloat16 [512, 2048], P(('dp', 'cont')), may hold values from -0.25 to 0.25
- up_bias: bfloat16 [2048], P(('dp', 'cont')), may hold values from -1.5 to 1.5
- w_down: bfloat16 [2048, 512], P(('dp', 'cont')), may hold values from -0.1875 to 0.1875
- down_bias: bfloat16 [512], P(('dp', 'cont')), may hold values from -1.5 to 1.5
Outputs:
- prompt_y: bfloat16 [16, 1024, 512], P('dp', 'cont')
- cont_y: bfloat16 [16, 4, 128, 512], P('dp', 'cont')
- loss: float32 [], replicated
- prompt_dx: float32 [16, 1024, 512], P('dp', 'cont')
- cont_dx: float32 [16, 4, 128, 512], P('dp', 'cont')
- grad_norm1_gain: float32 [512], P(('dp', 'cont'))
- grad_norm1_bias: float32 [512], P(('dp', 'cont'))
- grad_w_query: float32 [512, 512], P(('dp', 'cont'))
- grad_w_key: float32 [512, 512], P(('dp', 'cont'))
- grad_w_value: float32 [512, 512], P(('dp', 'cont'))
- grad_w_out: float32 [512, 512], P(('dp', 'cont'))
- grad_norm2_gain: float32 [512], P(('dp', 'cont'))
- grad_norm2_bias: float32 [512], P(('dp', 'cont'))
- grad_w_up: float32 [512, 2048], P(('dp', 'cont'))
- grad_up_bias: float32 [2048], P(('dp', 'cont'))
- grad_w_down: float32 [2048, 512], P(('dp', 'cont'))
- grad_down_bias: float32 [512], P(('dp', 'cont'))
The draws below stay inside these ranges and needn't reach their ends.
Inputs may be any that keep to these rules, and one draw needn't show every extreme that they name: `cont_lengths`: some continuation has length 128.
All inputs are finite; a program needn't handle non-finite values.
Results may differ from the reference program's by a relative error of at most 0.0095.
Values may be sent and summed in bfloat16 or wider, within the bound.
A program may use at most 192 MiB of HBM per device.

```python
import jax
import jax.numpy as jnp
from jax import lax

D = 512
HEADS = 8
HEAD_DIM = 64
FF = 2048
BLOCK = 16
CONT_LEN = 128
PROMPT = 1024
CONTS = 4
GROUPS = 16


def draw_cont_lengths(key, part):
    group_ids = jnp.arange(GROUPS, dtype=jnp.int32)
    upper_len = CONT_LEN // 4 + 3 * CONT_LEN // 4 * group_ids // max(GROUPS - 1, 1)
    lower_len = jnp.maximum(upper_len // 2, 1)
    lengths = jax.random.randint(key, (GROUPS, CONTS), lower_len[:, None], upper_len[:, None] + 1, dtype=jnp.int32)
    return lengths.at[GROUPS - 1, 0].set(CONT_LEN)


def rough_part(key, shape):
    return jax.random.normal(key, shape, jnp.float32)


def group_vectors(key):
    return jax.random.normal(jax.random.fold_in(key, 101), (GROUPS, D), jnp.float32)


def prompt_float(key):
    group_vec = group_vectors(key)
    block_vec = jax.random.normal(jax.random.fold_in(key, 102), (GROUPS, PROMPT // CONT_LEN, D), jnp.float32)
    block_rows = jnp.repeat(block_vec, CONT_LEN, axis=1)
    rows = 0.4 * group_vec[:, None, :] + 0.5 * block_rows + 0.75 * rough_part(jax.random.fold_in(key, 104), (GROUPS, PROMPT, D))
    return jnp.clip(rows, -6.0, 6.0)


def cont_float(key):
    group_vec = group_vectors(key)
    block_vec = jax.random.normal(jax.random.fold_in(key, 103), (GROUPS, CONTS, D), jnp.float32)
    noise = rough_part(jax.random.fold_in(key, 105), (GROUPS, CONTS, CONT_LEN, D))
    rows = 0.4 * group_vec[:, None, None, :] + 0.5 * block_vec[:, :, None, :] + 0.75 * noise
    return jnp.clip(rows, -6.0, 6.0)


def draw_prompt_x(key, part):
    return prompt_float(key).astype(jnp.bfloat16)


def draw_cont_x(key, part):
    return cont_float(key).astype(jnp.bfloat16)


def draw_prompt_dy(key, part):
    noise = rough_part(jax.random.fold_in(key, 106), (GROUPS, PROMPT, D))
    rows = 0.7 * prompt_float(key) + 0.7 * noise
    return jnp.clip(rows, -6.0, 6.0).astype(jnp.bfloat16)


def draw_cont_dy(key, part):
    noise = rough_part(jax.random.fold_in(key, 107), (GROUPS, CONTS, CONT_LEN, D))
    rows = 0.7 * cont_float(key) + 0.7 * noise
    return jnp.clip(rows, -6.0, 6.0).astype(jnp.bfloat16)


def block_scale(own_key, dims, shards, least, largest):
    gain = 1.0
    for dim, shards_of in shards:
        steps = jax.random.uniform(jax.random.fold_in(jax.random.fold_in(own_key, 6), dim), (shards_of,), jnp.float32, least / len(shards), largest / len(shards))
        gain = gain * jnp.repeat(jnp.exp(steps), dims[dim] // shards_of).reshape((-1,) + (1,) * (len(dims) - 1 - dim))
    return gain


def bell_draw(stream_key, shape, width, most, split=(), kind=jnp.bfloat16):
    array = width * jax.random.normal(stream_key, shape, jnp.float32)
    if split:
        array = array * block_scale(stream_key, shape, split, -0.22, 0.18)
    return jnp.clip(array, -most, most).astype(kind)


def setup_inputs(seed: int = 0) -> dict:
    keys = jax.random.split(jax.random.key(seed), 20)
    return {
        "prompt_x": draw_prompt_x(jax.random.fold_in(keys[19], 71), 0),
        "cont_x": draw_cont_x(jax.random.fold_in(keys[19], 71), 0),
        "prompt_dy": draw_prompt_dy(jax.random.fold_in(keys[19], 71), 0),
        "cont_dy": draw_cont_dy(jax.random.fold_in(keys[19], 71), 0),
        "teacher": bell_draw(keys[4], (GROUPS, CONTS, CONT_LEN, D), 1.0, 6.0, ((0, 8), (1, 4))),
        "cont_lengths": draw_cont_lengths(jax.random.fold_in(keys[19], 71), 0),
        "loss_scale": jnp.clip(jax.random.uniform(keys[6], (), jnp.float32, 131072.0, 524288.0), 131072.0, 524288.0),
        "norm1_gain": jnp.clip(1.0 + 0.1 * jax.random.normal(keys[7], (D,), jnp.float32), 0.5, 1.5).astype(jnp.bfloat16),
        "norm1_bias": bell_draw(keys[8], (D,), 0.3, 1.5, ((0, 32),)),
        "w_query": bell_draw(keys[9], (D, D), (D // 2) ** -0.5, 0.375, ((0, 32),)),
        "w_key": bell_draw(keys[10], (D, D), D ** -0.5, 0.25, ((0, 32),)),
        "w_value": bell_draw(keys[11], (D, D), D ** -0.5, 0.25, ((0, 32),)),
        "w_out": bell_draw(keys[12], (D, D), (max(D // 256, 1)) ** -0.5, 4.0, ((0, 32),)),
        "norm2_gain": jnp.clip(1.0 + 0.1 * jax.random.normal(keys[13], (D,), jnp.float32), 0.5, 1.5).astype(jnp.bfloat16),
        "norm2_bias": bell_draw(keys[14], (D,), 0.3, 1.5, ((0, 32),)),
        "w_up": bell_draw(keys[15], (D, FF), D ** -0.5, 0.25, ((0, 32),)),
        "up_bias": bell_draw(keys[16], (FF,), 0.3, 1.5, ((0, 32),)),
        "w_down": bell_draw(keys[17], (FF, D), (FF // 2) ** -0.5, 0.1875, ((0, 32),)),
        "down_bias": bell_draw(keys[18], (D,), 0.3, 1.5, ((0, 32),)),
    }


@jax.custom_vjp
def low(v):
    return lax.optimization_barrier(v.astype(jnp.bfloat16)).astype(jnp.float32)

@jax.custom_vjp
def low_back(v):
    return v

def low_keep(v):
    return (low(v), None)

def low_pass(kept, grad):
    return (grad,)

def back_keep(v):
    return (v, None)

def back_low(kept, grad):
    return (low(grad),)
low.defvjp(low_keep, low_pass)
low_back.defvjp(back_keep, back_low)
epsilon = 1e-05
largest_score = lax.Precision.HIGHEST

def matmul(left_rows, right_rows):
    return jnp.dot(left_rows, right_rows, precision=largest_score, preferred_element_type=jnp.float32)

def layer_norm(row_data, gain_vec, offset_vec):
    center = row_data - lax.optimization_barrier(jnp.mean(row_data, -1, keepdims=True))
    variance = lax.optimization_barrier(jnp.mean(center * center, -1, keepdims=True))
    return center * lax.rsqrt(variance + epsilon) * gain_vec + offset_vec

def divide_into_heads(row_data):
    return row_data.reshape(row_data.shape[:-1] + (HEADS, HEAD_DIM))

def pair_sum(row_data):
    old_shape = row_data.shape
    return row_data.reshape((old_shape[0], old_shape[1] // 2, 2) + old_shape[2:]).sum(2)

def coarse_sum(row_data):
    factor = CONT_LEN // BLOCK
    old_shape = row_data.shape
    return row_data.reshape(old_shape[:-2] + (old_shape[-2] // factor, factor, old_shape[-1])).sum(-2)

def diagonal_terms(query_tier_rows, key_level, value_level, count_level, logit_scale_factor):
    batch_blocks, positions = (query_tier_rows.shape[0], query_tier_rows.shape[1])
    blocks = positions // BLOCK
    query_block = query_tier_rows.reshape(batch_blocks, blocks, BLOCK, HEADS, HEAD_DIM)
    key_block = key_level.reshape(batch_blocks, blocks, BLOCK, HEADS, HEAD_DIM)
    value_block = value_level.reshape(batch_blocks, blocks, BLOCK, HEADS, HEAD_DIM)
    count_block = count_level.reshape(batch_blocks, blocks, BLOCK)
    causal = (jnp.arange(BLOCK)[:, None] >= jnp.arange(BLOCK)[None, :]).astype(jnp.float32)
    expo_scores = jnp.exp(jnp.einsum('abqhd,abkhd->abhqk', query_block, key_block, precision=largest_score) * logit_scale_factor) * causal
    numerator = jnp.einsum('abhqk,abkhd->abqhd', expo_scores, value_block, precision=largest_score)
    denominator = jnp.einsum('abhqk,abk->abqh', expo_scores, count_block, precision=largest_score)
    return (numerator.reshape(batch_blocks, positions, HEADS, HEAD_DIM), denominator.reshape(batch_blocks, positions, HEADS))

def sibling_terms(query_tier_rows, key_level, value_level, count_level, logit_scale_factor):
    batch_blocks, positions = (query_tier_rows.shape[0], query_tier_rows.shape[1])
    pair_count = positions // (2 * BLOCK)
    query_odd = query_tier_rows.reshape(batch_blocks, pair_count, 2, BLOCK, HEADS, HEAD_DIM)[:, :, 1]
    key_even = key_level.reshape(batch_blocks, pair_count, 2, BLOCK, HEADS, HEAD_DIM)[:, :, 0]
    value_even = value_level.reshape(batch_blocks, pair_count, 2, BLOCK, HEADS, HEAD_DIM)[:, :, 0]
    count_even = count_level.reshape(batch_blocks, pair_count, 2, BLOCK)[:, :, 0]
    expo_scores = jnp.exp(jnp.einsum('abqhd,abkhd->abhqk', query_odd, key_even, precision=largest_score) * logit_scale_factor)
    numerator = jnp.einsum('abhqk,abkhd->abqhd', expo_scores, value_even, precision=largest_score)
    denominator = jnp.einsum('abhqk,abk->abqh', expo_scores, count_even, precision=largest_score)
    numerator = jnp.stack([jnp.zeros_like(numerator), numerator], 2).reshape(batch_blocks, positions, HEADS, HEAD_DIM)
    denominator = jnp.stack([jnp.zeros_like(denominator), denominator], 2).reshape(batch_blocks, positions, HEADS)
    return (numerator, denominator)

def hier_attention(query_rows, key_rows, value_rows, valid_rows, distant_key_rows, distant_value_rows, distant_allow_mask):
    logit_scale_factor = HEAD_DIM ** (-0.5)
    batch_blocks, top_len = (query_rows.shape[0], query_rows.shape[1])
    query_tier_rows = divide_into_heads(query_rows)
    key_level = divide_into_heads(key_rows * valid_rows[..., None])
    value_level = divide_into_heads(value_rows * valid_rows[..., None])
    count_level = valid_rows
    numerator, denominator = diagonal_terms(query_tier_rows, key_level, value_level, count_level, logit_scale_factor)
    factor = 1
    while top_len // factor >= 2 * BLOCK:
        level_numerator, level_denominator = sibling_terms(query_tier_rows, key_level, value_level, count_level, logit_scale_factor)
        numerator = numerator + jnp.repeat(level_numerator, factor, axis=1)
        denominator = denominator + jnp.repeat(level_denominator, factor, axis=1)
        query_tier_rows = 0.5 * pair_sum(query_tier_rows)
        key_level = 0.5 * pair_sum(key_level)
        value_level = pair_sum(value_level)
        count_level = pair_sum(count_level)
        factor = factor * 2
    distant_score_rows = jnp.exp(jnp.einsum('cfgi,ugi->cgfu', query_tier_rows, divide_into_heads(distant_key_rows), precision=largest_score) * logit_scale_factor) * distant_allow_mask[:, None, None, :]
    upper_tier_numerator = jnp.einsum('ewcl,lwr->ecwr', distant_score_rows, divide_into_heads(distant_value_rows), precision=largest_score)
    top_denominator = float(factor) * jnp.transpose(lax.optimization_barrier(jnp.sum(distant_score_rows, axis=3)), (0, 2, 1))
    numerator = numerator + jnp.repeat(upper_tier_numerator, factor, axis=1)
    denominator = denominator + jnp.repeat(top_denominator, factor, axis=1)
    return (numerator / denominator[..., None]).reshape(batch_blocks, top_len, HEADS * HEAD_DIM)

def group_forward(params, prompt_rows, cont_rows, mask_rows):
    norm1_gain, norm1_bias, w_query, w_key, w_value, w_out, norm2_gain, norm2_bias, w_up, up_bias, w_down, down_bias = params
    coarse = CONT_LEN // BLOCK
    prompt_len = prompt_rows.shape[0]
    conts_all = cont_rows.shape[0]
    prompt_blocks = prompt_len // CONT_LEN
    far_len = prompt_len // coarse
    inputs = jnp.concatenate([prompt_rows, cont_rows.reshape(-1, D)], 0)
    normed_one = low(layer_norm(inputs, norm1_gain, norm1_bias))
    queries = low_back(low(matmul(normed_one, w_query)))
    key_all = low_back(low(matmul(normed_one, w_key)))
    value_all = low_back(low(matmul(normed_one, w_value)))
    distant_key_rows = low(coarse_sum(key_all[:prompt_len]) * (1.0 / coarse))
    distant_value_rows = low(coarse_sum(value_all[:prompt_len]))
    prompt_allow = (jnp.arange(far_len)[None, :] // BLOCK < jnp.arange(prompt_blocks)[:, None]).astype(jnp.float32)
    allow_all = jnp.concatenate([prompt_allow, jnp.ones((conts_all, far_len), jnp.float32)], 0)
    valid_all = jnp.concatenate([jnp.ones((prompt_blocks, CONT_LEN), jnp.float32), mask_rows], 0)
    shaped = (-1, CONT_LEN, D)
    attended = hier_attention(queries.reshape(shaped), key_all.reshape(shaped), value_all.reshape(shaped), valid_all, distant_key_rows, distant_value_rows, allow_all)
    attended = low(attended.reshape(-1, D))
    mixed = inputs + low_back(matmul(attended, w_out))
    normed_two = low(layer_norm(mixed, norm2_gain, norm2_bias))
    hidden = low(jax.nn.relu(low_back(matmul(normed_two, w_up) + up_bias)))
    output = mixed + low_back(matmul(hidden, w_down)) + down_bias
    return (output[:prompt_len], output[prompt_len:].reshape(conts_all, CONT_LEN, D))

def reference(prompt_x, cont_x, prompt_dy, cont_dy, teacher, cont_lengths, loss_scale, norm1_gain, norm1_bias, w_query, w_key, w_value, w_out, norm2_gain, norm2_bias, w_up, up_bias, w_down, down_bias):
    params = tuple((weight.astype(jnp.float32) for weight in (norm1_gain, norm1_bias, w_query, w_key, w_value, w_out, norm2_gain, norm2_bias, w_up, up_bias, w_down, down_bias)))
    valid = (jnp.arange(CONT_LEN, dtype=jnp.int32)[None, None, :] < cont_lengths[:, :, None]).astype(jnp.float32)
    token_count = jnp.sum(valid)
    teacher_f = teacher.astype(jnp.float32)

    def forward_all(weights, prompt_all, cont_all):

        def scan_step(square_total, pieces):
            prompt_rows, cont_rows, mask_rows, teach_rows = pieces
            prompt_out, cont_out = jax.checkpoint(group_forward)(weights, prompt_rows, cont_rows, mask_rows)
            difference = cont_out - teach_rows
            return (square_total + jnp.sum(mask_rows[..., None] * difference * difference), (prompt_out, cont_out))
        square_total, (prompt_out, cont_out) = lax.scan(scan_step, jnp.zeros((), jnp.float32), (prompt_all, cont_all, valid, teacher_f))
        return (prompt_out, cont_out, square_total)
    (prompt_y, cont_y, square_total), pullback = jax.vjp(forward_all, params, prompt_x.astype(jnp.float32), cont_x.astype(jnp.float32))
    scale_all = token_count * D
    loss_value = square_total / scale_all
    grads, prompt_dx, cont_dx = pullback((prompt_dy.astype(jnp.float32), cont_dy.astype(jnp.float32), loss_scale / scale_all))
    return (prompt_y.astype(jnp.bfloat16), cont_y.astype(jnp.bfloat16), loss_value, prompt_dx, cont_dx, grads[0], grads[1], grads[2], grads[3], grads[4], grads[5], grads[6], grads[7], grads[8], grads[9], grads[10], grads[11])
```

```python
import functools
import types

import jax
import jax.numpy as jnp
from jax import lax
from jax.experimental import pallas as pl
from jax.experimental.pallas import tpu as pltpu
from jax.sharding import PartitionSpec as P

D = 512
HEADS = 8
HEAD_DIM = 64
FF = 2048
BLOCK = 16
CONT_LEN = 128
COARSE = CONT_LEN // BLOCK
PAIRS = HEADS // 2
EPS = 1e-5
SCORE = HEAD_DIM**-0.5
LOG2E = 1.4426950408889634
AWAY = -1e30
F32 = jnp.float32
BF16 = jnp.bfloat16
MESH = pl.DeviceIdType.MESH
LANES = 128


def nn(a, b):
    return jnp.dot(a, b, preferred_element_type=F32)


def nt(a, b):
    return lax.dot_general(a, b, (((1,), (1,)), ((), ())), preferred_element_type=F32)


def tn(a, b):
    return lax.dot_general(a, b, (((0,), (0,)), ((), ())), preferred_element_type=F32)


def iota(shape, dim):
    return lax.broadcasted_iota(jnp.int32, shape, dim)


def norm_stats(x):
    center = x - jnp.mean(x, -1, keepdims=True)
    rstd = lax.rsqrt(jnp.mean(center * center, -1, keepdims=True) + EPS)
    return center * rstd, rstd


def norm_back(xhat, rstd, gain, dn):
    dxhat = dn * gain
    mean_one = jnp.mean(dxhat, -1, keepdims=True)
    mean_two = jnp.mean(dxhat * xhat, -1, keepdims=True)
    return rstd * (dxhat - mean_one - xhat * mean_two)


def colsum(x):
    return jnp.sum(x, 0, keepdims=True)


class Sizes:
    def __init__(self, groups, prompt, conts, nz, exchange, ndev):
        self.groups = groups
        self.prompt = prompt
        self.conts = conts
        self.nz = nz
        self.exchange = exchange
        self.ndev = ndev
        self.nb = prompt // CONT_LEN
        self.tb = self.nb + conts
        self.rows_g = self.tb * CONT_LEN
        self.rows = groups * self.rows_g
        self.blocks = groups * self.tb
        self.far_own = prompt // COARSE
        self.far = self.far_own * nz
        self.r = D // ndev
        self.rf = FF // ndev


def kernel(s, names, *refs):
    r = types.SimpleNamespace(**dict(zip(names, refs)))
    z = lax.axis_index("cont")
    dp = lax.axis_index("dp")
    zs = [lax.rem(z + d, s.nz) for d in range(1, s.nz)]
    pending = []

    def remote(src, dst, ssem, rsem, dev):
        return pltpu.make_async_remote_copy(
            src_ref=src, dst_ref=dst, send_sem=ssem, recv_sem=rsem, device_id=dev, device_id_type=MESH
        )

    def send(src, dst, ssem, rsem, dev):
        copy = remote(src, dst, ssem, rsem, dev)
        copy.start()
        pending.append(copy)

    def wait_recv(dst, ssem, rsem, dev):
        remote(dst, dst, ssem, rsem, dev).wait_recv()

    local_count = [0]

    def local(src, dst):
        copy = pltpu.make_async_copy(src, dst, r.lsem.at[local_count[0]])
        local_count[0] += 1
        copy.start()
        return copy

    def rows_in(prompt, cont, dst):
        out = []
        for g in range(s.groups):
            base = g * s.rows_g
            out.append(local(prompt.at[g], dst.at[pl.ds(base, s.prompt)]))
            for c in range(s.conts):
                out.append(local(cont.at[g, c], dst.at[pl.ds(base + s.prompt + c * CONT_LEN, CONT_LEN)]))
        return out

    if s.exchange:
        core = lax.rem(dp, 2)
        ix = lax.rem(dp // 2, 2)
        iy = dp // 4
        sib = dp + 1 - 2 * core
        xn = dp + 2 - 4 * ix
        yn = dp + 4 - 8 * iy
        cell = dp // 2
        cell_x = cell + 1 - 2 * ix
        cell_y = cell + 2 - 4 * iy
        cell_d = cell_x + cell_y - cell
        sibcore = 1 - core
        other = dp + sib - dp
        del other
        me = dp * s.nz + z

        def sq(first, count):
            return lambda a, n: r.w4.at[pl.ds(first, count), pl.ds(pl.multiple_of(a * s.r, s.r), n * s.r)]

        slicers = [
            lambda a, n: r.tiles.at[pl.ds(a, n)],
            sq(0, 3),
            sq(3, 1),
            lambda a, n: r.wu.at[pl.ds(pl.multiple_of(a * s.r, s.r), n * s.r)],
            lambda a, n: r.wd.at[pl.ds(pl.multiple_of(a * s.rf, s.rf), n * s.rf)],
        ]

        def zset(cell_id, core_id):
            return (cell_id * 2 + core_id) * s.nz

        half = s.nz // 2

        def ag0(k):
            for zz in zs:
                own = slicers[k](me, 1)
                send(own, own, r.ags.at[k, zz], r.agr.at[k, z], (dp, zz))

        def ag1(k):
            for zz in zs:
                wait_recv(slicers[k](dp * s.nz + zz, 1), r.ags.at[k, zz], r.agr.at[k, zz], (dp, zz))
            own = slicers[k](zset(cell, core), s.nz)
            send(own, own, r.ags.at[k, 4], r.agr.at[k, 4], (xn, z))
            send(own, own, r.ags.at[k, 5], r.agr.at[k, 5], (yn, z))
            send(own, own, r.ags.at[k, 8], r.agr.at[k, 8], (sib, z))

        def ag2(k):
            xset = slicers[k](zset(cell_x, core), s.nz)
            yset = slicers[k](zset(cell_y, core), s.nz)
            wait_recv(xset, r.ags.at[k, 4], r.agr.at[k, 4], (xn, z))
            lo = slicers[k](zset(cell_x, core), half)
            send(lo, lo, r.ags.at[k, 6], r.agr.at[k, 6], (yn, z))
            send(xset, xset, r.ags.at[k, 9], r.agr.at[k, 9], (sib, z))
            wait_recv(yset, r.ags.at[k, 5], r.agr.at[k, 5], (yn, z))
            hi = slicers[k](zset(cell_y, core) + half, half)
            send(hi, hi, r.ags.at[k, 7], r.agr.at[k, 7], (xn, z))
            send(yset, yset, r.ags.at[k, 10], r.agr.at[k, 10], (sib, z))

        def ag3(k):
            lo = slicers[k](zset(cell_d, core), half)
            hi = slicers[k](zset(cell_d, core) + half, half)
            wait_recv(lo, r.ags.at[k, 6], r.agr.at[k, 6], (yn, z))
            wait_recv(hi, r.ags.at[k, 7], r.agr.at[k, 7], (xn, z))
            both = slicers[k](zset(cell_d, core), s.nz)
            send(both, both, r.ags.at[k, 11], r.agr.at[k, 11], (sib, z))

        def ag4(k):
            for i, c in enumerate((cell, cell_x, cell_y, cell_d)):
                wait_recv(slicers[k](zset(c, sibcore), s.nz), r.ags.at[k, 8 + i], r.agr.at[k, 8 + i], (sib, z))

        grads = [(r.gq, r.rcq, r.rdq, r.rxq, r.rzq), (r.go, r.rco, r.rdo, r.rxo, r.rzo),
                 (r.gu, r.rcu, r.rdu, r.rxu, r.rzu), (r.gd, r.rcd, r.rdd, r.rxd, r.rzd)]

        def rs0(k):
            g, rc, _, _, _ = grads[k]
            send(g.at[:, :, sibcore], rc, r.rss.at[k, 0], r.rsr.at[k, 0], (sib, z))

        def add_to(g, j, c, lo, n, term):
            place = (j, c, core, pl.ds(lo, n))
            g[place] = (g[place].astype(F32) + term).astype(BF16)

        def rs1(k):
            g, rc, rd, _, _ = grads[k]
            nj, m = g.shape[0], g.shape[3]
            wait_recv(rc, r.rss.at[k, 0], r.rsr.at[k, 0], (sib, z))
            for j in range(nj):
                add_to(g, j, cell_d, 0, m, rc[j, cell_d].astype(F32))
            mh = m // 2
            send(g.at[:, cell_d, core, pl.ds(0, mh)], rd.at[0], r.rss.at[k, 1], r.rsr.at[k, 1], (yn, z))
            send(g.at[:, cell_d, core, pl.ds(mh, mh)], rd.at[1], r.rss.at[k, 2], r.rsr.at[k, 2], (xn, z))
            for c in (cell_x, cell_y, cell):
                for j in range(nj):
                    add_to(g, j, c, 0, m, rc[j, c].astype(F32))

        def rs2(k):
            g, _, rd, rx, _ = grads[k]
            nj, m = g.shape[0], g.shape[3]
            mh = m // 2
            wait_recv(rd.at[0], r.rss.at[k, 1], r.rsr.at[k, 1], (yn, z))
            for j in range(nj):
                add_to(g, j, cell_x, 0, mh, rd[0, j].astype(F32))
            send(g.at[:, cell_x, core], rx.at[0], r.rss.at[k, 3], r.rsr.at[k, 3], (xn, z))
            wait_recv(rd.at[1], r.rss.at[k, 2], r.rsr.at[k, 2], (xn, z))
            for j in range(nj):
                add_to(g, j, cell_y, mh, mh, rd[1, j].astype(F32))
            send(g.at[:, cell_y, core], rx.at[1], r.rss.at[k, 4], r.rsr.at[k, 4], (yn, z))

        def piece(g, zz):
            n = g.shape[3] // s.nz
            return pl.ds(pl.multiple_of(zz * n, n), n)

        def rs3(k):
            g, _, _, rx, rz = grads[k]
            nj, m = g.shape[0], g.shape[3]
            wait_recv(rx.at[0], r.rss.at[k, 3], r.rsr.at[k, 3], (xn, z))
            wait_recv(rx.at[1], r.rss.at[k, 4], r.rsr.at[k, 4], (yn, z))
            for j in range(nj):
                add_to(g, j, cell, 0, m, rx[0, j].astype(F32) + rx[1, j].astype(F32))
            for zz in zs:
                send(g.at[:, cell, core, piece(g, zz)], rz.at[z], r.rss.at[k, 5 + zz], r.rsr.at[k, 5 + z], (dp, zz))

        def rs4(k, outs):
            g, _, _, _, rz = grads[k]
            for zz in zs:
                wait_recv(rz.at[zz], r.rss.at[k, 5 + zz], r.rsr.at[k, 5 + zz], (dp, zz))
            for j, out in enumerate(outs):
                total = g[j, cell, core, piece(g, z)].astype(F32)
                for zz in zs:
                    total = total + rz[zz, j].astype(F32)
                out[...] = total
    else:

        def nothing(*_):
            return None

        ag0 = ag1 = ag2 = ag3 = ag4 = rs0 = rs1 = rs2 = rs3 = rs4 = nothing

    if s.exchange:
        weights_in = [
            local(r.wq, r.w4.at[0, pl.ds(pl.multiple_of(me * s.r, s.r), s.r)]),
            local(r.wk, r.w4.at[1, pl.ds(pl.multiple_of(me * s.r, s.r), s.r)]),
            local(r.wv, r.w4.at[2, pl.ds(pl.multiple_of(me * s.r, s.r), s.r)]),
            local(r.wo, r.w4.at[3, pl.ds(pl.multiple_of(me * s.r, s.r), s.r)]),
            local(r.wup, slicers[3](me, 1)),
            local(r.wdn, slicers[4](me, 1)),
        ]
    else:
        weights_in = [local(w, r.w4.at[j]) for j, w in enumerate((r.wq, r.wk, r.wv, r.wo))]
        weights_in += [local(r.wup, r.wu), local(r.wdn, r.wd)]
    x_in = rows_in(r.px, r.cx, r.x)
    later_in = rows_in(r.pdy, r.cdy, r.dy) + [
        local(r.te.at[g, c], r.teach.at[g * s.conts + c]) for g in range(s.groups) for c in range(s.conts)
    ]

    barrier = pltpu.get_barrier_semaphore()
    partners = [(dp, zz) for zz in zs]
    if s.exchange:
        partners += [(sib, z), (xn, z), (yn, z)]
    for dev in partners:
        pl.semaphore_signal(barrier, inc=1, device_id=dev, device_id_type=MESH)

    if s.exchange:
        r.build[...] = jnp.zeros_like(r.build)
        for i, v in enumerate((r.v1g, r.v1b, r.v2g, r.v2b, r.vdb)):
            r.build[pl.ds(i, 1), pl.ds(0, s.r)] = v[...].astype(F32)
        r.build[pl.ds(5, 1), pl.ds(0, s.rf)] = r.vub[...].astype(F32)
        own_tokens = 0
        for g in range(s.groups):
            for c in range(s.conts):
                own_tokens = own_tokens + r.lens[g, c]
        tile = r.build[...]
        row = iota((8, LANES), 0)
        placed = jnp.where(
            row < 5,
            pltpu.roll(tile, lax.rem(me, LANES // s.r) * s.r, 1),
            pltpu.roll(tile, lax.rem(me, LANES // s.rf) * s.rf, 1),
        )
        r.tiles[me] = jnp.where(row == 6, own_tokens.astype(F32), placed)

    lane_lo = iota((CONT_LEN, LANES), 1) < HEAD_DIM
    ri = iota((3 * CONT_LEN, CONT_LEN), 0)
    ci = iota((3 * CONT_LEN, CONT_LEN), 1)
    level = ri // CONT_LEN + 1
    rep = jnp.where(((ri % CONT_LEN) >> level) == (ci >> level), 1.0, 0.0)
    scale_l = jnp.where(level == 1, 0.5, jnp.where(level == 2, 0.25, 0.125))
    r.rep[...] = (rep * scale_l).astype(BF16)
    ri = iota((64, CONT_LEN), 0)
    ci = iota((64, CONT_LEN), 1)
    coarse_ci = jnp.where(ri < 32, ci >> 1, jnp.where(ri < 48, ci >> 2, ci >> 3))
    position = jnp.where(ri < 16, ri, jnp.where(ri < 32, ri + 16, jnp.where(ri < 48, ri - 32, ri - 48)))
    r.pool[...] = jnp.where(coarse_ci == position, 1.0, 0.0).astype(BF16)
    ri = iota((CONT_LEN, CONT_LEN), 0)
    ci = iota((CONT_LEN, CONT_LEN), 1)
    bi, bj = ri >> 4, ci >> 4
    near = ((bi == bj) & (ci <= ri)) | (((bi & 1) == 1) & (bj == bi - 1))
    r.bias0[...] = jnp.where(near, 0.0, AWAY)
    ri = iota((CONT_LEN, 64), 0)
    ci = iota((CONT_LEN, 64), 1)
    reader = jnp.where(ci < 32, ri >> 5, ri >> 6)
    wanted = jnp.where(ci < 16, 1, jnp.where(ci < 32, 3, jnp.where(ci < 48, 1, 9)))
    r.bias1[...] = jnp.where(reader == wanted, 0.0, AWAY)
    r.vg[...] = jnp.zeros_like(r.vg)
    r.df[...] = jnp.zeros_like(r.df)

    for copy in weights_in:
        copy.wait()
    pl.semaphore_wait(barrier, len(partners))

    if s.exchange:
        for k in range(5):
            ag0(k)
        ag1(0)
        ag1(1)
        ag2(0)
        ag2(1)
        ag3(0)
        ag3(1)
        ag4(0)
        count = 8
        for k in range(s.ndev // count):
            part = jnp.sum(r.tiles[pl.ds(k * count, count)], 0)
            r.vec[:, pl.ds(k * LANES, LANES)] = part
        for k in range(s.ndev // 2):
            part = r.tiles[2 * k] + r.tiles[2 * k + 1]
            r.upb[:, pl.ds(k * LANES, LANES)] = part[5:6]
        ag1(2)
    else:
        r.vec[...] = r.vecs[...]
        r.upb[...] = r.upbs[...]

    def vec(i):
        return r.vec[pl.ds(i, 1), :]

    token_row = r.vec[pl.ds(6, 1), pl.ds(0, LANES)]
    for k in range(1, D // LANES):
        token_row = token_row + r.vec[pl.ds(6, 1), pl.ds(k * LANES, LANES)]
    token_row = jnp.concatenate([token_row] * (D // LANES), 1)

    def length_of(g, b):
        c = jnp.clip(b - s.nb, 0, s.conts - 1)
        return jnp.where(b >= s.nb, r.lens[g, c], CONT_LEN)

    for copy in x_in:
        copy.wait()

    def norm_one(i, carry):
        rows = pl.ds(pl.multiple_of(i * CONT_LEN, CONT_LEN), CONT_LEN)
        xhat, _ = norm_stats(r.x[rows].astype(F32))
        r.n1[rows] = (xhat * vec(0) + vec(1)).astype(BF16)
        return carry

    lax.fori_loop(0, s.blocks, norm_one, 0)
    ag1(3)
    ag4(1)

    def project(t, carry):
        g, b = t // s.tb, lax.rem(t, s.tb)
        rows = pl.ds(pl.multiple_of(t * CONT_LEN, CONT_LEN), CONT_LEN)
        n1 = r.n1[rows]
        keep = iota((CONT_LEN, D), 0) < length_of(g, b)
        qv = nn(n1, r.w4[0]).astype(BF16)
        kv = jnp.where(keep, nn(n1, r.w4[1]), 0.0).astype(BF16)
        vv = jnp.where(keep, nn(n1, r.w4[2]), 0.0).astype(BF16)
        r.q[rows] = qv
        r.k[rows] = kv
        r.v[rows] = vv
        pr = iota((64, D), 0)
        mean_scale = jnp.where(pr < 32, 0.5, jnp.where(pr < 48, 0.25, 0.125))
        r.kl[t] = (nn(r.pool[...], kv) * mean_scale).astype(BF16)
        r.vl[t] = nn(r.pool[...], vv).astype(BF16)
        return carry

    lax.fori_loop(0, s.blocks, project, 0)
    for g in range(s.groups):
        for b in range(s.nb):
            place = pl.ds(pl.multiple_of(z * s.far_own + b * BLOCK, BLOCK), BLOCK)
            r.fkv[0, g, place] = r.kl[g * s.tb + b, pl.ds(48, BLOCK)]
            r.fkv[1, g, place] = r.vl[g * s.tb + b, pl.ds(48, BLOCK)]

    def far_rows(zz):
        return r.fkv.at[:, :, pl.ds(pl.multiple_of(zz * s.far_own, s.far_own), s.far_own)]

    for zz in zs:
        send(far_rows(z), far_rows(z), r.fs.at[0, zz], r.fr.at[0, z], (dp, zz))
    ag1(4)
    ag2(2)
    ag2(3)

    def reps(t, carry):
        rows = pl.ds(pl.multiple_of(t * CONT_LEN, CONT_LEN), CONT_LEN)
        r.qr[t] = nn(r.rep[...], r.q[rows]).astype(BF16)
        return carry

    lax.fori_loop(0, s.blocks, reps, 0)
    ag3(2)
    for zz in zs:
        wait_recv(far_rows(zz), r.fs.at[0, zz], r.fr.at[0, zz], (dp, zz))

    def two(a):
        zero = jnp.zeros_like(a)
        return jnp.concatenate([jnp.where(lane_lo, a, zero), jnp.where(lane_lo, zero, a)], 0)

    def pick(a):
        return jnp.where(lane_lo, a[:CONT_LEN], a[CONT_LEN:])

    def operands(t, g, p):
        rows = pl.ds(pl.multiple_of(t * CONT_LEN, CONT_LEN), CONT_LEN)
        lanes = pl.ds(p * LANES, LANES)
        q = r.q[rows, lanes]
        q1 = r.qr[t, pl.ds(0, CONT_LEN), lanes]
        q2 = r.qr[t, pl.ds(CONT_LEN, CONT_LEN), lanes]
        q3 = r.qr[t, pl.ds(2 * CONT_LEN, CONT_LEN), lanes]
        q03 = jnp.concatenate([two(q), two(q3)], 1)
        q12 = jnp.concatenate([two(q1), two(q2)], 1)
        k0 = r.k[rows, lanes]
        kf = r.fkv[0, g, :, lanes]
        zero = jnp.zeros_like(k0)
        k03 = jnp.concatenate([jnp.concatenate([k0, zero], 1), jnp.concatenate([zero, kf], 1)], 0)
        kl = r.kl[t, :, lanes]
        kr = iota(kl.shape, 0)
        zl = jnp.zeros_like(kl)
        k12 = jnp.concatenate(
            [jnp.where(kr < 32, kl, zl), jnp.where((kr >= 32) & (kr < 48), kl, zl)], 1
        )
        return q03, q12, k03, k12

    def value_operands(t, g, p, counts0, counts1):
        rows = pl.ds(pl.multiple_of(t * CONT_LEN, CONT_LEN), CONT_LEN)
        lanes = pl.ds(p * LANES, LANES)
        v0 = r.v[rows, lanes]
        vf = r.fkv[1, g, :, lanes]
        eight = jnp.full((s.far, LANES), float(COARSE), BF16)
        vn03 = jnp.concatenate(
            [jnp.concatenate([v0, counts0], 1), jnp.concatenate([vf, eight], 1)], 0
        )
        vn12 = jnp.concatenate([r.vl[t, :, lanes], counts1], 1)
        return vn03, vn12

    def counts(length):
        i0 = iota((CONT_LEN, LANES), 0)
        counts0 = jnp.where(i0 < length, 1.0, 0.0).astype(BF16)
        i1 = iota((64, LANES), 0)
        first = jnp.where(i1 < 16, 2 * i1, jnp.where(i1 < 32, 2 * (i1 + 16), 4 * (i1 - 32)))
        width = jnp.where(i1 < 32, 2, 4)
        counts1 = jnp.where(i1 < 48, jnp.clip(length - first, 0, width), 0).astype(F32).astype(BF16)
        return counts0, counts1

    def attend(t, carry):
        g, b = t // s.tb, lax.rem(t, s.tb)
        rows = pl.ds(pl.multiple_of(t * CONT_LEN, CONT_LEN), CONT_LEN)
        counts0, counts1 = counts(length_of(g, b))
        limit = jnp.where(b >= s.nb, s.far, BLOCK * (z * s.nb + b))
        bias_far = jnp.where(iota((CONT_LEN, s.far), 1) < limit, 0.0, AWAY)
        bias = jnp.concatenate([r.bias0[...], bias_far], 1)
        bias = jnp.concatenate([bias, bias], 0)
        bias1 = jnp.concatenate([r.bias1[...], r.bias1[...]], 0)
        for p in range(PAIRS):
            q03, q12, k03, k12 = operands(t, g, p)
            vn03, vn12 = value_operands(t, g, p, counts0, counts1)
            e03 = jnp.exp2(nt(q03, k03) * (SCORE * LOG2E) + bias).astype(BF16)
            e12 = jnp.exp2(nt(q12, k12) * (SCORE * LOG2E) + bias1).astype(BF16)
            r.e03[t * PAIRS + p] = e03
            r.e12[t * PAIRS + p] = e12
            total = nn(e03, vn03) + nn(e12, vn12)
            numerator = pick(total[:, :LANES])
            denominator = pick(total[:, LANES:])
            lanes = pl.ds(p * LANES, LANES)
            r.att[rows, lanes] = (numerator / denominator).astype(BF16)
            r.den[rows, lanes] = denominator
        return carry

    lax.fori_loop(0, s.tb, attend, 0)
    ag2(4)
    ag3(3)
    lax.fori_loop(s.tb, s.blocks, attend, 0)
    ag3(4)
    ag4(2)

    for copy in later_in:
        copy.wait()
    for g in range(s.groups):
        rows = pl.ds(g * s.rows_g, s.rows_g)
        mixed = r.x[rows].astype(F32) + nn(r.att[rows], r.w4[3])
        r.mix[rows] = mixed
        xhat, _ = norm_stats(mixed)
        r.n2[rows] = (xhat * vec(2) + vec(3)).astype(BF16)
    ag4(3)
    for g in range(s.groups):
        rows = pl.ds(g * s.rows_g, s.rows_g)
        for n in range(FF // D):
            cols = pl.ds(n * D, D)
            pre = nn(r.n2[rows], r.wu[:, cols]) + r.upb[:, cols]
            r.h[rows, cols] = jnp.maximum(pre, 0.0).astype(BF16)
    ag4(4)
    outs = []

    def rows_out(src, prompt, cont, g):
        base = g * s.rows_g
        outs.append(local(src.at[pl.ds(base, s.prompt)], prompt.at[g]))
        for c in range(s.conts):
            outs.append(local(src.at[pl.ds(base + s.prompt + c * CONT_LEN, CONT_LEN)], cont.at[g, c]))

    extra = 2.0 * r.ls[0, 0] / (token_row * float(D))
    for g in range(s.groups):
        base = g * s.rows_g
        rows = pl.ds(base, s.rows_g)
        y = r.mix[rows] + nn(r.h[rows], r.wd[...]) + vec(4)
        r.y[rows] = y.astype(BF16)
        rows_out(r.y, r.py, r.cy, g)
        gy = r.dy[rows].astype(F32)
        parts = [gy[: s.prompt]]
        for c in range(s.conts):
            lo = s.prompt + c * CONT_LEN
            keep = iota((CONT_LEN, D), 0) < r.lens[g, c]
            diff = jnp.where(keep, y[lo : lo + CONT_LEN] - r.teach[g * s.conts + c].astype(F32), 0.0)
            r.vg[pl.ds(5, 1), :] += colsum(diff * diff)
            parts.append(gy[lo : lo + CONT_LEN] + extra * diff)
        gy = jnp.concatenate(parts, 0)
        r.gy[rows] = gy
        r.gyb[rows] = gy.astype(BF16)
        r.vg[pl.ds(4, 1), :] += colsum(gy)

    for n in range(FF // D):
        cols = pl.ds(n * D, D)
        r.gd[0, n] = tn(r.h[:, cols], r.gyb[...]).astype(BF16).reshape(2, FF // 8, D)
    rs0(3)
    for n in range(FF // D):
        cols = pl.ds(n * D, D)
        for g in range(s.groups):
            rows = pl.ds(g * s.rows_g, s.rows_g)
            dh = nt(r.gyb[rows], r.wd[cols])
            dpre = jnp.where(r.h[rows, cols] > 0, dh, 0.0).astype(BF16)
            r.h[rows, cols] = dpre
            r.vg[pl.ds(8 + n, 1), :] += colsum(dpre.astype(F32))
        r.gu[0, :, :, :, cols] = tn(r.n2[...], r.h[:, cols]).astype(BF16).reshape(4, 2, D // 8, D)
    rs0(2)
    rs1(3)
    for g in range(s.groups):
        rows = pl.ds(g * s.rows_g, s.rows_g)
        dn2 = nt(r.h[rows], r.wu[...])
        xhat, rstd = norm_stats(r.mix[rows])
        r.vg[pl.ds(2, 1), :] += colsum(dn2 * xhat)
        r.vg[pl.ds(3, 1), :] += colsum(dn2)
        dmixed = r.gy[rows] + norm_back(xhat, rstd, vec(2), dn2)
        r.gy[rows] = dmixed
        r.gyb[rows] = dmixed.astype(BF16)
    rs1(2)
    rs2(3)
    r.go[0] = tn(r.att[...], r.gyb[...]).astype(BF16).reshape(4, 2, D // 8, D)
    rs0(1)
    for g in range(s.groups):
        rows = pl.ds(g * s.rows_g, s.rows_g)
        dnum = nt(r.gyb[rows], r.w4[3]) / r.den[rows]
        r.dnum[rows] = dnum.astype(BF16)
        r.xo[rows] = (-dnum * r.att[rows].astype(F32)).astype(BF16)
    rs2(2)
    rs1(1)
    rs3(3)

    def attend_back(t, carry):
        g, b = t // s.tb, lax.rem(t, s.tb)
        rows = pl.ds(pl.multiple_of(t * CONT_LEN, CONT_LEN), CONT_LEN)
        length = length_of(g, b)
        counts0, counts1 = counts(length)
        keep = iota((CONT_LEN, LANES), 0) < length
        for p in range(PAIRS):
            lanes = pl.ds(p * LANES, LANES)
            q03, q12, k03, k12 = operands(t, g, p)
            vn03, vn12 = value_operands(t, g, p, counts0, counts1)
            dnum = two(r.dnum[rows, lanes])
            x = jnp.concatenate([dnum, two(r.xo[rows, lanes])], 1)
            e03 = r.e03[t * PAIRS + p]
            e12 = r.e12[t * PAIRS + p]
            ds03 = (nt(x, vn03) * e03.astype(F32)).astype(BF16)
            ds12 = (nt(x, vn12) * e12.astype(F32)).astype(BF16)
            dq03 = nn(ds03, k03)
            dq12 = nn(ds12, k12)
            coarse = jnp.concatenate(
                [pick(dq12[:, :LANES]), pick(dq12[:, LANES:]), pick(dq03[:, LANES:])], 0
            ).astype(BF16)
            dq = pick(dq03[:, :LANES]) + tn(r.rep[...], coarse)
            r.dqkv[0, rows, lanes] = (dq * SCORE).astype(BF16)
            dk03 = tn(ds03, q03)
            dk12 = tn(ds12, q12)
            dv03 = tn(e03, dnum)
            dv12 = tn(e12, dnum)
            kr = iota((64, LANES), 0)
            dkl = jnp.where(
                kr < 32, 0.5 * dk12[:, :LANES], jnp.where(kr < 48, 0.25 * dk12[:, LANES:], 0.0)
            ).astype(BF16)
            dk = dk03[:CONT_LEN, :LANES] + tn(r.pool[...], dkl)
            dv = dv03[:CONT_LEN] + tn(r.pool[...], dv12.astype(BF16))
            r.dkv[0, rows, lanes] = jnp.where(keep, dk * SCORE, 0.0)
            r.dkv[1, rows, lanes] = jnp.where(keep, dv, 0.0)
            r.df[0, g, :, lanes] += dk03[CONT_LEN:, LANES:] * SCORE
            r.df[1, g, :, lanes] += dv03[CONT_LEN:]
        return carry

    def far_part(ref, g, zz):
        return ref.at[g, :, pl.ds(pl.multiple_of(zz * s.far_own, s.far_own), s.far_own)]

    def far_back(g):
        for i in range(2):
            r.dfs[g, i] = r.df[i, g].astype(BF16)
        for zz in zs:
            send(far_part(r.dfs, g, zz), r.rf.at[g, z], r.fs.at[1 + g, zz], r.fr.at[1 + g, z], (dp, zz))

    for g in range(s.groups):
        lax.fori_loop(g * s.tb, (g + 1) * s.tb, attend_back, 0)
        far_back(g)
        if g == 0:
            rs3(2)
            rs2(1)
            rs4(3, [r.ogd] if s.exchange else None)
    r.gq[0] = tn(r.n1[...], r.dqkv[0]).astype(BF16).reshape(4, 2, D // 8, D)
    rs3(1)
    rs4(2, [r.ogu] if s.exchange else None)
    spread = jnp.where(
        iota((s.prompt, s.far_own), 0) // COARSE == iota((s.prompt, s.far_own), 1), 1.0, 0.0
    ).astype(BF16)
    for g in range(s.groups):
        base = g * s.rows_g
        for zz in zs:
            wait_recv(r.rf.at[g, zz], r.fs.at[1 + g, zz], r.fr.at[1 + g, zz], (dp, zz))
        own = pl.ds(pl.multiple_of(z * s.far_own, s.far_own), s.far_own)
        for i, scale in enumerate((1.0 / COARSE, 1.0)):
            total = r.df[i, g, own]
            for zz in zs:
                total = total + r.rf[g, zz, i].astype(F32)
            wide = nn(spread, total.astype(BF16)) * scale
            rows = pl.ds(base, s.prompt)
            r.dqkv[1 + i, rows] = (r.dkv[i, rows] + wide).astype(BF16)
            rows = pl.ds(base + s.prompt, s.rows_g - s.prompt)
            r.dqkv[1 + i, rows] = r.dkv[i, rows].astype(BF16)

    for j in (1, 2):
        r.gq[j] = tn(r.n1[...], r.dqkv[j]).astype(BF16).reshape(4, 2, D // 8, D)
    rs0(0)
    for g in range(s.groups):
        rows = pl.ds(g * s.rows_g, s.rows_g)
        dn1 = nt(r.dqkv[0, rows], r.w4[0]) + nt(r.dqkv[1, rows], r.w4[1]) + nt(r.dqkv[2, rows], r.w4[2])
        xhat, rstd = norm_stats(r.x[rows].astype(F32))
        r.vg[pl.ds(0, 1), :] += colsum(dn1 * xhat)
        r.vg[pl.ds(1, 1), :] += colsum(dn1)
        r.gy[rows] = r.gy[rows] + norm_back(xhat, rstd, vec(0), dn1)
        rows_out(r.gy, r.pdx, r.cdx, g)

    if s.exchange:
        def vsend(src, i, ssem, dev, ri):
            send(src, r.rv.at[i], r.vs.at[ssem], r.vr.at[ri], dev)

        vsend(r.vg, 0, 0, (sib, z), 0)
        rs1(0)
        rs4(1, [r.ogo])
        wait_recv(r.rv.at[0], r.vs.at[0], r.vr.at[0], (sib, z))
        r.vt[0] = r.vg[...] + r.rv[0]
        vsend(r.vt.at[0], 1, 1, (xn, z), 1)
        rs2(0)
        wait_recv(r.rv.at[1], r.vs.at[1], r.vr.at[1], (xn, z))
        r.vt[1] = r.vt[0] + r.rv[1]
        vsend(r.vt.at[1], 2, 2, (yn, z), 2)
        rs3(0)
        wait_recv(r.rv.at[2], r.vs.at[2], r.vr.at[2], (yn, z))
        r.vt[2] = r.vt[1] + r.rv[2]
        for zz in zs:
            send(r.vt.at[2], r.rv.at[3 + z], r.vs.at[3 + zz], r.vr.at[3 + z], (dp, zz))
        for zz in zs:
            wait_recv(r.rv.at[3 + zz], r.vs.at[3 + zz], r.vr.at[3 + zz], (dp, zz))
        r.rv[3 + z] = r.vt[2]
        total = r.rv[3]
        for i in range(1, s.nz):
            total = total + r.rv[3 + i]
        loss = jnp.sum(total[5:6], 1, keepdims=True) / (token_row[:, :1] * float(D))
        mine = jnp.zeros((8, LANES), F32)
        per = LANES // s.r
        for k in range(D // LANES):
            mine = jnp.where(me // per == k, total[:8, k * LANES : (k + 1) * LANES], mine)
        mine = pltpu.roll(mine, lax.rem(LANES - lax.rem(me, per) * s.r, LANES), 1)
        per = LANES // s.rf
        up = jnp.zeros((1, LANES), F32)
        for k in range(FF // LANES):
            i, j = divmod(k, D // LANES)
            up = jnp.where(me // per == k, total[8 + i : 9 + i, j * LANES : (j + 1) * LANES], up)
        up = jnp.broadcast_to(up, (8, LANES))
        up = pltpu.roll(up, lax.rem(LANES - lax.rem(me, per) * s.rf, LANES), 1)
        row = iota((8, LANES), 0)
        r.ov[...] = jnp.where(row < 5, mine, jnp.where(row == 5, loss, up))
        rs4(0, [r.ogq, r.ogk, r.ogv])
    else:
        r.ov[...] = r.vg[...]
        for src, dst in ((r.gq, r.fgq), (r.go, r.fgo), (r.gu, r.fgu), (r.gd, r.fgd)):
            outs.append(local(src, dst))
    for copy in outs:
        copy.wait()
    for copy in pending:
        copy.wait_send()


def layer(
    mesh,
    prompt_x,
    cont_x,
    prompt_dy,
    cont_dy,
    teacher,
    cont_lengths,
    loss_scale,
    norm1_gain,
    norm1_bias,
    w_query,
    w_key,
    w_value,
    w_out,
    norm2_gain,
    norm2_bias,
    w_up,
    up_bias,
    w_down,
    down_bias,
):
    nz, ndp = mesh.shape["cont"], mesh.shape["dp"]
    ndev = nz * ndp
    exchange = ndp == 8 and nz == 4
    groups, prompt = prompt_x.shape[:2]
    conts = cont_x.shape[1]
    s = Sizes(groups, prompt, conts, nz, exchange, ndev)
    both = ("dp", "cont")
    any_spec = pl.BlockSpec(memory_space=pl.ANY)
    vmem = pl.BlockSpec(memory_space=pltpu.VMEM)
    smem = pl.BlockSpec(memory_space=pltpu.SMEM)

    inputs = {
        "px": (prompt_x, any_spec),
        "cx": (cont_x, any_spec),
        "pdy": (prompt_dy, any_spec),
        "cdy": (cont_dy, any_spec),
        "te": (teacher, any_spec),
        "lens": (cont_lengths, smem),
        "ls": (loss_scale.reshape(1, 1), smem),
    }
    weights = {"wq": w_query, "wk": w_key, "wv": w_value, "wo": w_out, "wup": w_up, "wdn": w_down}
    vectors = {"v1g": norm1_gain, "v1b": norm1_bias, "v2g": norm2_gain, "v2b": norm2_bias, "vdb": down_bias}
    if exchange:
        for name, w in weights.items():
            inputs[name] = (w, any_spec)
        for name, v in vectors.items():
            inputs[name] = (v.reshape(1, -1), vmem)
        inputs["vub"] = (up_bias.reshape(1, -1), vmem)
    else:
        for name, w in weights.items():
            inputs[name] = (lax.all_gather(w, both, axis=0, tiled=True), any_spec)
        tokens = lax.psum(jnp.sum(cont_lengths).astype(F32), both)
        full = [lax.all_gather(v, both, axis=0, tiled=True).astype(F32) for v in vectors.values()]
        zero = jnp.zeros((D,), F32)
        inputs["vecs"] = (jnp.stack(full + [zero, jnp.full((D,), tokens / (D // LANES)), zero]), vmem)
        up_full = lax.all_gather(up_bias, both, axis=0, tiled=True).astype(F32)
        inputs["upbs"] = (up_full.reshape(1, FF), vmem)

    m, mf = D // 8, FF // 8
    outputs = {
        "py": (prompt_x.shape, BF16, any_spec),
        "cy": (cont_x.shape, BF16, any_spec),
        "pdx": (prompt_x.shape, F32, any_spec),
        "cdx": (cont_x.shape, F32, any_spec),
    }
    if exchange:
        for name in ("ogq", "ogk", "ogv", "ogo"):
            outputs[name] = ((s.r, D), F32, vmem)
        outputs["ogu"] = ((s.r, FF), F32, vmem)
        outputs["ogd"] = ((s.rf, D), F32, vmem)
        outputs["ov"] = ((8, LANES), F32, vmem)
    else:
        outputs["fgq"] = ((3, 4, 2, m, D), BF16, any_spec)
        outputs["fgo"] = ((1, 4, 2, m, D), BF16, any_spec)
        outputs["fgu"] = ((1, 4, 2, m, FF), BF16, any_spec)
        outputs["fgd"] = ((1, 4, 2, mf, D), BF16, any_spec)
        outputs["ov"] = ((16, D), F32, vmem)

    rows, blocks = s.rows, s.blocks
    dma = pltpu.SemaphoreType.DMA
    scratch = {
        "w4": ((4, D, D), BF16),
        "wu": ((D, FF), BF16),
        "wd": ((FF, D), BF16),
        "vec": ((8, D), F32),
        "upb": ((1, FF), F32),
        "x": ((rows, D), BF16),
        "dy": ((rows, D), BF16),
        "teach": ((groups * conts, CONT_LEN, D), BF16),
        "y": ((rows, D), BF16),
        "n1": ((rows, D), BF16),
        "q": ((rows, D), BF16),
        "k": ((rows, D), BF16),
        "v": ((rows, D), BF16),
        "qr": ((blocks, 3 * CONT_LEN, D), BF16),
        "kl": ((blocks, 64, D), BF16),
        "vl": ((blocks, 64, D), BF16),
        "fkv": ((2, groups, s.far, D), BF16),
        "rep": ((3 * CONT_LEN, CONT_LEN), BF16),
        "pool": ((64, CONT_LEN), BF16),
        "bias0": ((CONT_LEN, CONT_LEN), F32),
        "bias1": ((CONT_LEN, 64), F32),
        "e03": ((blocks * PAIRS, 2 * CONT_LEN, CONT_LEN + s.far), BF16),
        "e12": ((blocks * PAIRS, 2 * CONT_LEN, 64), BF16),
        "att": ((rows, D), BF16),
        "den": ((rows, D), F32),
        "mix": ((rows, D), F32),
        "n2": ((rows, D), BF16),
        "h": ((rows, FF), BF16),
        "gy": ((rows, D), F32),
        "gyb": ((rows, D), BF16),
        "dnum": ((rows, D), BF16),
        "xo": ((rows, D), BF16),
        "dqkv": ((3, rows, D), BF16),
        "dkv": ((2, rows, D), F32),
        "df": ((2, groups, s.far, D), F32),
        "dfs": ((groups, 2, s.far, D), BF16),
        "rf": ((groups, nz, 2, s.far_own, D), BF16),
        "vg": ((16, D), F32),
        "gq": ((3, 4, 2, m, D), BF16),
        "go": ((1, 4, 2, m, D), BF16),
        "gu": ((1, 4, 2, m, FF), BF16),
        "gd": ((1, 4, 2, mf, D), BF16),
        "lsem": dma((64,)),
        "fs": dma((1 + groups, nz)),
        "fr": dma((1 + groups, nz)),
    }
    if exchange:
        scratch["tiles"] = ((ndev, 8, LANES), F32)
        scratch["build"] = ((8, LANES), F32)
        for name, (nj, rr, cc) in {"q": (3, m, D), "o": (1, m, D), "u": (1, m, FF), "d": (1, mf, D)}.items():
            scratch["rc" + name] = ((nj, 4, rr, cc), BF16)
            scratch["rd" + name] = ((2, nj, rr // 2, cc), BF16)
            scratch["rx" + name] = ((2, nj, rr, cc), BF16)
            scratch["rz" + name] = ((nz, nj, rr // nz, cc), BF16)
        scratch["rv"] = ((3 + nz, 16, D), F32)
        scratch["vt"] = ((3, 16, D), F32)
        scratch["ags"] = dma((5, 12))
        scratch["agr"] = dma((5, 12))
        scratch["rss"] = dma((4, 5 + nz))
        scratch["rsr"] = dma((4, 5 + nz))
        scratch["vs"] = dma((3 + nz,))
        scratch["vr"] = dma((3 + nz,))

    names = list(inputs) + list(outputs) + list(scratch)
    results = pl.pallas_call(
        functools.partial(kernel, s, names),
        out_shape=[jax.ShapeDtypeStruct(shape, dtype) for shape, dtype, _ in outputs.values()],
        in_specs=[spec for _, spec in inputs.values()],
        out_specs=[spec for _, _, spec in outputs.values()],
        scratch_shapes=[pltpu.VMEM(*v) if isinstance(v, tuple) else v for v in scratch.values()],
        compiler_params=pltpu.CompilerParams(
            collective_id=0, has_side_effects=True, vmem_limit_bytes=64 * 1024 * 1024 - 65536
        ),
        name="layer",
    )(*[a for a, _ in inputs.values()])
    o = types.SimpleNamespace(**dict(zip(outputs, results)))
    if exchange:
        vec = [o.ov[i, : s.r] for i in range(5)]
        loss = o.ov[5, 0]
        up_vec = o.ov[6, : s.rf]
        mats = [o.ogq, o.ogk, o.ogv, o.ogo, o.ogu, o.ogd]
    else:
        whole = [o.fgq[0], o.fgq[1], o.fgq[2], o.fgo[0], o.fgu[0], o.fgd[0]]
        whole = [w.reshape(-1, w.shape[-1]).astype(F32) for w in whole]
        parts = [o.ov[i] for i in range(5)] + [o.ov[8:12].reshape(FF)]
        *mats, v0, v1, v2, v3, v4, up_vec = [
            lax.psum_scatter(w, both, scatter_dimension=0, tiled=True) for w in whole + parts
        ]
        vec = [v0, v1, v2, v3, v4]
        loss = lax.psum(jnp.sum(o.ov[5]), both) / (tokens * D)
    return (
        o.py,
        o.cy,
        loss,
        o.pdx,
        o.cdx,
        vec[0],
        vec[1],
        mats[0],
        mats[1],
        mats[2],
        mats[3],
        vec[2],
        vec[3],
        mats[4],
        up_vec,
        mats[5],
        vec[4],
    )


def solution(mesh):
    rows = P("dp", "cont", None)
    conts = P("dp", "cont", None, None)
    vector = P(("dp", "cont"))
    matrix = P(("dp", "cont"), None)
    return jax.shard_map(
        functools.partial(layer, mesh),
        mesh=mesh,
        in_specs=(rows, conts, rows, conts, conts, P("dp", "cont"), P())
        + (vector, vector, matrix, matrix, matrix, matrix, vector, vector, matrix, vector, matrix, vector),
        out_specs=(rows, conts, P(), rows, conts)
        + (vector, vector, matrix, matrix, matrix, matrix, vector, vector, matrix, vector, matrix, vector),
        check_vma=False,
    )
```

```python
import functools
import types

import jax
import jax.numpy as jnp
from jax import lax
from jax.experimental import pallas as pl
from jax.experimental.pallas import tpu as pltpu
from jax.sharding import PartitionSpec as P

D = 512
HEADS = 8
HEAD_DIM = 64
FF = 2048
BLOCK = 16
CONT_LEN = 128
COARSE = CONT_LEN // BLOCK
PAIRS = HEADS // 2
EPS = 1e-5
SCORE = HEAD_DIM**-0.5
LOG2E = 1.4426950408889634
AWAY = -1e30
F32 = jnp.float32
BF16 = jnp.bfloat16
MESH = pl.DeviceIdType.MESH
LANES = 128
SENDS = 24


def nn(a, b):
    return jnp.dot(a, b, preferred_element_type=F32)


def nt(a, b):
    return lax.dot_general(a, b, (((1,), (1,)), ((), ())), preferred_element_type=F32)


def tn(a, b):
    return lax.dot_general(a, b, (((0,), (0,)), ((), ())), preferred_element_type=F32)


def iota(shape, dim):
    return lax.broadcasted_iota(jnp.int32, shape, dim)


def norm_stats(x):
    center = x - jnp.mean(x, -1, keepdims=True)
    rstd = lax.rsqrt(jnp.mean(center * center, -1, keepdims=True) + EPS)
    return center * rstd, rstd


def norm_back(xhat, rstd, gain, dn):
    dxhat = dn * gain
    mean_one = jnp.mean(dxhat, -1, keepdims=True)
    mean_two = jnp.mean(dxhat * xhat, -1, keepdims=True)
    return rstd * (dxhat - mean_one - xhat * mean_two)


def colsum(x):
    return jnp.sum(x, 0, keepdims=True)


class Sizes:
    def __init__(self, groups, prompt, conts, nz, exchange, ndev):
        self.groups = groups
        self.prompt = prompt
        self.conts = conts
        self.nz = nz
        self.exchange = exchange
        self.ndev = ndev
        self.nb = prompt // CONT_LEN
        self.tb = self.nb + conts
        self.rows_g = self.tb * CONT_LEN
        self.rows = groups * self.rows_g
        self.blocks = groups * self.tb
        self.far_own = prompt // COARSE
        self.far = self.far_own * nz
        self.r = D // ndev
        self.rf = FF // ndev


def kernel(s, names, *refs):
    r = types.SimpleNamespace(**dict(zip(names, refs)))
    z = lax.axis_index("cont")
    dp = lax.axis_index("dp")
    zs = [lax.rem(z + d, s.nz) for d in range(1, s.nz)]
    pending = {}
    sent = [0]

    def remote(src, dst, ssem, rsem, dev):
        return pltpu.make_async_remote_copy(
            src_ref=src, dst_ref=dst, send_sem=ssem, recv_sem=rsem, device_id=dev, device_id_type=MESH
        )

    def send(src, dst, rsem, dev):
        slot = sent[0] % SENDS
        sent[0] += 1
        if slot in pending:
            pending[slot].wait_send()
        copy = remote(src, dst, r.ss.at[slot], rsem, dev)
        copy.start()
        pending[slot] = copy

    def wait_recv(ref, rsem):
        pltpu.make_async_copy(ref, ref, rsem).wait()

    local_count = [0]
    outs = []

    def local(pairs, whole=None):
        sem = r.lsem.at[local_count[0]]
        local_count[0] += 1
        copies = [pltpu.make_async_copy(src, dst, sem) for src, dst in pairs]
        for copy in copies:
            copy.start()
        return copies[0] if whole is None else pltpu.make_async_copy(whole, whole, sem)

    def row_pairs(prompt, cont, rows):
        out = []
        for g in range(s.groups):
            base = g * s.rows_g
            out.append((prompt.at[g], rows.at[pl.ds(base, s.prompt)]))
            for c in range(s.conts):
                out.append((cont.at[g, c], rows.at[pl.ds(base + s.prompt + c * CONT_LEN, CONT_LEN)]))
        return out

    if s.exchange:
        core = lax.rem(dp, 2)
        ix = lax.rem(dp // 2, 2)
        iy = dp // 4
        sib = dp + 1 - 2 * core
        xn = dp + 2 - 4 * ix
        yn = dp + 4 - 8 * iy
        cell = dp // 2
        cell_x = cell + 1 - 2 * ix
        cell_y = cell + 2 - 4 * iy
        cell_d = cell_x + cell_y - cell
        sibcore = 1 - core
        me = dp * s.nz + z

        def view(k, a, n, part=None):
            if k == 0:
                return r.tiles.at[pl.ds(a, n)]
            ref, rows = [(r.w4, s.r), (r.w4, s.r), (r.wu, s.r), (r.wd, s.rf)][k - 1]
            place = pl.ds(pl.multiple_of(a * rows, rows), n * rows)
            width = ref.shape[-1]
            cols = pl.ds(0, width) if part is None else pl.ds(part * (width // 2), width // 2)
            if k == 1:
                return ref.at[pl.ds(0, 3), place, cols]
            if k == 2:
                return ref.at[3, place, cols]
            return ref.at[place, cols]

        def shard(c, co, zz):
            return (c * 2 + co) * s.nz + zz

        def ag_move(k, kind, a, n, dev, part=None):
            v = view(k, a, n, part)
            send(v, v, r.agr.at[k, kind], dev)

        def ag_got(k, kind, n, part=None):
            wait_recv(view(k, 0, n, part), r.agr.at[k, kind])

        def ag_z(k):
            for zz in zs:
                ag_move(k, 0, me, 1, (dp, zz))

        def ag_out(k, wave, starts, n):
            if wave == 1 or n > 1:
                ag_got(k, 0, s.nz - 1)
            for zz in starts:
                a = shard(cell, core, zz)
                ag_move(k, 1 + wave, a, n, (xn, z))
                ag_move(k, 3 + wave, a, n, (yn, z))
            for zz in starts:
                ag_move(k, 9, shard(cell, core, zz), n, (sib, z))

        def ag_pass(k, wave, starts, n):
            total = len(starts) * n
            ag_got(k, 1 + wave, total)
            for zz in starts:
                ag_move(k, 5 + wave, shard(cell_x, core, zz), n, (yn, z), 0)
            ag_got(k, 3 + wave, total)
            if k > 0:
                for zz in starts:
                    ag_move(k, 7 + wave, shard(cell_y, core, zz), n, (xn, z), 1)
            for zz in starts:
                ag_move(k, 9, shard(cell_x, core, zz), n, (sib, z))
                ag_move(k, 9, shard(cell_y, core, zz), n, (sib, z))

        def ag_last(k, wave, starts, n):
            total = len(starts) * n
            ag_got(k, 5 + wave, total, 0)
            if k > 0:
                ag_got(k, 7 + wave, total, 1)
            for zz in starts:
                ag_move(k, 9, shard(cell_d, core, zz), n, (sib, z))

        def ag1(k):
            ag_out(k, 0, [0], s.nz)

        def ag2(k):
            ag_pass(k, 0, [0], s.nz)

        def ag3(k):
            ag_last(k, 0, [0], s.nz)

        def ag4(k):
            ag_got(k, 9, 4 * s.nz)

        grads = [(r.gd.at[...], r.rcd, r.rdd, r.rxd, r.rzd), (r.gu.at[...], r.rcu, r.rdu, r.rxu, r.rzu),
                 (r.go.at[...], r.rco, r.rdo, r.rxo, r.rzo)]
        for p in range(PAIRS):
            grads.append((r.gq.at[p], r.rcq.at[p], r.rdq.at[p], r.rxq.at[p], r.rzq.at[p]))

        def rs0(k):
            g, rc, _, _, _ = grads[k]
            send(g.at[:, sibcore], rc, r.rsr.at[k, 0], (sib, z))

        def add_to(g, c, lo, n, term):
            place = (c, core, pl.ds(lo, n))
            g[place] = (g[place].astype(F32) + term).astype(BF16)

        def rs1(k):
            g, rc, rd, _, _ = grads[k]
            m = g.shape[2]
            wait_recv(rc, r.rsr.at[k, 0])
            add_to(g, cell_d, 0, m, rc[cell_d].astype(F32))
            mh = m // 2
            send(g.at[cell_d, core, pl.ds(0, mh)], rd.at[0], r.rsr.at[k, 1], (yn, z))
            send(g.at[cell_d, core, pl.ds(mh, mh)], rd.at[1], r.rsr.at[k, 2], (xn, z))
            for c in (cell_x, cell_y, cell):
                add_to(g, c, 0, m, rc[c].astype(F32))

        def rs2(k):
            g, _, rd, rx, _ = grads[k]
            mh = g.shape[2] // 2
            wait_recv(rd.at[0], r.rsr.at[k, 1])
            add_to(g, cell_x, 0, mh, rd[0].astype(F32))
            send(g.at[cell_x, core], rx.at[0], r.rsr.at[k, 3], (xn, z))
            wait_recv(rd.at[1], r.rsr.at[k, 2])
            add_to(g, cell_y, mh, mh, rd[1].astype(F32))
            send(g.at[cell_y, core], rx.at[1], r.rsr.at[k, 3], (yn, z))

        def piece(g, zz):
            n = g.shape[2] // s.nz
            return pl.ds(pl.multiple_of(zz * n, n), n)

        def rs3(k):
            g, _, _, rx, rz = grads[k]
            wait_recv(rx, r.rsr.at[k, 3])
            add_to(g, cell, 0, g.shape[2], rx[0].astype(F32) + rx[1].astype(F32))
            for d, zz in enumerate(zs):
                send(g.at[cell, core, piece(g, zz)], rz.at[d], r.rsr.at[k, 4], (dp, zz))

        def rs4(k):
            g, _, _, _, rz = grads[k]
            wait_recv(rz, r.rsr.at[k, 4])
            total = g[cell, core, piece(g, z)].astype(F32)
            for d in range(s.nz - 1):
                total = total + rz[d].astype(F32)
            if k < 3:
                held, out = ((r.hgd, r.ogd), (r.hgu, r.ogu), (r.hgo, r.ogo))[k]
                held[...] = total
                outs.append(local([(held, out)]))
            else:
                lanes = pl.ds((k - 3) * LANES, LANES)
                for j, (held, out) in enumerate(((r.hgq, r.ogq), (r.hgk, r.ogk), (r.hgv, r.ogv))):
                    held[:, lanes] = total[:, j * LANES : (j + 1) * LANES]
                    if k == 2 + PAIRS:
                        outs.append(local([(held, out)]))
    else:

        def nothing(*_):
            return None

        ag1 = ag2 = ag3 = ag4 = ag_z = ag_out = ag_pass = ag_last = nothing
        rs0 = rs1 = rs2 = rs3 = rs4 = nothing

    scalars_in = [local([(r.lens_in, r.lens)]), local([(r.ls_in, r.ls)])]
    if s.exchange:
        vectors_in = (r.v1g, r.v1b, r.v2g, r.v2b, r.vdb)
        scalars_in.append(local([(v, r.small.at[i]) for i, v in enumerate(vectors_in)], r.small))
        scalars_in.append(local([(r.vub, r.smallup)]))
        own_rows = pl.ds(pl.multiple_of(me * s.r, s.r), s.r)
        weights_in = [
            local([(w, r.w4.at[j, own_rows]) for j, w in enumerate((r.wq, r.wk, r.wv, r.wo))], r.w4.at[:, own_rows]),
            local([(r.wup, view(3, me, 1))]),
            local([(r.wdn, view(4, me, 1))]),
        ]
    else:
        weights_in = [local([(w, r.w4.at[j]) for j, w in enumerate((r.wq, r.wk, r.wv, r.wo))], r.w4)]
        weights_in += [local([(r.wup, r.wu)]), local([(r.wdn, r.wd)])]
    barrier = pltpu.get_barrier_semaphore()
    partners = [(dp, zz) for zz in zs]
    if s.exchange:
        partners += [(sib, z), (xn, z), (yn, z)]
    for dev in partners:
        pl.semaphore_signal(barrier, inc=1, device_id=dev, device_id_type=MESH)
    x_in = [local(row_pairs(r.px, r.cx, r.x), r.x)]
    teach_pairs = [(r.te.at[g, c], r.teach.at[g * s.conts + c]) for g in range(s.groups) for c in range(s.conts)]
    later_in = [local(row_pairs(r.pdy, r.cdy, r.dy), r.dy), local(teach_pairs, r.teach)]

    for copy in scalars_in:
        copy.wait()
    if s.exchange:
        r.build[...] = jnp.zeros_like(r.build)
        for i in range(5):
            r.build[pl.ds(i, 1), pl.ds(0, s.r)] = r.small[i].astype(F32)
        r.build[pl.ds(5, 1), pl.ds(0, s.rf)] = r.smallup[...].astype(F32)
        own_tokens = 0
        for g in range(s.groups):
            for c in range(s.conts):
                own_tokens = own_tokens + r.lens[c, g]
        tile = r.build[...]
        row = iota((8, LANES), 0)
        placed = jnp.where(
            row < 5,
            pltpu.roll(tile, lax.rem(me, LANES // s.r) * s.r, 1),
            pltpu.roll(tile, lax.rem(me, LANES // s.rf) * s.rf, 1),
        )
        r.tiles[me] = jnp.where(row == 6, own_tokens.astype(F32), placed)

    for copy in weights_in:
        copy.wait()
    pl.semaphore_wait(barrier, len(partners))
    first, rest = [z], zs
    ag_z(0)
    ag_z(1)
    ag_out(1, 0, first, 1)

    lane_lo = iota((CONT_LEN, LANES), 1) < HEAD_DIM
    lane_lo48 = iota((48, LANES), 1) < HEAD_DIM
    ri = iota((64, CONT_LEN), 0)
    ci = iota((64, CONT_LEN), 1)
    coarse_ci = jnp.where(ri < 32, ci >> 1, jnp.where(ri < 48, ci >> 2, ci >> 3))
    position = jnp.where(ri < 16, ri, jnp.where(ri < 32, ri + 16, jnp.where(ri < 48, ri - 32, ri - 48)))
    r.poolk[...] = jnp.where(coarse_ci == position, 1.0, 0.0).astype(BF16)
    position = jnp.where(ri < 48, position + 16, position)
    r.poolq[...] = jnp.where(coarse_ci == position, 1.0, 0.0).astype(BF16)
    ri = iota((CONT_LEN, 96), 0)
    ci = lax.rem(iota((CONT_LEN, 96), 1), 48)
    coarse_ri = jnp.where(ci < 32, ri >> 1, ri >> 2)
    position = jnp.where(ci < 16, ci + 16, jnp.where(ci < 32, ci + 32, ci - 16))
    r.widen[...] = jnp.where(coarse_ri == position, 1.0, 0.0).astype(BF16)
    ri = iota((CONT_LEN, CONT_LEN), 0)
    ci = iota((CONT_LEN, CONT_LEN), 1)
    bi, bj = ri >> 4, ci >> 4
    near = ((bi == bj) & (ci <= ri)) | (((bi & 1) == 1) & (bj == bi - 1))
    near = jnp.where(near, 0.0, AWAY)
    r.bias0[pl.ds(0, CONT_LEN)] = near
    r.bias0[pl.ds(CONT_LEN, CONT_LEN)] = near
    ri = lax.rem(iota((96, 48), 0), 48)
    r.bias1[...] = jnp.where((ri >> 4) == (iota((96, 48), 1) >> 4), 0.0, AWAY)
    nq = s.tb * BLOCK
    blk = lax.rem(iota((2 * nq, s.far), 0), nq) >> 4
    limit = jnp.where(blk >= s.nb, s.far, BLOCK * (z * s.nb + blk))
    r.biasf[...] = jnp.where(iota((2 * nq, s.far), 1) < limit, 0.0, AWAY)
    scale_rows = iota((64, D), 0)
    mean_scale = jnp.where(scale_rows < 32, 0.5, jnp.where(scale_rows < 48, 0.25, 0.125))
    r.vg[...] = jnp.zeros_like(r.vg)

    ag_pass(1, 0, first, 1)
    ag1(0)
    ag_out(1, 1, rest, 1)
    ag_z(2)
    ag_z(3)
    ag_last(1, 0, first, 1)
    ag2(0)
    ag_pass(1, 1, rest, 1)
    ag1(2)
    ag3(0)
    ag4(0)
    if s.exchange:
        count = 8
        for k in range(s.ndev // count):
            part = jnp.sum(r.tiles[pl.ds(k * count, count)], 0)
            r.vec[:, pl.ds(k * LANES, LANES)] = part
        for k in range(s.ndev // 2):
            part = r.tiles[2 * k] + r.tiles[2 * k + 1]
            r.upb[:, pl.ds(k * LANES, LANES)] = part[5:6]
    else:
        r.vec[...] = r.vecs[...]
        r.upb[...] = r.upbs[...]

    def vec(i):
        return r.vec[pl.ds(i, 1), :]

    token_row = r.vec[pl.ds(6, 1), pl.ds(0, LANES)]
    for k in range(1, D // LANES):
        token_row = token_row + r.vec[pl.ds(6, 1), pl.ds(k * LANES, LANES)]
    token_row = jnp.concatenate([token_row] * (D // LANES), 1)

    def length_of(g, b):
        if isinstance(b, int):
            return CONT_LEN if b < s.nb else r.lens[b - s.nb, g]
        c = jnp.clip(b - s.nb, 0, s.conts - 1)
        return jnp.where(b >= s.nb, r.lens[c, g], CONT_LEN)

    def block_rows(t):
        if isinstance(t, int):
            return pl.ds(t * CONT_LEN, CONT_LEN)
        return pl.ds(pl.multiple_of(t * CONT_LEN, CONT_LEN), CONT_LEN)

    for copy in x_in:
        copy.wait()

    def norm_one(i, carry):
        rows = block_rows(i)
        xhat, _ = norm_stats(r.x[rows].astype(F32))
        r.n1[rows] = (xhat * vec(0) + vec(1)).astype(BF16)
        return carry

    lax.fori_loop(0, s.blocks, norm_one, 0)
    ag_z(4)
    ag1(3)
    ag_last(1, 1, rest, 1)
    ag4(1)

    def project(t, carry):
        g, b = t // s.tb, lax.rem(t, s.tb)
        rows = block_rows(t)
        n1 = r.n1[rows]
        keep = iota((CONT_LEN, D), 0) < length_of(g, b)
        qv = nn(n1, r.w4[0]).astype(BF16)
        kv = jnp.where(keep, nn(n1, r.w4[1]), 0.0).astype(BF16)
        vv = jnp.where(keep, nn(n1, r.w4[2]), 0.0).astype(BF16)
        r.q[rows] = qv
        r.k[rows] = kv
        r.v[rows] = vv
        r.ql[t] = (nn(r.poolq[...], qv) * mean_scale).astype(BF16)
        r.kl[t] = (nn(r.poolk[...], kv) * mean_scale).astype(BF16)
        r.vl[t] = nn(r.poolk[...], vv).astype(BF16)
        return carry

    lax.fori_loop(0, s.blocks, project, 0)
    for g in range(s.groups):
        for b in range(s.nb):
            place = pl.ds(pl.multiple_of(z * s.far_own + b * BLOCK, BLOCK), BLOCK)
            r.fkv[0, g, place] = r.kl[g * s.tb + b, pl.ds(48, BLOCK)]
            r.fkv[1, g, place] = r.vl[g * s.tb + b, pl.ds(48, BLOCK)]

    def far_rows(zz):
        return r.fkv.at[:, :, pl.ds(pl.multiple_of(zz * s.far_own, s.far_own), s.far_own)]

    for zz in zs:
        send(far_rows(z), far_rows(z), r.fr.at[0], (dp, zz))
    ag2(2)
    ag2(3)
    ag1(4)

    def two(a):
        low = lane_lo if a.shape[0] == CONT_LEN else lane_lo48
        zero = jnp.zeros_like(a)
        return jnp.concatenate([jnp.where(low, a, zero), jnp.where(low, zero, a)], 0)

    def pick(a):
        n = a.shape[0] // 2
        return jnp.where(lane_lo if n == CONT_LEN else lane_lo48, a[:n], a[n:])

    def counts(length):
        i0 = iota((CONT_LEN, LANES), 0)
        counts0 = jnp.where(i0 < length, 1.0, 0.0).astype(BF16)
        i1 = iota((48, LANES), 0)
        first = jnp.where(i1 < 16, 2 * i1, jnp.where(i1 < 32, 2 * (i1 + 16), 4 * (i1 - 32)))
        width = jnp.where(i1 < 32, 2, 4)
        counts1 = jnp.clip(length - first, 0, width).astype(F32).astype(BF16)
        return counts0, counts1

    def pair_lanes(p):
        return pl.ds(p * LANES, LANES)

    low48 = pl.ds(0, 48)
    far16 = pl.ds(48, BLOCK)

    def near(t, carry):
        g, b = t // s.tb, lax.rem(t, s.tb)
        rows = block_rows(t)
        counts0, counts1 = counts(length_of(g, b))
        for p in range(PAIRS):
            lanes = pair_lanes(p)
            e0 = jnp.exp2(nt(two(r.q[rows, lanes]), r.k[rows, lanes]) * (SCORE * LOG2E) + r.bias0[...])
            e0 = e0.astype(BF16)
            e1 = jnp.exp2(
                nt(two(r.ql[t, low48, lanes]), r.kl[t, low48, lanes]) * (SCORE * LOG2E) + r.bias1[...]
            ).astype(BF16)
            r.e0[t * PAIRS + p] = e0
            r.e1[t * PAIRS + p] = e1
            t0 = nn(e0, jnp.concatenate([r.v[rows, lanes], counts0], 1))
            t1 = nn(e1, jnp.concatenate([r.vl[t, low48, lanes], counts1], 1))
            t1 = jnp.concatenate([pick(t1[:, :LANES]), pick(t1[:, LANES:])], 1)
            high = t1.astype(BF16)
            t1 = nn(r.widen[...], jnp.concatenate([high, (t1 - high.astype(F32)).astype(BF16)], 0))
            r.num[rows, lanes] = pick(t0[:, :LANES]) + t1[:, :LANES]
            r.den[rows, lanes] = pick(t0[:, LANES:]) + t1[:, LANES:]
        return carry

    eight = jnp.full((s.far, LANES), float(COARSE), BF16)

    def gathered(ref, g, lanes):
        return jnp.concatenate([ref[g * s.tb + b, far16, lanes] for b in range(s.tb)], 0)

    def repeat_rows(a):
        n = a.shape[0]
        return jnp.broadcast_to(a[:, None, :], (n, COARSE, LANES)).reshape(n * COARSE, LANES)

    def far_forward(g):
        rows = pl.ds(g * s.rows_g, s.rows_g)
        for p in range(PAIRS):
            lanes = pair_lanes(p)
            ef = nt(two(gathered(r.ql, g, lanes)), r.fkv[0, g, :, lanes]) * (SCORE * LOG2E) + r.biasf[...]
            ef = jnp.exp2(ef).astype(BF16)
            r.ef[g, p] = ef
            total = nn(ef, jnp.concatenate([r.fkv[1, g, :, lanes], eight], 1))
            denominator = r.den[rows, lanes] + repeat_rows(pick(total[:, LANES:]))
            numerator = r.num[rows, lanes] + repeat_rows(pick(total[:, :LANES]))
            r.den[rows, lanes] = denominator
            r.att[rows, lanes] = (numerator / denominator).astype(BF16)

    lax.fori_loop(0, s.tb, near, 0)
    ag3(2)
    ag3(3)
    ag2(4)
    lax.fori_loop(s.tb, s.blocks, near, 0)
    wait_recv(r.fkv.at[:, :, pl.ds(0, s.far - s.far_own)], r.fr.at[0])
    for g in range(s.groups):
        far_forward(g)
    ag4(2)
    ag3(4)

    for copy in later_in:
        copy.wait()
    for g in range(s.groups):
        rows = pl.ds(g * s.rows_g, s.rows_g)
        mixed = r.x[rows].astype(F32) + nn(r.att[rows], r.w4[3])
        r.mix[rows] = mixed
        xhat, _ = norm_stats(mixed)
        r.n2[rows] = (xhat * vec(2) + vec(3)).astype(BF16)
    ag4(3)
    for g in range(s.groups):
        rows = pl.ds(g * s.rows_g, s.rows_g)
        for n in range(FF // D):
            cols = pl.ds(n * D, D)
            pre = nn(r.n2[rows], r.wu[:, cols]) + r.upb[:, cols]
            r.h[rows, cols] = jnp.maximum(pre, 0.0).astype(BF16)
    ag4(4)
    extra = 2.0 * r.ls[0, 0] / (token_row * float(D))
    for g in range(s.groups):
        base = g * s.rows_g
        rows = pl.ds(base, s.rows_g)
        y = r.mix[rows] + nn(r.h[rows], r.wd[...]) + vec(4)
        r.y[rows] = y.astype(BF16)
        gy = r.dy[rows].astype(F32)
        parts = [gy[: s.prompt]]
        for c in range(s.conts):
            lo = s.prompt + c * CONT_LEN
            keep = iota((CONT_LEN, D), 0) < r.lens[c, g]
            diff = jnp.where(keep, y[lo : lo + CONT_LEN] - r.teach[g * s.conts + c].astype(F32), 0.0)
            r.vg[pl.ds(5, 1), :] += colsum(diff * diff)
            parts.append(gy[lo : lo + CONT_LEN] + extra * diff)
        gy = jnp.concatenate(parts, 0)
        r.gy[rows] = gy
        r.gyb[rows] = gy.astype(BF16)
        r.vg[pl.ds(4, 1), :] += colsum(gy)

    outs.append(local([(b, a) for a, b in row_pairs(r.py, r.cy, r.y)], r.y))

    for n in range(FF // D):
        cols = pl.ds(n * D, D)
        r.gd[n] = tn(r.h[:, cols], r.gyb[...]).astype(BF16).reshape(2, FF // 8, D)
    rs0(0)
    for n in range(FF // D):
        cols = pl.ds(n * D, D)
        for g in range(s.groups):
            rows = pl.ds(g * s.rows_g, s.rows_g)
            dh = nt(r.gyb[rows], r.wd[cols])
            dpre = jnp.where(r.h[rows, cols] > 0, dh, 0.0).astype(BF16)
            r.h[rows, cols] = dpre
            r.vg[pl.ds(8 + n, 1), :] += colsum(dpre.astype(F32))
        if n == 1:
            rs1(0)
    for g in range(s.groups):
        rows = pl.ds(g * s.rows_g, s.rows_g)
        dn2 = nt(r.h[rows], r.wu[...])
        xhat, rstd = norm_stats(r.mix[rows])
        r.vg[pl.ds(2, 1), :] += colsum(dn2 * xhat)
        r.vg[pl.ds(3, 1), :] += colsum(dn2)
        dmixed = r.gy[rows] + norm_back(xhat, rstd, vec(2), dn2)
        r.gy[rows] = dmixed
        r.gyb[rows] = dmixed.astype(BF16)
    rs2(0)
    for g in range(s.groups):
        rows = pl.ds(g * s.rows_g, s.rows_g)
        dnum = nt(r.gyb[rows], r.w4[3]) / r.den[rows]
        r.dnum[rows] = dnum.astype(BF16)
        r.xo[rows] = (-dnum * r.att[rows].astype(F32)).astype(BF16)
        for b in range(s.tb):
            t = g * s.tb + b
            for ref, fine in ((r.dnl, r.dnum), (r.xol, r.xo)):
                pooled = nn(r.poolq[...], fine[block_rows(t)])
                high = pooled.astype(BF16)
                ref[0, t] = high
                ref[1, t] = (pooled - high.astype(F32)).astype(BF16)

    for g in range(s.groups):
        for p in range(PAIRS):
            lanes = pair_lanes(p)
            d3, x3, d3_low, x3_low = [two(gathered(ref.at[i], g, lanes)) for i in range(2) for ref in (r.dnl, r.xol)]
            x = jnp.concatenate([d3, x3, d3_low, x3_low], 1)
            vn = jnp.concatenate([r.fkv[1, g, :, lanes], eight], 1)
            ef = r.ef[g, p]
            kf = r.fkv[0, g, :, lanes]
            ds = nt(x, jnp.concatenate([vn, vn], 1)) * ef.astype(F32)
            ds = ds.astype(BF16)
            dq3 = (pick(nn(ds, kf)) * 0.125).astype(BF16)
            for b in range(s.tb):
                r.dql[g * s.tb + b, :, lanes] = dq3[b * BLOCK : (b + 1) * BLOCK]
            dkf = tn(ds, two(gathered(r.ql, g, lanes)))
            dvf = tn(ef, d3)
            r.df[g, 0, :, lanes] = dkf
            r.df[g, 1, :, lanes] = dvf
            r.dfs[g, 0, :, lanes] = dkf.astype(BF16)
            r.dfs[g, 1, :, lanes] = dvf.astype(BF16)

    def far_part(zz):
        return r.dfs.at[:, :, pl.ds(pl.multiple_of(zz * s.far_own, s.far_own), s.far_own)]

    for d, zz in enumerate(zs):
        send(far_part(zz), r.rf.at[d], r.fr.at[1], (dp, zz))
    for n in range(FF // D):
        cols = pl.ds(n * D, D)
        r.gu[:, :, :, cols] = tn(r.n2[...], r.h[:, cols]).astype(BF16).reshape(4, 2, D // 8, D)
    rs0(1)
    rs3(0)
    r.go[...] = tn(r.att[...], r.gyb[...]).astype(BF16).reshape(4, 2, D // 8, D)
    rs0(2)
    rs1(1)

    def near_back(t, g, b, p):
        lanes = pair_lanes(p)
        rows = block_rows(t)
        length = length_of(g, b)
        counts0, counts1 = counts(length)
        q2 = two(r.q[rows, lanes])
        ql2 = two(r.ql[t, low48, lanes])
        k0 = r.k[rows, lanes]
        kl = r.kl[t, low48, lanes]
        e0 = r.e0[t * PAIRS + p]
        e1 = r.e1[t * PAIRS + p]
        dn2 = two(r.dnum[rows, lanes])
        dnl2 = two(r.dnl[0, t, low48, lanes])
        x0 = jnp.concatenate([dn2, two(r.xo[rows, lanes])], 1)
        x1 = [dnl2, two(r.xol[0, t, low48, lanes]), two(r.dnl[1, t, low48, lanes]), two(r.xol[1, t, low48, lanes])]
        x1 = jnp.concatenate(x1, 1)
        vn1 = jnp.concatenate([r.vl[t, low48, lanes], counts1], 1)
        ds0 = nt(x0, jnp.concatenate([r.v[rows, lanes], counts0], 1)) * e0.astype(F32)
        ds1 = nt(x1, jnp.concatenate([vn1, vn1], 1)) * e1.astype(F32)
        ds0 = ds0.astype(BF16)
        ds1 = ds1.astype(BF16)
        lr = iota((48, LANES), 0)
        level_scale = jnp.where(lr < 32, 0.5, 0.25)
        dql = (pick(nn(ds1, kl)) * level_scale).astype(BF16)
        dql = jnp.concatenate([dql, r.dql[t, :, lanes]], 0)
        dq = pick(nn(ds0, k0)) + tn(r.poolq[...], dql)
        dk0 = tn(ds0, q2)
        dv0 = tn(e0, dn2)
        dkl = (tn(ds1, ql2) * level_scale).astype(BF16)
        dvl = tn(e1, dnl2).astype(BF16)
        coarse = jnp.concatenate([dkl, dvl], 1)
        if b < s.nb:
            own = pl.ds(b * BLOCK, BLOCK)
            coarse = jnp.concatenate(
                [coarse, jnp.concatenate([r.ft[g, 0, own, lanes], r.ft[g, 1, own, lanes]], 1)], 0
            )
            fine = tn(r.poolk[...], coarse)
        else:
            fine = tn(r.poolk[low48], coarse)
        dk = dk0 + fine[:, :LANES]
        dv = dv0 + fine[:, LANES:]
        if b >= s.nb:
            keep = iota((CONT_LEN, LANES), 0) < length
            dk = jnp.where(keep, dk, 0.0)
            dv = jnp.where(keep, dv, 0.0)
        r.dqkv[p, rows, pl.ds(0, LANES)] = (dq * SCORE).astype(BF16)
        r.dqkv[p, rows, pl.ds(LANES, LANES)] = (dk * SCORE).astype(BF16)
        r.dqkv[p, rows, pl.ds(2 * LANES, LANES)] = dv.astype(BF16)

    def conts_back(g, carry):
        for b in range(s.nb, s.tb):
            for p in range(PAIRS):
                near_back(g * s.tb + b, g, b, p)
        return carry

    lax.fori_loop(0, s.groups, conts_back, 0)
    rs2(1)
    rs1(2)
    wait_recv(r.rf, r.fr.at[1])
    own = pl.ds(pl.multiple_of(z * s.far_own, s.far_own), s.far_own)
    for g in range(s.groups):
        for i, scale in enumerate((1.0 / COARSE, 1.0)):
            total = r.df[g, i, own]
            for d in range(s.nz - 1):
                total = total + r.rf[d, g, i].astype(F32)
            r.ft[g, i] = (total * scale).astype(BF16)
    rs4(0)
    rs2(2)

    def prompts_back(p):
        def body(g, carry):
            for b in range(s.nb):
                near_back(g * s.tb + b, g, b, p)
            return carry

        lax.fori_loop(0, s.groups, body, 0)
        r.gq[p] = tn(r.n1[...], r.dqkv[p]).astype(BF16).reshape(4, 2, D // 8, 3 * LANES)

    prompts_back(0)
    rs0(3)
    rs3(1)
    rs3(2)
    prompts_back(1)
    rs0(4)
    rs1(3)
    prompts_back(2)
    rs0(5)
    rs2(3)
    rs1(4)
    rs4(1)
    prompts_back(3)
    rs0(6)
    rs3(3)
    rs2(4)
    rs1(5)

    for g in range(s.groups):
        rows = pl.ds(g * s.rows_g, s.rows_g)
        dn1 = 0.0
        for j in range(3):
            d = jnp.concatenate([r.dqkv[p, rows, pl.ds(j * LANES, LANES)] for p in range(PAIRS)], 1)
            dn1 = dn1 + nt(d, r.w4[j])
        xhat, rstd = norm_stats(r.x[rows].astype(F32))
        r.vg[pl.ds(0, 1), :] += colsum(dn1 * xhat)
        r.vg[pl.ds(1, 1), :] += colsum(dn1)
        r.gy[rows] = r.gy[rows] + norm_back(xhat, rstd, vec(0), dn1)
        if g == 0:
            rs1(6)
            rs2(5)
            rs3(4)

    outs.append(local([(b, a) for a, b in row_pairs(r.pdx, r.cdx, r.gy)], r.gy))
    if s.exchange:

        def vsend(src, i, dev):
            send(src, r.rv.at[i], r.vr.at[i], dev)

        vsend(r.vg, 0, (sib, z))
        rs2(6)
        rs3(5)
        wait_recv(r.rv.at[0], r.vr.at[0])
        r.vt[0] = r.vg[...] + r.rv[0]
        vsend(r.vt.at[0], 1, (xn, z))
        rs4(2)
        rs4(3)
        rs3(6)
        wait_recv(r.rv.at[1], r.vr.at[1])
        r.vt[1] = r.vt[0] + r.rv[1]
        vsend(r.vt.at[1], 2, (yn, z))
        rs4(4)
        wait_recv(r.rv.at[2], r.vr.at[2])
        r.vt[2] = r.vt[1] + r.rv[2]
        for zz in zs:
            send(r.vt.at[2], r.rv.at[3 + z], r.vr.at[3], (dp, zz))
        rs4(5)
        rs4(6)
        wait_recv(r.rv.at[pl.ds(3, s.nz - 1)], r.vr.at[3])
        r.rv[3 + z] = r.vt[2]
        total = r.rv[3]
        for i in range(1, s.nz):
            total = total + r.rv[3 + i]
        loss = jnp.sum(total[5:6], 1, keepdims=True) / (token_row[:, :1] * float(D))
        mine = jnp.zeros((8, LANES), F32)
        per = LANES // s.r
        for k in range(D // LANES):
            mine = jnp.where(me // per == k, total[:8, k * LANES : (k + 1) * LANES], mine)
        mine = pltpu.roll(mine, lax.rem(LANES - lax.rem(me, per) * s.r, LANES), 1)
        per = LANES // s.rf
        up = jnp.zeros((1, LANES), F32)
        for k in range(FF // LANES):
            i, j = divmod(k, D // LANES)
            up = jnp.where(me // per == k, total[8 + i : 9 + i, j * LANES : (j + 1) * LANES], up)
        up = jnp.broadcast_to(up, (8, LANES))
        up = pltpu.roll(up, lax.rem(LANES - lax.rem(me, per) * s.rf, LANES), 1)
        row = iota((8, LANES), 0)
        r.hv[...] = jnp.where(row < 5, mine, jnp.where(row == 5, loss, up))
        outs.append(local([(r.hv, r.ov)]))
    else:
        r.ov[...] = r.vg[...]
        for src, dst in ((r.gq, r.fgq), (r.go, r.fgo), (r.gu, r.fgu), (r.gd, r.fgd)):
            outs.append(local([(src, dst)]))
    for copy in outs:
        copy.wait()
    for copy in pending.values():
        copy.wait_send()


def finish(n_mats, *refs):
    ov = refs[0]
    srcs = refs[1 : 1 + n_mats]
    dsts = refs[1 + n_mats : 1 + 2 * n_mats]
    vectors = refs[1 + 2 * n_mats : -1 - n_mats]
    held = refs[-1 - n_mats : -1]
    sems = refs[-1]
    reads = [pltpu.make_async_copy(a, b, sems.at[0, i]) for i, (a, b) in enumerate(zip(srcs, held))]
    writes = [pltpu.make_async_copy(a, b, sems.at[1, i]) for i, (a, b) in enumerate(zip(held, dsts))]
    for copy in reads:
        copy.start()
    for i, out in enumerate(vectors):
        out[...] = ov[pl.ds(i, 1), pl.ds(0, out.shape[1])]
    for read, write in zip(reads, writes):
        read.wait()
        write.start()
    for copy in writes:
        copy.wait()


def layer(
    mesh,
    prompt_x,
    cont_x,
    prompt_dy,
    cont_dy,
    teacher,
    cont_lengths,
    loss_scale,
    norm1_gain,
    norm1_bias,
    w_query,
    w_key,
    w_value,
    w_out,
    norm2_gain,
    norm2_bias,
    w_up,
    up_bias,
    w_down,
    down_bias,
):
    nz, ndp = mesh.shape["cont"], mesh.shape["dp"]
    ndev = nz * ndp
    exchange = ndp == 8 and nz == 4
    groups, prompt = prompt_x.shape[:2]
    conts = cont_x.shape[1]
    s = Sizes(groups, prompt, conts, nz, exchange, ndev)
    both = ("dp", "cont")
    any_spec = pl.BlockSpec(memory_space=pl.ANY)
    vmem = pl.BlockSpec(memory_space=pltpu.VMEM)

    inputs = {
        "px": (prompt_x, any_spec),
        "cx": (cont_x, any_spec),
        "pdy": (prompt_dy, any_spec),
        "cdy": (cont_dy, any_spec),
        "te": (teacher, any_spec),
        "lens_in": (cont_lengths.T, any_spec),
        "ls_in": (loss_scale.reshape(1, 1), any_spec),
    }
    weights = {"wq": w_query, "wk": w_key, "wv": w_value, "wo": w_out, "wup": w_up, "wdn": w_down}
    vectors = {"v1g": norm1_gain, "v1b": norm1_bias, "v2g": norm2_gain, "v2b": norm2_bias, "vdb": down_bias}
    if exchange:
        for name, w in weights.items():
            inputs[name] = (w, any_spec)
        for name, v in vectors.items():
            inputs[name] = (v.reshape(1, -1), any_spec)
        inputs["vub"] = (up_bias.reshape(1, -1), any_spec)
    else:
        for name, w in weights.items():
            inputs[name] = (lax.all_gather(w, both, axis=0, tiled=True), any_spec)
        tokens = lax.psum(jnp.sum(cont_lengths).astype(F32), both)
        full = [lax.all_gather(v, both, axis=0, tiled=True).astype(F32) for v in vectors.values()]
        zero = jnp.zeros((D,), F32)
        inputs["vecs"] = (jnp.stack(full + [zero, jnp.full((D,), tokens / (D // LANES)), zero]), vmem)
        up_full = lax.all_gather(up_bias, both, axis=0, tiled=True).astype(F32)
        inputs["upbs"] = (up_full.reshape(1, FF), vmem)

    m, mf = D // 8, FF // 8
    outputs = {
        "py": (prompt_x.shape, BF16, any_spec),
        "cy": (cont_x.shape, BF16, any_spec),
        "pdx": (prompt_x.shape, F32, any_spec),
        "cdx": (cont_x.shape, F32, any_spec),
    }
    if exchange:
        for name in ("ogq", "ogk", "ogv", "ogo"):
            outputs[name] = ((s.r, D), F32, any_spec)
        outputs["ogu"] = ((s.r, FF), F32, any_spec)
        outputs["ogd"] = ((s.rf, D), F32, any_spec)
        outputs["ov"] = ((8, LANES), F32, any_spec)
    else:
        outputs["fgq"] = ((PAIRS, 4, 2, m, 3 * LANES), BF16, any_spec)
        outputs["fgo"] = ((4, 2, m, D), BF16, any_spec)
        outputs["fgu"] = ((4, 2, m, FF), BF16, any_spec)
        outputs["fgd"] = ((4, 2, mf, D), BF16, any_spec)
        outputs["ov"] = ((16, D), F32, vmem)

    rows, blocks = s.rows, s.blocks
    dma = pltpu.SemaphoreType.DMA
    scratch = {
        "w4": ((4, D, D), BF16),
        "wu": ((D, FF), BF16),
        "wd": ((FF, D), BF16),
        "vec": ((8, D), F32),
        "upb": ((1, FF), F32),
        "x": ((rows, D), BF16),
        "dy": ((rows, D), BF16),
        "teach": ((groups * conts, CONT_LEN, D), BF16),
        "y": ((rows, D), BF16),
        "n1": ((rows, D), BF16),
        "q": ((rows, D), BF16),
        "k": ((rows, D), BF16),
        "v": ((rows, D), BF16),
        "ql": ((blocks, 64, D), BF16),
        "kl": ((blocks, 64, D), BF16),
        "vl": ((blocks, 64, D), BF16),
        "fkv": ((2, groups, s.far, D), BF16),
        "poolk": ((64, CONT_LEN), BF16),
        "poolq": ((64, CONT_LEN), BF16),
        "widen": ((CONT_LEN, 96), BF16),
        "bias0": ((2 * CONT_LEN, CONT_LEN), F32),
        "bias1": ((96, 48), F32),
        "biasf": ((2 * s.tb * BLOCK, s.far), F32),
        "e0": ((blocks * PAIRS, 2 * CONT_LEN, CONT_LEN), BF16),
        "e1": ((blocks * PAIRS, 96, 48), BF16),
        "ef": ((groups, PAIRS, 2 * s.tb * BLOCK, s.far), BF16),
        "num": ((rows, D), F32),
        "att": ((rows, D), BF16),
        "den": ((rows, D), F32),
        "mix": ((rows, D), F32),
        "n2": ((rows, D), BF16),
        "h": ((rows, FF), BF16),
        "gy": ((rows, D), F32),
        "gyb": ((rows, D), BF16),
        "dnum": ((rows, D), BF16),
        "xo": ((rows, D), BF16),
        "dnl": ((2, blocks, 64, D), BF16),
        "xol": ((2, blocks, 64, D), BF16),
        "dql": ((blocks, BLOCK, D), BF16),
        "dqkv": ((PAIRS, rows, 3 * LANES), BF16),
        "df": ((groups, 2, s.far, D), F32),
        "dfs": ((groups, 2, s.far, D), BF16),
        "rf": ((nz - 1, groups, 2, s.far_own, D), BF16),
        "ft": ((groups, 2, s.far_own, D), BF16),
        "vg": ((16, D), F32),
        "gq": ((PAIRS, 4, 2, m, 3 * LANES), BF16),
        "go": ((4, 2, m, D), BF16),
        "gu": ((4, 2, m, FF), BF16),
        "gd": ((4, 2, mf, D), BF16),
        "lens": pltpu.SMEM((conts, groups), jnp.int32),
        "ls": pltpu.SMEM((1, 1), F32),
        "lsem": dma((20,)),
        "ss": dma((SENDS,)),
        "fr": dma((2,)),
    }
    if exchange:
        scratch["tiles"] = ((ndev, 8, LANES), F32)
        scratch["build"] = ((8, LANES), F32)
        scratch["small"] = ((5, 1, s.r), BF16)
        scratch["smallup"] = ((1, s.rf), BF16)
        for name in ("q", "k", "v", "o"):
            scratch["hg" + name] = ((s.r, D), F32)
        scratch["hgu"] = ((s.r, FF), F32)
        scratch["hgd"] = ((s.rf, D), F32)
        scratch["hv"] = ((8, LANES), F32)
        for name, lead, rr, cc in (("q", (PAIRS,), m, 3 * LANES), ("o", (), m, D), ("u", (), m, FF), ("d", (), mf, D)):
            scratch["rc" + name] = (lead + (4, rr, cc), BF16)
            scratch["rd" + name] = (lead + (2, rr // 2, cc), BF16)
            scratch["rx" + name] = (lead + (2, rr, cc), BF16)
            scratch["rz" + name] = (lead + (nz - 1, rr // nz, cc), BF16)
        scratch["rv"] = ((3 + nz, 16, D), F32)
        scratch["vt"] = ((3, 16, D), F32)
        scratch["agr"] = dma((5, 10))
        scratch["rsr"] = dma((3 + PAIRS, 5))
        scratch["vr"] = dma((4,))

    names = list(inputs) + list(outputs) + list(scratch)
    results = pl.pallas_call(
        functools.partial(kernel, s, names),
        out_shape=[jax.ShapeDtypeStruct(shape, dtype) for shape, dtype, _ in outputs.values()],
        in_specs=[spec for _, spec in inputs.values()],
        out_specs=[spec for _, _, spec in outputs.values()],
        scratch_shapes=[pltpu.VMEM(*v) if isinstance(v, tuple) else v for v in scratch.values()],
        compiler_params=pltpu.CompilerParams(
            collective_id=0, has_side_effects=True, vmem_limit_bytes=64 * 1024 * 1024 - 65536
        ),
        name="layer",
    )(*[a for a, _ in inputs.values()])
    o = types.SimpleNamespace(**dict(zip(outputs, results)))
    if exchange:
        bulk = ["py", "cy", "pdx", "cdx", "ogq", "ogk", "ogv", "ogo", "ogu", "ogd"]
        shapes = [jax.ShapeDtypeStruct(outputs[k][0], outputs[k][1]) for k in bulk]
        vectors = [jax.ShapeDtypeStruct((1, n), F32) for n in [s.r] * 5 + [1, s.rf]]
        done = pl.pallas_call(
            functools.partial(finish, len(bulk)),
            out_shape=shapes + vectors,
            in_specs=[vmem] + [any_spec] * len(bulk),
            out_specs=[any_spec] * len(bulk) + [vmem] * len(vectors),
            scratch_shapes=[pltpu.VMEM(v.shape, v.dtype) for v in shapes] + [dma((2, len(bulk)))],
            name="finish",
        )(o.ov, *[getattr(o, k) for k in bulk])
        for k, v in zip(bulk, done):
            setattr(o, k, v)
        *vec, loss, up_vec = [v.reshape(-1) for v in done[len(bulk) :]]
        loss = loss.reshape(())
        mats = [o.ogq, o.ogk, o.ogv, o.ogo, o.ogu, o.ogd]
    else:
        three = o.fgq.reshape(PAIRS, D, 3, LANES).transpose(2, 1, 0, 3).reshape(3, D, D)
        whole = [three[0], three[1], three[2], o.fgo, o.fgu, o.fgd]
        whole = [w.reshape(-1, w.shape[-1]).astype(F32) for w in whole]
        parts = [o.ov[i] for i in range(5)] + [o.ov[8:12].reshape(FF)]
        *mats, v0, v1, v2, v3, v4, up_vec = [
            lax.psum_scatter(w, both, scatter_dimension=0, tiled=True) for w in whole + parts
        ]
        vec = [v0, v1, v2, v3, v4]
        loss = lax.psum(jnp.sum(o.ov[5]), both) / (tokens * D)
    return (
        o.py,
        o.cy,
        loss,
        o.pdx,
        o.cdx,
        vec[0],
        vec[1],
        mats[0],
        mats[1],
        mats[2],
        mats[3],
        vec[2],
        vec[3],
        mats[4],
        up_vec,
        mats[5],
        vec[4],
    )


def solution(mesh):
    rows = P("dp", "cont", None)
    conts = P("dp", "cont", None, None)
    vector = P(("dp", "cont"))
    matrix = P(("dp", "cont"), None)
    return jax.shard_map(
        functools.partial(layer, mesh),
        mesh=mesh,
        in_specs=(rows, conts, rows, conts, conts, P("dp", "cont"), P())
        + (vector, vector, matrix, matrix, matrix, matrix, vector, vector, matrix, vector, matrix, vector),
        out_specs=(rows, conts, P(), rows, conts)
        + (vector, vector, matrix, matrix, matrix, matrix, vector, vector, matrix, vector, matrix, vector),
        check_vma=False,
    )
```

```python
import functools
import types

import jax
import jax.numpy as jnp
from jax import lax
from jax.experimental import pallas as pl
from jax.experimental.pallas import tpu as pltpu
from jax.sharding import PartitionSpec as P

D = 512
HEADS = 8
HEAD_DIM = 64
FF = 2048
BLOCK = 16
CONT_LEN = 128
COARSE = CONT_LEN // BLOCK
PAIRS = HEADS // 2
EPS = 1e-5
SCORE = HEAD_DIM**-0.5
LOG2E = 1.4426950408889634
AWAY = -1e30
F32 = jnp.float32
BF16 = jnp.bfloat16
MESH = pl.DeviceIdType.MESH
LANES = 128
SENDS = 24


def nn(a, b):
    return jnp.dot(a, b, preferred_element_type=F32)


def nt(a, b):
    return lax.dot_general(a, b, (((1,), (1,)), ((), ())), preferred_element_type=F32)


def tn(a, b):
    return lax.dot_general(a, b, (((0,), (0,)), ((), ())), preferred_element_type=F32)


def iota(shape, dim):
    return lax.broadcasted_iota(jnp.int32, shape, dim)


def norm_stats(x):
    center = x - jnp.mean(x, -1, keepdims=True)
    rstd = lax.rsqrt(jnp.mean(center * center, -1, keepdims=True) + EPS)
    return center * rstd, rstd


def norm_back(xhat, rstd, gain, dn):
    dxhat = dn * gain
    mean_one = jnp.mean(dxhat, -1, keepdims=True)
    mean_two = jnp.mean(dxhat * xhat, -1, keepdims=True)
    return rstd * (dxhat - mean_one - xhat * mean_two)


def colsum(x):
    return jnp.sum(x, 0, keepdims=True)


class Sizes:
    def __init__(self, groups, prompt, conts, nz, exchange, ndev):
        self.groups = groups
        self.prompt = prompt
        self.conts = conts
        self.nz = nz
        self.exchange = exchange
        self.ndev = ndev
        self.nb = prompt // CONT_LEN
        self.tb = self.nb + conts
        self.rows_g = self.tb * CONT_LEN
        self.rows = groups * self.rows_g
        self.nl = 48 * self.tb
        self.blocks = groups * self.tb
        self.far_own = prompt // COARSE
        self.far = self.far_own * nz
        self.r = D // ndev
        self.rf = FF // ndev


def kernel(s, names, *refs):
    r = types.SimpleNamespace(**dict(zip(names, refs)))
    z = lax.axis_index("cont")
    dp = lax.axis_index("dp")
    zs = [lax.rem(z + d, s.nz) for d in range(1, s.nz)]
    pending = {}
    sent = [0]

    def remote(src, dst, ssem, rsem, dev):
        return pltpu.make_async_remote_copy(
            src_ref=src, dst_ref=dst, send_sem=ssem, recv_sem=rsem, device_id=dev, device_id_type=MESH
        )

    def send(src, dst, rsem, dev, cond=None):
        slot = sent[0] % SENDS
        sent[0] += 1
        if slot in pending:
            left(slot)
        copy = remote(src, dst, r.ss.at[slot], rsem, dev)
        on(cond, copy.start)
        pending[slot] = (cond, copy)

    def on(cond, act):
        if cond is None:
            act()
        else:
            pl.when(cond)(act)

    def left(slot):
        cond, copy = pending[slot]
        on(cond, copy.wait_send)

    def line_send(src, dst, rsem):
        for d, zz in enumerate(zs):
            cond = None
            if s.exchange and d != 1:
                cond = z != (s.nz - 1 if d == 0 else 0)
            send(src, dst, rsem, (dp, zz), cond)

    middle = (z == 1) | (z == 2)
    far_end = jnp.clip(3 * (z - 1), 0, s.nz - 1)

    def line_relay(piece, rsem):
        if s.exchange:
            ref = piece(3 - far_end)
            send(ref, ref, rsem, (dp, far_end), middle)

    def wait_recv(ref, rsem):
        pltpu.make_async_copy(ref, ref, rsem).wait()

    local_count = [0]
    outs = []

    def local(pairs, whole=None):
        sem = r.lsem.at[local_count[0]]
        local_count[0] += 1
        copies = [pltpu.make_async_copy(src, dst, sem) for src, dst in pairs]
        for copy in copies:
            copy.start()
        return copies[0] if whole is None else pltpu.make_async_copy(whole, whole, sem)

    def row_pairs(prompt, cont, rows):
        out = []
        for g in range(s.groups):
            base = g * s.rows_g
            out.append((prompt.at[g], rows.at[pl.ds(base, s.prompt)]))
            for c in range(s.conts):
                out.append((cont.at[g, c], rows.at[pl.ds(base + s.prompt + c * CONT_LEN, CONT_LEN)]))
        return out

    if s.exchange:
        core = lax.rem(dp, 2)
        ix = lax.rem(dp // 2, 2)
        iy = dp // 4
        sib = dp + 1 - 2 * core
        xn = dp + 2 - 4 * ix
        yn = dp + 4 - 8 * iy
        cell = dp // 2
        cell_x = cell + 1 - 2 * ix
        cell_y = cell + 2 - 4 * iy
        cell_d = cell_x + cell_y - cell
        sibcore = 1 - core
        me = dp * s.nz + z

        def view(k, a, n, part=None):
            if k == 0:
                return r.tiles.at[pl.ds(a, n)]
            ref, rows = (r.w4, s.r) if k < 5 else (r.wu, s.r) if k == 5 else (r.wd, s.rf)
            place = pl.ds(pl.multiple_of(a * rows, rows), n * rows)
            width = ref.shape[-1]
            cols = pl.ds(0, width) if part is None else pl.ds(part * (width // 2), width // 2)
            if k < 5:
                return ref.at[(1, 2, 0, 3)[k - 1], place, cols]
            return ref.at[place, cols]

        def shard(c, co, zz):
            return (c * 2 + co) * s.nz + zz

        def ag_sem(k, kind, wave):
            return r.agw.at[kind - 1] if wave and 0 < kind < 5 else r.agr.at[k, kind]

        def ag_move(k, kind, a, n, dev, part=None, wave=0):
            v = view(k, a, n, part)
            send(v, v, ag_sem(k, kind, wave), dev)

        def ag_got(k, kind, n, part=None, wave=0):
            wait_recv(view(k, 0, n, part), ag_sem(k, kind, wave))

        def ag_z(k):
            own = view(k, me, 1)
            line_send(own, own, ag_sem(k, 0, 0))

        def ag_out(k, wave, starts, n):
            if wave == 1 or n > 1:
                ag_got(k, 0, s.nz - 1)
                line_relay(lambda zz: view(k, dp * s.nz + zz, 1), ag_sem(k, 0, 0))
            for zz in starts:
                a = shard(cell, core, zz)
                ag_move(k, 1, a, n, (xn, z), None, wave)
                ag_move(k, 2, a, n, (yn, z), None, wave)
            for zz in starts:
                ag_move(k, 5, shard(cell, core, zz), n, (sib, z))

        def ag_pass(k, wave, starts, n):
            total = len(starts) * n
            ag_got(k, 1, total, None, wave)
            for zz in starts:
                ag_move(k, 3, shard(cell_x, core, zz), n, (yn, z), 0, wave)
            ag_got(k, 2, total, None, wave)
            if k > 0:
                for zz in starts:
                    ag_move(k, 4, shard(cell_y, core, zz), n, (xn, z), 1, wave)
            for zz in starts:
                ag_move(k, 5, shard(cell_x, core, zz), n, (sib, z))
                ag_move(k, 5, shard(cell_y, core, zz), n, (sib, z))

        def ag_last(k, wave, starts, n):
            total = len(starts) * n
            ag_got(k, 3, total, 0, wave)
            if k > 0:
                ag_got(k, 4, total, 1, wave)
            for zz in starts:
                ag_move(k, 5, shard(cell_d, core, zz), n, (sib, z))

        def ag1(k):
            ag_out(k, 0, [0], s.nz)

        def ag2(k):
            ag_pass(k, 0, [0], s.nz)

        def ag3(k):
            ag_last(k, 0, [0], s.nz)

        def ag4(k):
            ag_got(k, 5, 4 * s.nz)

        grads = [(r.gd.at[...], r.rcd, r.rdd, r.rxd, r.rzd), (r.gu.at[...], r.rcu, r.rdu, r.rxu, r.rzu),
                 (r.go.at[...], r.rco, r.rdo, r.rxo, r.rzo)]
        for p in range(PAIRS):
            grads.append((r.gq.at[p], r.rcq.at[p], r.rdq.at[p], r.rxq.at[p], r.rzq.at[p]))

        def rs0(k):
            g, rc, _, _, _ = grads[k]
            send(g.at[:, sibcore], rc, r.rsr.at[k, 0], (sib, z))

        def add_to(g, c, lo, n, term):
            place = (c, core, pl.ds(lo, n))
            g[place] = (g[place].astype(F32) + term.astype(F32)).astype(BF16) if term.dtype == F32 else g[place] + term

        def rs1(k):
            g, rc, rd, _, _ = grads[k]
            m = g.shape[2]
            wait_recv(rc, r.rsr.at[k, 0])
            add_to(g, cell_d, 0, m, rc[cell_d])
            mh = m // 2
            send(g.at[cell_d, core, pl.ds(0, mh)], rd.at[0], r.rsr.at[k, 1], (yn, z))
            send(g.at[cell_d, core, pl.ds(mh, mh)], rd.at[1], r.rsr.at[k, 2], (xn, z))
            for c in (cell_x, cell_y, cell):
                add_to(g, c, 0, m, rc[c])

        def rs2(k):
            g, _, rd, rx, _ = grads[k]
            mh = g.shape[2] // 2
            wait_recv(rd.at[0], r.rsr.at[k, 1])
            add_to(g, cell_x, 0, mh, rd[0])
            send(g.at[cell_x, core], rx.at[0], r.rsr.at[k, 3], (xn, z))
            wait_recv(rd.at[1], r.rsr.at[k, 2])
            add_to(g, cell_y, mh, mh, rd[1])
            send(g.at[cell_y, core], rx.at[1], r.rsr.at[k, 3], (yn, z))

        def piece(g, zz):
            n = g.shape[2] // s.nz
            return pl.ds(pl.multiple_of(zz * n, n), n)

        def rs3(k):
            g, _, _, rx, rz = grads[k]
            wait_recv(rx, r.rsr.at[k, 3])
            add_to(g, cell, 0, g.shape[2], rx[0].astype(F32) + rx[1].astype(F32))
            for d, zz in enumerate(zs):
                send(g.at[cell, core, piece(g, zz)], rz.at[d], r.rsr.at[k, 4], (dp, zz))

        def rs4(k):
            g, _, _, _, rz = grads[k]
            wait_recv(rz, r.rsr.at[k, 4])
            total = g[cell, core, piece(g, z)].astype(F32)
            for d in range(s.nz - 1):
                total = total + rz[d].astype(F32)
            if k < 3:
                held, out = ((r.hgd, r.ogd), (r.hgu, r.ogu), (r.hgo, r.ogo))[k]
                held[...] = total
                outs.append(local([(held, out)]))
            else:
                lanes = pl.ds((k - 3) * LANES, LANES)
                for j, (held, out) in enumerate(((r.hgq, r.ogq), (r.hgk, r.ogk), (r.hgv, r.ogv))):
                    held[:, lanes] = total[:, j * LANES : (j + 1) * LANES]
                    if k == 2 + PAIRS:
                        outs.append(local([(held, out)]))
    else:

        def nothing(*_):
            return None

        ag1 = ag2 = ag3 = ag4 = ag_z = ag_out = ag_pass = ag_last = nothing
        rs0 = rs1 = rs2 = rs3 = rs4 = nothing

    scalars_in = [local([(r.lens_in, r.lens)]), local([(r.ls_in, r.ls)])]
    if s.exchange:
        vectors_in = (r.v1g, r.v1b, r.v2g, r.v2b, r.vdb)
        scalars_in.append(local([(v, r.small.at[i]) for i, v in enumerate(vectors_in)], r.small))
        scalars_in.append(local([(r.vub, r.smallup)]))
        own_rows = pl.ds(pl.multiple_of(me * s.r, s.r), s.r)
        weights_in = [
            local([(w, r.w4.at[j, own_rows]) for j, w in enumerate((r.wq, r.wk, r.wv, r.wo))], r.w4.at[:, own_rows]),
            local([(r.wup, view(5, me, 1))]),
            local([(r.wdn, view(6, me, 1))]),
        ]
    else:
        weights_in = [local([(w, r.w4.at[j]) for j, w in enumerate((r.wq, r.wk, r.wv, r.wo))], r.w4)]
        weights_in += [local([(r.wup, r.wu)]), local([(r.wdn, r.wd)])]
    barrier = pltpu.get_barrier_semaphore()
    partners = [(dp, zz) for zz in zs]
    if s.exchange:
        partners += [(sib, z), (xn, z), (yn, z)]
    for dev in partners:
        pl.semaphore_signal(barrier, inc=1, device_id=dev, device_id_type=MESH)
    x_in = [local(row_pairs(r.px, r.cx, r.x), r.x)]
    teach_pairs = [(r.te.at[g, c], r.teach.at[g * s.conts + c]) for g in range(s.groups) for c in range(s.conts)]
    later_in = [local(row_pairs(r.pdy, r.cdy, r.dy), r.dy), local(teach_pairs, r.teach)]

    for copy in scalars_in:
        copy.wait()
    if s.exchange:
        r.build[...] = jnp.zeros_like(r.build)
        for i in range(5):
            r.build[pl.ds(i, 1), pl.ds(0, s.r)] = r.small[i].astype(F32)
        r.build[pl.ds(5, 1), pl.ds(0, s.rf)] = r.smallup[...].astype(F32)
        own_tokens = 0
        for g in range(s.groups):
            for c in range(s.conts):
                own_tokens = own_tokens + r.lens[c, g]
        tile = r.build[...]
        row = iota((8, LANES), 0)
        placed = jnp.where(
            row < 5,
            pltpu.roll(tile, lax.rem(me, LANES // s.r) * s.r, 1),
            pltpu.roll(tile, lax.rem(me, LANES // s.rf) * s.rf, 1),
        )
        r.tiles[me] = jnp.where(row == 6, own_tokens.astype(F32), placed)

    for copy in weights_in:
        copy.wait()
    pl.semaphore_wait(barrier, len(partners))
    first, rest = [z], zs
    ag_z(0)
    ag_z(1)
    ag_out(1, 0, first, 1)
    ag_z(2)

    ri = iota((64, CONT_LEN), 0)
    ci = iota((64, CONT_LEN), 1)
    coarse_ci = jnp.where(ri < 32, ci >> 1, jnp.where(ri < 48, ci >> 2, ci >> 3))
    position = jnp.where(ri < 16, ri, jnp.where(ri < 32, ri + 16, jnp.where(ri < 48, ri - 32, ri - 48)))
    r.poolk[...] = jnp.where(coarse_ci == position, 1.0, 0.0).astype(BF16)
    position = jnp.where(ri < 48, position + 16, position)
    r.poolq[...] = jnp.where(coarse_ci == position, 1.0, 0.0).astype(BF16)
    r.pq3[...] = jnp.zeros_like(r.pq3)
    r.pk3[...] = jnp.zeros_like(r.pk3)
    for b in range(s.tb):
        cols = pl.ds(b * CONT_LEN, CONT_LEN)
        for first_row in (0, s.nl):
            r.pq3[pl.ds(first_row + b * 48, 48), cols] = r.poolq[pl.ds(0, 48)]
        r.pq3[pl.ds(2 * s.nl + b * BLOCK, BLOCK), cols] = r.poolq[pl.ds(48, BLOCK)]
        r.pk3[pl.ds(b * 48, 48), cols] = r.poolk[pl.ds(0, 48)]
    ri = iota((CONT_LEN, CONT_LEN), 0)
    ci = iota((CONT_LEN, CONT_LEN), 1)
    bi, bj = ri >> 4, ci >> 4
    near = ((bi == bj) & (ci <= ri)) | (((bi & 1) == 1) & (bj == bi - 1))
    near = jnp.where(near, 0.0, AWAY)
    r.bias0[pl.ds(0, CONT_LEN)] = near
    r.bias0[pl.ds(CONT_LEN, CONT_LEN)] = near
    ri = iota((2 * s.nl, s.nl), 0)
    ri = jnp.where(ri >= s.nl, ri - s.nl, ri)
    r.bias1[...] = jnp.where((ri >> 4) == (iota((2 * s.nl, s.nl), 1) >> 4), 0.0, AWAY)
    nq = s.tb * BLOCK
    blk = lax.rem(iota((2 * nq, s.far), 0), nq) >> 4
    limit = jnp.where(blk >= s.nb, s.far, BLOCK * (z * s.nb + blk))
    r.biasf[...] = jnp.where(iota((2 * nq, s.far), 1) < limit, 0.0, AWAY)
    scale_rows = iota((64, D), 0)
    mean_scale = jnp.where(scale_rows < 32, 0.5, jnp.where(scale_rows < 48, 0.25, 0.125))
    r.vg[...] = jnp.zeros_like(r.vg)

    ag_pass(1, 0, first, 1)
    ag1(0)
    ag_out(1, 1, rest, 1)
    ag_z(3)
    ag_last(1, 0, first, 1)
    ag1(2)
    ag_z(4)
    ag_z(5)
    ag2(0)
    ag_pass(1, 1, rest, 1)
    ag1(3)
    ag3(0)
    ag_z(6)
    ag_last(1, 1, rest, 1)
    ag2(2)
    ag4(0)
    if s.exchange:
        count = 8
        for k in range(s.ndev // count):
            part = jnp.sum(r.tiles[pl.ds(k * count, count)], 0)
            r.vec[:, pl.ds(k * LANES, LANES)] = part
        for k in range(s.ndev // 2):
            part = r.tiles[2 * k] + r.tiles[2 * k + 1]
            r.upb[:, pl.ds(k * LANES, LANES)] = part[5:6]
    else:
        r.vec[...] = r.vecs[...]
        r.upb[...] = r.upbs[...]

    def vec(i):
        return r.vec[pl.ds(i, 1), :]

    token_row = r.vec[pl.ds(6, 1), pl.ds(0, LANES)]
    for k in range(1, D // LANES):
        token_row = token_row + r.vec[pl.ds(6, 1), pl.ds(k * LANES, LANES)]
    token_row = jnp.concatenate([token_row] * (D // LANES), 1)

    def length_of(g, b):
        if isinstance(b, int):
            return CONT_LEN if b < s.nb else r.lens[b - s.nb, g]
        c = jnp.clip(b - s.nb, 0, s.conts - 1)
        return jnp.where(b >= s.nb, r.lens[c, g], CONT_LEN)

    def block_rows(t):
        if isinstance(t, int):
            return pl.ds(t * CONT_LEN, CONT_LEN)
        return pl.ds(pl.multiple_of(t * CONT_LEN, CONT_LEN), CONT_LEN)

    for copy in x_in:
        copy.wait()

    def norm_one(i, carry):
        rows = block_rows(i)
        xhat, _ = norm_stats(r.x[rows].astype(F32))
        r.n1[rows] = (xhat * vec(0) + vec(1)).astype(BF16)
        return carry

    lax.fori_loop(0, s.blocks, norm_one, 0)
    ag2(3)
    ag4(1)

    def project(j, out, pools):
        for g in range(s.groups):
            rows = pl.ds(g * s.rows_g, s.rows_g)
            value = nn(r.n1[rows], r.w4[j])
            parts = [value[: s.prompt]]
            for c in range(s.conts):
                lo = s.prompt + c * CONT_LEN
                part = value[lo : lo + CONT_LEN]
                if j > 0:
                    part = jnp.where(iota((CONT_LEN, D), 0) < r.lens[c, g], part, 0.0)
                parts.append(part)
            value = jnp.concatenate(parts, 0).astype(BF16)
            out[rows] = value
            pool, pooled, scale = pools
            for b in range(s.tb):
                pooled[g * s.tb + b] = (nn(pool[...], value[b * CONT_LEN : (b + 1) * CONT_LEN]) * scale).astype(BF16)

    project(1, r.k, (r.poolk, r.kl, mean_scale))
    ag3(2)
    ag1(4)
    ag1(5)
    ag4(2)
    project(2, r.v, (r.poolk, r.vl, 1.0))
    for g in range(s.groups):
        for b in range(s.nb):
            place = pl.ds(pl.multiple_of(z * s.far_own + b * BLOCK, BLOCK), BLOCK)
            r.fkv[0, g, place] = r.kl[g * s.tb + b, pl.ds(48, BLOCK)]
            r.fkv[1, g, place] = r.vl[g * s.tb + b, pl.ds(48, BLOCK)]

    def far_rows(zz):
        return r.fkv.at[:, :, pl.ds(pl.multiple_of(zz * s.far_own, s.far_own), s.far_own)]

    line_send(far_rows(z), far_rows(z), r.fr.at[0])

    def far_got():
        wait_recv(r.fkv.at[:, :, pl.ds(0, s.far - s.far_own)], r.fr.at[0])

    ag3(3)
    ag2(4)
    ag4(3)
    project(0, r.q, (r.poolq, r.ql, mean_scale))
    ag2(5)
    ag1(6)

    def two(a):
        low = iota(a.shape, 1) < HEAD_DIM
        zero = jnp.zeros_like(a)
        return jnp.concatenate([jnp.where(low, a, zero), jnp.where(low, zero, a)], 0)

    def pick(a):
        n = a.shape[0] // 2
        return jnp.where(iota((n, LANES), 1) < HEAD_DIM, a[:n], a[n:])

    def counts(length):
        i0 = iota((CONT_LEN, LANES), 0)
        counts0 = jnp.where(i0 < length, 1.0, 0.0).astype(BF16)
        i1 = iota((48, LANES), 0)
        first = jnp.where(i1 < 16, 2 * i1, jnp.where(i1 < 32, 2 * (i1 + 16), 4 * (i1 - 32)))
        width = jnp.where(i1 < 32, 2, 4)
        counts1 = jnp.clip(length - first, 0, width).astype(F32).astype(BF16)
        return counts0, counts1

    def pair_lanes(p):
        return pl.ds(p * LANES, LANES)

    low48 = pl.ds(0, 48)
    far16 = pl.ds(48, BLOCK)

    def near(t, carry):
        g, b = t // s.tb, lax.rem(t, s.tb)
        rows = block_rows(t)
        counts0, _ = counts(length_of(g, b))
        for p in range(PAIRS):
            lanes = pair_lanes(p)
            e0 = jnp.exp2(nt(two(r.q[rows, lanes]), r.k[rows, lanes]) * (SCORE * LOG2E) + r.bias0[...])
            e0 = e0.astype(BF16)
            r.e0[t * PAIRS + p] = e0
            t0 = nn(e0, jnp.concatenate([r.v[rows, lanes], counts0], 1))
            r.num[rows, lanes] = pick(t0[:, :LANES])
            r.den[rows, lanes] = pick(t0[:, LANES:])
        return carry

    eight = jnp.full((s.far, LANES), float(COARSE), BF16)

    def gathered(ref, g, lanes, part=None):
        part = far16 if part is None else part
        return jnp.concatenate([ref[g * s.tb + b, part, lanes] for b in range(s.tb)], 0)

    def coarse_values(g, lanes):
        widths = jnp.concatenate([counts(length_of(g, b))[1] for b in range(s.tb)], 0)
        return jnp.concatenate([gathered(r.vl, g, lanes, low48), widths], 1)

    def group_rows(g):
        if isinstance(g, int):
            return pl.ds(g * s.rows_g, s.rows_g)
        return pl.ds(pl.multiple_of(g * s.rows_g, CONT_LEN), s.rows_g)

    def coarse_forward(g):
        rows = group_rows(g)
        for p in range(PAIRS):
            lanes = pair_lanes(p)
            e1 = nt(two(gathered(r.ql, g, lanes, low48)), gathered(r.kl, g, lanes, low48))
            e1 = jnp.exp2(e1 * (SCORE * LOG2E) + r.bias1[...]).astype(BF16)
            r.e1[g, p] = e1
            t1 = nn(e1, coarse_values(g, lanes))
            t1 = jnp.concatenate([pick(t1[:, :LANES]), pick(t1[:, LANES:])], 1)
            high = t1.astype(BF16)
            both = jnp.concatenate([high, (t1 - high.astype(F32)).astype(BF16)], 0)
            t1 = tn(r.pq3[pl.ds(0, 2 * s.nl)], both)
            r.num[rows, lanes] += t1[:, :LANES]
            r.den[rows, lanes] += t1[:, LANES:]

    def repeat_rows(a):
        n = a.shape[0]
        return jnp.broadcast_to(a[:, None, :], (n, COARSE, LANES)).reshape(n * COARSE, LANES)

    def far_forward(g):
        rows = pl.ds(g * s.rows_g, s.rows_g)
        for p in range(PAIRS):
            lanes = pair_lanes(p)
            ef = nt(two(gathered(r.ql, g, lanes)), r.fkv[0, g, :, lanes]) * (SCORE * LOG2E) + r.biasf[...]
            ef = jnp.exp2(ef).astype(BF16)
            r.ef[g, p] = ef
            total = nn(ef, jnp.concatenate([r.fkv[1, g, :, lanes], eight], 1))
            denominator = r.den[rows, lanes] + repeat_rows(pick(total[:, LANES:]))
            numerator = r.num[rows, lanes] + repeat_rows(pick(total[:, :LANES]))
            r.den[rows, lanes] = denominator
            r.att[rows, lanes] = (numerator / denominator).astype(BF16)

    lax.fori_loop(0, s.tb, near, 0)
    ag3(4)
    ag3(5)
    ag2(6)
    if s.exchange:
        on(middle, far_got)
    line_relay(far_rows, r.fr.at[0])
    coarse_forward(0)
    lax.fori_loop(s.tb, s.blocks, near, 0)
    for g in range(1, s.groups):
        coarse_forward(g)
    on(jnp.logical_not(middle) if s.exchange else None, far_got)
    for g in range(s.groups):
        far_forward(g)
    ag4(4)
    ag3(6)

    for copy in later_in:
        copy.wait()
    for g in range(s.groups):
        rows = pl.ds(g * s.rows_g, s.rows_g)
        mixed = r.x[rows].astype(F32) + nn(r.att[rows], r.w4[3])
        r.mix[rows] = mixed
        xhat, _ = norm_stats(mixed)
        r.n2[rows] = (xhat * vec(2) + vec(3)).astype(BF16)
    ag4(5)
    for g in range(s.groups):
        rows = pl.ds(g * s.rows_g, s.rows_g)
        for n in range(FF // D):
            cols = pl.ds(n * D, D)
            pre = nn(r.n2[rows], r.wu[:, cols]) + r.upb[:, cols]
            r.h[rows, cols] = jnp.maximum(pre, 0.0).astype(BF16)
    ag4(6)
    extra = 2.0 * r.ls[0, 0] / (token_row * float(D))
    for g in range(s.groups):
        base = g * s.rows_g
        rows = pl.ds(base, s.rows_g)
        y = r.mix[rows] + nn(r.h[rows], r.wd[...]) + vec(4)
        r.y[rows] = y.astype(BF16)
        gy = r.dy[rows].astype(F32)
        parts = [gy[: s.prompt]]
        for c in range(s.conts):
            lo = s.prompt + c * CONT_LEN
            keep = iota((CONT_LEN, D), 0) < r.lens[c, g]
            diff = jnp.where(keep, y[lo : lo + CONT_LEN] - r.teach[g * s.conts + c].astype(F32), 0.0)
            r.vg[pl.ds(5, 1), :] += colsum(diff * diff)
            parts.append(gy[lo : lo + CONT_LEN] + extra * diff)
        gy = jnp.concatenate(parts, 0)
        r.gy[rows] = gy
        r.gyb[rows] = gy.astype(BF16)
        r.vg[pl.ds(4, 1), :] += colsum(gy)

    outs.append(local([(b, a) for a, b in row_pairs(r.py, r.cy, r.y)], r.y))

    for n in range(FF // D):
        cols = pl.ds(n * D, D)
        r.gd[n] = tn(r.h[:, cols], r.gyb[...]).astype(BF16).reshape(2, FF // 8, D)
    rs0(0)
    for n in range(FF // D):
        cols = pl.ds(n * D, D)
        for g in range(s.groups):
            rows = pl.ds(g * s.rows_g, s.rows_g)
            dh = nt(r.gyb[rows], r.wd[cols])
            dpre = jnp.where(r.h[rows, cols] > 0, dh, 0.0).astype(BF16)
            r.h[rows, cols] = dpre
            r.vg[pl.ds(8 + n, 1), :] += colsum(dpre.astype(F32))
    rs1(0)
    for g in range(s.groups):
        rows = pl.ds(g * s.rows_g, s.rows_g)
        dn2 = nt(r.h[rows], r.wu[...])
        xhat, rstd = norm_stats(r.mix[rows])
        r.vg[pl.ds(2, 1), :] += colsum(dn2 * xhat)
        r.vg[pl.ds(3, 1), :] += colsum(dn2)
        dmixed = r.gy[rows] + norm_back(xhat, rstd, vec(2), dn2)
        r.gy[rows] = dmixed
        r.gyb[rows] = dmixed.astype(BF16)
    for g in range(s.groups):
        rows = pl.ds(g * s.rows_g, s.rows_g)
        dnum = nt(r.gyb[rows], r.w4[3]) / r.den[rows]
        r.dnum[rows] = dnum.astype(BF16)
        r.xo[rows] = (-dnum * r.att[rows].astype(F32)).astype(BF16)
        for b in range(s.tb):
            t = g * s.tb + b
            for ref, fine in ((r.dnl, r.dnum), (r.xol, r.xo)):
                pooled = nn(r.poolq[...], fine[block_rows(t)])
                high = pooled.astype(BF16)
                ref[0, t] = high
                ref[1, t] = (pooled - high.astype(F32)).astype(BF16)

    rs2(0)
    for g in range(s.groups):
        for p in range(PAIRS):
            lanes = pair_lanes(p)
            d3, x3, d3_low, x3_low = [two(gathered(ref.at[i], g, lanes)) for i in range(2) for ref in (r.dnl, r.xol)]
            x = jnp.concatenate([d3, x3, d3_low, x3_low], 1)
            vn = jnp.concatenate([r.fkv[1, g, :, lanes], eight], 1)
            ef = r.ef[g, p]
            kf = r.fkv[0, g, :, lanes]
            ds = nt(x, jnp.concatenate([vn, vn], 1)) * ef.astype(F32)
            ds = ds.astype(BF16)
            dq3 = (pick(nn(ds, kf)) * 0.125).astype(BF16)
            for b in range(s.tb):
                r.dql[g * s.tb + b, :, lanes] = dq3[b * BLOCK : (b + 1) * BLOCK]
            dkf = tn(ds, two(gathered(r.ql, g, lanes)))
            dvf = tn(ef, d3)
            r.df[g, 0, :, lanes] = dkf
            r.df[g, 1, :, lanes] = dvf
            r.dfs[g, 0, :, lanes] = dkf.astype(BF16)
            r.dfs[g, 1, :, lanes] = dvf.astype(BF16)

    def far_part(zz):
        return r.dfs.at[:, :, pl.ds(pl.multiple_of(zz * s.far_own, s.far_own), s.far_own)]

    for d, zz in enumerate(zs):
        send(far_part(zz), r.rf.at[d], r.fr.at[1], (dp, zz))
    for n in range(FF // D):
        cols = pl.ds(n * D, D)
        r.gu[:, :, :, cols] = tn(r.n2[...], r.h[:, cols]).astype(BF16).reshape(4, 2, D // 8, D)
    rs0(1)
    r.go[...] = tn(r.att[...], r.gyb[...]).astype(BF16).reshape(4, 2, D // 8, D)
    rs0(2)

    def pair_back(p, g):
        lanes = pair_lanes(p)
        e1 = r.e1[g, p]
        q1 = two(gathered(r.ql, g, lanes, low48))
        k1 = gathered(r.kl, g, lanes, low48)
        d1, x1, d1_low, x1_low = [
            two(gathered(ref.at[i], g, lanes, low48)) for i in range(2) for ref in (r.dnl, r.xol)
        ]
        vn1 = coarse_values(g, lanes)
        ds1 = nt(jnp.concatenate([d1, x1, d1_low, x1_low], 1), jnp.concatenate([vn1, vn1], 1))
        ds1 = (ds1 * e1.astype(F32)).astype(BF16)
        lr = lax.rem(iota((s.nl, LANES), 0), 48)
        level_scale = jnp.where(lr < 32, 0.5, 0.25)
        dql = (pick(nn(ds1, k1)) * level_scale).astype(BF16)
        dql = jnp.concatenate([dql] + [r.dql[g * s.tb + b, :, lanes] for b in range(s.tb)], 0)
        fine_q = tn(r.pq3[pl.ds(s.nl, s.nl + s.tb * BLOCK)], dql)
        dkl = (tn(ds1, q1) * level_scale).astype(BF16)
        dvl = tn(e1, d1).astype(BF16)
        fine = tn(r.pk3[...], jnp.concatenate([dkl, dvl], 1))
        for b in range(s.tb):
            t = g * s.tb + b
            rows = block_rows(t)
            length = length_of(g, b)
            counts0, _ = counts(length)
            q2 = two(r.q[rows, lanes])
            e0 = r.e0[t * PAIRS + p]
            dn2 = two(r.dnum[rows, lanes])
            x0 = jnp.concatenate([dn2, two(r.xo[rows, lanes])], 1)
            ds0 = nt(x0, jnp.concatenate([r.v[rows, lanes], counts0], 1)) * e0.astype(F32)
            ds0 = ds0.astype(BF16)
            part = slice(b * CONT_LEN, (b + 1) * CONT_LEN)
            dq = pick(nn(ds0, r.k[rows, lanes])) + fine_q[part]
            dkv = tn(jnp.concatenate([ds0, e0], 1), jnp.concatenate([q2, dn2], 1))
            dk = (dkv[:CONT_LEN, :LANES] + fine[part, :LANES]) * SCORE
            dv = dkv[CONT_LEN:, LANES:] + fine[part, LANES:]
            r.dqkv[p, rows, pl.ds(0, LANES)] = (dq * SCORE).astype(BF16)
            if b >= s.nb:
                keep = iota((CONT_LEN, LANES), 0) < length
                dk = jnp.where(keep, dk, 0.0)
                dv = jnp.where(keep, dv, 0.0)
            elif p == 0:
                r.num[rows, pl.ds(0, LANES)] = dk
                r.num[rows, pl.ds(LANES, LANES)] = dv
                continue
            else:
                far_k, far_v = far_terms(p, g, b)
                dk = dk + far_k
                dv = dv + far_v
            r.dqkv[p, rows, pl.ds(LANES, LANES)] = dk.astype(BF16)
            r.dqkv[p, rows, pl.ds(2 * LANES, LANES)] = dv.astype(BF16)

    def far_terms(p, g, b):
        own = pl.ds(b * BLOCK, BLOCK)
        lanes = pair_lanes(p)
        return repeat_rows(r.ft[g, 0, own, lanes]), repeat_rows(r.ft[g, 1, own, lanes])

    def each_group(p):
        def body(g, carry):
            pair_back(p, g)
            return carry

        lax.fori_loop(0, s.groups, body, 0)

    each_group(0)
    rs1(1)
    rs1(2)
    rs3(0)
    wait_recv(r.rf, r.fr.at[1])
    own = pl.ds(pl.multiple_of(z * s.far_own, s.far_own), s.far_own)
    for g in range(s.groups):
        for i, scale in enumerate((SCORE / COARSE, 1.0)):
            total = r.df[g, i, own]
            for d in range(s.nz - 1):
                total = total + r.rf[d, g, i].astype(F32)
            r.ft[g, i] = total.astype(BF16).astype(F32) * scale
    for g in range(s.groups):
        for b in range(s.nb):
            rows = block_rows(g * s.tb + b)
            far_k, far_v = far_terms(0, g, b)
            r.dqkv[0, rows, pl.ds(LANES, LANES)] = (r.num[rows, pl.ds(0, LANES)] + far_k).astype(BF16)
            r.dqkv[0, rows, pl.ds(2 * LANES, LANES)] = (r.num[rows, pl.ds(LANES, LANES)] + far_v).astype(BF16)

    def prompts_back(p):
        if p > 0:
            each_group(p)
        r.gq[p] = tn(r.n1[...], r.dqkv[p]).astype(BF16).reshape(4, 2, D // 8, 3 * LANES)

    def dn1_part(p, g):
        rows = pl.ds(g * s.rows_g, s.rows_g)
        w = jnp.concatenate([r.w4[j, :, pair_lanes(p)] for j in range(3)], 1)
        return nt(r.dqkv[p, rows], w)

    def dn1_add(p):
        for g in range(s.groups):
            rows = pl.ds(g * s.rows_g, s.rows_g)
            part = dn1_part(p, g)
            r.num[rows] = part if p == 0 else r.num[rows] + part

    prompts_back(0)
    rs0(3)
    rs2(1)
    rs2(2)
    dn1_add(0)
    rs1(3)
    prompts_back(1)
    rs0(4)
    rs4(0)
    dn1_add(1)
    rs1(4)
    rs2(3)
    prompts_back(2)
    rs0(5)
    rs3(1)
    rs3(2)
    dn1_add(2)
    rs2(4)
    rs1(5)
    rs3(3)
    prompts_back(3)
    rs0(6)
    rs2(5)

    for g in range(s.groups):
        rows = pl.ds(g * s.rows_g, s.rows_g)
        dn1 = r.num[rows] + dn1_part(PAIRS - 1, g)
        xhat, rstd = norm_stats(r.x[rows].astype(F32))
        r.vg[pl.ds(0, 1), :] += colsum(dn1 * xhat)
        r.vg[pl.ds(1, 1), :] += colsum(dn1)
        r.gy[rows] = r.gy[rows] + norm_back(xhat, rstd, vec(0), dn1)
        if g == 0:
            rs1(6)
            rs3(4)

    outs.append(local([(b, a) for a, b in row_pairs(r.pdx, r.cdx, r.gy)], r.gy))
    if s.exchange:

        def vsend(src, i, dev):
            send(src, r.rv.at[i], r.vr.at[i], dev)

        vsend(r.vg, 0, (sib, z))
        rs2(6)
        wait_recv(r.rv.at[0], r.vr.at[0])
        r.vt[0] = r.vg[...] + r.rv[0]
        vsend(r.vt.at[0], 1, (xn, z))
        rs3(5)
        rs4(1)
        wait_recv(r.rv.at[1], r.vr.at[1])
        r.vt[1] = r.vt[0] + r.rv[1]
        vsend(r.vt.at[1], 2, (yn, z))
        rs4(2)
        rs3(6)
        wait_recv(r.rv.at[2], r.vr.at[2])
        r.vt[2] = r.vt[1] + r.rv[2]
        for zz in zs:
            send(r.vt.at[2], r.rv.at[3 + z], r.vr.at[3], (dp, zz))
        rs4(3)
        rs4(4)
        rs4(5)
        rs4(6)
        wait_recv(r.rv.at[pl.ds(3, s.nz - 1)], r.vr.at[3])
        r.rv[3 + z] = r.vt[2]
        total = r.rv[3]
        for i in range(1, s.nz):
            total = total + r.rv[3 + i]
        loss = jnp.sum(total[5:6], 1, keepdims=True) / (token_row[:, :1] * float(D))
        mine = jnp.zeros((8, LANES), F32)
        per = LANES // s.r
        for k in range(D // LANES):
            mine = jnp.where(me // per == k, total[:8, k * LANES : (k + 1) * LANES], mine)
        mine = pltpu.roll(mine, lax.rem(LANES - lax.rem(me, per) * s.r, LANES), 1)
        per = LANES // s.rf
        up = jnp.zeros((1, LANES), F32)
        for k in range(FF // LANES):
            i, j = divmod(k, D // LANES)
            up = jnp.where(me // per == k, total[8 + i : 9 + i, j * LANES : (j + 1) * LANES], up)
        up = jnp.broadcast_to(up, (8, LANES))
        up = pltpu.roll(up, lax.rem(LANES - lax.rem(me, per) * s.rf, LANES), 1)
        row = iota((8, LANES), 0)
        r.hv[...] = jnp.where(row < 5, mine, jnp.where(row == 5, loss, up))
        outs.append(local([(r.hv, r.ov)]))
    else:
        r.ov[...] = r.vg[...]
        for src, dst in ((r.gq, r.fgq), (r.go, r.fgo), (r.gu, r.fgu), (r.gd, r.fgd)):
            outs.append(local([(src, dst)]))
    for copy in outs:
        copy.wait()
    for slot in pending:
        left(slot)


def finish(n_mats, *refs):
    ov = refs[0]
    srcs = refs[1 : 1 + n_mats]
    dsts = refs[1 + n_mats : 1 + 2 * n_mats]
    vectors = refs[1 + 2 * n_mats : -1 - n_mats]
    held = refs[-1 - n_mats : -1]
    sems = refs[-1]
    reads = [pltpu.make_async_copy(a, b, sems.at[0, i]) for i, (a, b) in enumerate(zip(srcs, held))]
    writes = [pltpu.make_async_copy(a, b, sems.at[1, i]) for i, (a, b) in enumerate(zip(held, dsts))]
    for copy in reads:
        copy.start()
    for i, out in enumerate(vectors):
        out[...] = ov[pl.ds(i, 1), pl.ds(0, out.shape[1])]
    for read, write in zip(reads, writes):
        read.wait()
        write.start()
    for copy in writes:
        copy.wait()


def layer(
    mesh,
    prompt_x,
    cont_x,
    prompt_dy,
    cont_dy,
    teacher,
    cont_lengths,
    loss_scale,
    norm1_gain,
    norm1_bias,
    w_query,
    w_key,
    w_value,
    w_out,
    norm2_gain,
    norm2_bias,
    w_up,
    up_bias,
    w_down,
    down_bias,
):
    nz, ndp = mesh.shape["cont"], mesh.shape["dp"]
    ndev = nz * ndp
    exchange = ndp == 8 and nz == 4
    groups, prompt = prompt_x.shape[:2]
    conts = cont_x.shape[1]
    s = Sizes(groups, prompt, conts, nz, exchange, ndev)
    both = ("dp", "cont")
    any_spec = pl.BlockSpec(memory_space=pl.ANY)
    vmem = pl.BlockSpec(memory_space=pltpu.VMEM)

    inputs = {
        "px": (prompt_x, any_spec),
        "cx": (cont_x, any_spec),
        "pdy": (prompt_dy, any_spec),
        "cdy": (cont_dy, any_spec),
        "te": (teacher, any_spec),
        "lens_in": (cont_lengths.T, any_spec),
        "ls_in": (loss_scale.reshape(1, 1), any_spec),
    }
    weights = {"wq": w_query, "wk": w_key, "wv": w_value, "wo": w_out, "wup": w_up, "wdn": w_down}
    vectors = {"v1g": norm1_gain, "v1b": norm1_bias, "v2g": norm2_gain, "v2b": norm2_bias, "vdb": down_bias}
    if exchange:
        for name, w in weights.items():
            inputs[name] = (w, any_spec)
        for name, v in vectors.items():
            inputs[name] = (v.reshape(1, -1), any_spec)
        inputs["vub"] = (up_bias.reshape(1, -1), any_spec)
    else:
        for name, w in weights.items():
            inputs[name] = (lax.all_gather(w, both, axis=0, tiled=True), any_spec)
        tokens = lax.psum(jnp.sum(cont_lengths).astype(F32), both)
        full = [lax.all_gather(v, both, axis=0, tiled=True).astype(F32) for v in vectors.values()]
        zero = jnp.zeros((D,), F32)
        inputs["vecs"] = (jnp.stack(full + [zero, jnp.full((D,), tokens / (D // LANES)), zero]), vmem)
        up_full = lax.all_gather(up_bias, both, axis=0, tiled=True).astype(F32)
        inputs["upbs"] = (up_full.reshape(1, FF), vmem)

    m, mf = D // 8, FF // 8
    outputs = {
        "py": (prompt_x.shape, BF16, any_spec),
        "cy": (cont_x.shape, BF16, any_spec),
        "pdx": (prompt_x.shape, F32, any_spec),
        "cdx": (cont_x.shape, F32, any_spec),
    }
    if exchange:
        for name in ("ogq", "ogk", "ogv", "ogo"):
            outputs[name] = ((s.r, D), F32, any_spec)
        outputs["ogu"] = ((s.r, FF), F32, any_spec)
        outputs["ogd"] = ((s.rf, D), F32, any_spec)
        outputs["ov"] = ((8, LANES), F32, any_spec)
    else:
        outputs["fgq"] = ((PAIRS, 4, 2, m, 3 * LANES), BF16, any_spec)
        outputs["fgo"] = ((4, 2, m, D), BF16, any_spec)
        outputs["fgu"] = ((4, 2, m, FF), BF16, any_spec)
        outputs["fgd"] = ((4, 2, mf, D), BF16, any_spec)
        outputs["ov"] = ((16, D), F32, vmem)

    rows, blocks = s.rows, s.blocks
    dma = pltpu.SemaphoreType.DMA
    scratch = {
        "w4": ((4, D, D), BF16),
        "wu": ((D, FF), BF16),
        "wd": ((FF, D), BF16),
        "vec": ((8, D), F32),
        "upb": ((1, FF), F32),
        "x": ((rows, D), BF16),
        "dy": ((rows, D), BF16),
        "teach": ((groups * conts, CONT_LEN, D), BF16),
        "y": ((rows, D), BF16),
        "n1": ((rows, D), BF16),
        "q": ((rows, D), BF16),
        "k": ((rows, D), BF16),
        "v": ((rows, D), BF16),
        "ql": ((blocks, 64, D), BF16),
        "kl": ((blocks, 64, D), BF16),
        "vl": ((blocks, 64, D), BF16),
        "fkv": ((2, groups, s.far, D), BF16),
        "poolk": ((64, CONT_LEN), BF16),
        "poolq": ((64, CONT_LEN), BF16),
        "pq3": ((2 * s.nl + s.tb * BLOCK, s.rows_g), BF16),
        "pk3": ((s.nl, s.rows_g), BF16),
        "bias0": ((2 * CONT_LEN, CONT_LEN), F32),
        "bias1": ((2 * s.nl, s.nl), F32),
        "biasf": ((2 * s.tb * BLOCK, s.far), F32),
        "e0": ((blocks * PAIRS, 2 * CONT_LEN, CONT_LEN), BF16),
        "e1": ((groups, PAIRS, 2 * s.nl, s.nl), BF16),
        "ef": ((groups, PAIRS, 2 * s.tb * BLOCK, s.far), BF16),
        "num": ((rows, D), F32),
        "att": ((rows, D), BF16),
        "den": ((rows, D), F32),
        "mix": ((rows, D), F32),
        "n2": ((rows, D), BF16),
        "h": ((rows, FF), BF16),
        "gy": ((rows, D), F32),
        "gyb": ((rows, D), BF16),
        "dnum": ((rows, D), BF16),
        "xo": ((rows, D), BF16),
        "dnl": ((2, blocks, 64, D), BF16),
        "xol": ((2, blocks, 64, D), BF16),
        "dql": ((blocks, BLOCK, D), BF16),
        "dqkv": ((PAIRS, rows, 3 * LANES), BF16),
        "df": ((groups, 2, s.far, D), F32),
        "dfs": ((groups, 2, s.far, D), BF16),
        "rf": ((nz - 1, groups, 2, s.far_own, D), BF16),
        "ft": ((groups, 2, s.far_own, D), F32),
        "vg": ((16, D), F32),
        "gq": ((PAIRS, 4, 2, m, 3 * LANES), BF16),
        "go": ((4, 2, m, D), BF16),
        "gu": ((4, 2, m, FF), BF16),
        "gd": ((4, 2, mf, D), BF16),
        "lens": pltpu.SMEM((conts, groups), jnp.int32),
        "ls": pltpu.SMEM((1, 1), F32),
        "lsem": dma((20,)),
        "ss": dma((SENDS,)),
        "fr": dma((2,)),
    }
    if exchange:
        scratch["tiles"] = ((ndev, 8, LANES), F32)
        scratch["build"] = ((8, LANES), F32)
        scratch["small"] = ((5, 1, s.r), BF16)
        scratch["smallup"] = ((1, s.rf), BF16)
        for name in ("q", "k", "v", "o"):
            scratch["hg" + name] = ((s.r, D), F32)
        scratch["hgu"] = ((s.r, FF), F32)
        scratch["hgd"] = ((s.rf, D), F32)
        scratch["hv"] = ((8, LANES), F32)
        for name, lead, rr, cc in (("q", (PAIRS,), m, 3 * LANES), ("o", (), m, D), ("u", (), m, FF), ("d", (), mf, D)):
            scratch["rc" + name] = (lead + (4, rr, cc), BF16)
            scratch["rd" + name] = (lead + (2, rr // 2, cc), BF16)
            scratch["rx" + name] = (lead + (2, rr, cc), BF16)
            scratch["rz" + name] = (lead + (nz - 1, rr // nz, cc), BF16)
        scratch["rv"] = ((3 + nz, 16, D), F32)
        scratch["vt"] = ((3, 16, D), F32)
        scratch["agr"] = dma((7, 6))
        scratch["agw"] = dma((4,))
        scratch["rsr"] = dma((3 + PAIRS, 5))
        scratch["vr"] = dma((4,))

    names = list(inputs) + list(outputs) + list(scratch)
    results = pl.pallas_call(
        functools.partial(kernel, s, names),
        out_shape=[jax.ShapeDtypeStruct(shape, dtype) for shape, dtype, _ in outputs.values()],
        in_specs=[spec for _, spec in inputs.values()],
        out_specs=[spec for _, _, spec in outputs.values()],
        scratch_shapes=[pltpu.VMEM(*v) if isinstance(v, tuple) else v for v in scratch.values()],
        compiler_params=pltpu.CompilerParams(
            collective_id=0, has_side_effects=True, vmem_limit_bytes=64 * 1024 * 1024 - 65536
        ),
        name="layer",
    )(*[a for a, _ in inputs.values()])
    o = types.SimpleNamespace(**dict(zip(outputs, results)))
    if exchange:
        bulk = ["py", "cy", "pdx", "cdx", "ogq", "ogk", "ogv", "ogo", "ogu", "ogd"]
        shapes = [jax.ShapeDtypeStruct(outputs[k][0], outputs[k][1]) for k in bulk]
        vectors = [jax.ShapeDtypeStruct((1, n), F32) for n in [s.r] * 5 + [1, s.rf]]
        done = pl.pallas_call(
            functools.partial(finish, len(bulk)),
            out_shape=shapes + vectors,
            in_specs=[vmem] + [any_spec] * len(bulk),
            out_specs=[any_spec] * len(bulk) + [vmem] * len(vectors),
            scratch_shapes=[pltpu.VMEM(v.shape, v.dtype) for v in shapes] + [dma((2, len(bulk)))],
            name="finish",
        )(o.ov, *[getattr(o, k) for k in bulk])
        for k, v in zip(bulk, done):
            setattr(o, k, v)
        *vec, loss, up_vec = [v.reshape(-1) for v in done[len(bulk) :]]
        loss = loss.reshape(())
        mats = [o.ogq, o.ogk, o.ogv, o.ogo, o.ogu, o.ogd]
    else:
        three = o.fgq.reshape(PAIRS, D, 3, LANES).transpose(2, 1, 0, 3).reshape(3, D, D)
        whole = [three[0], three[1], three[2], o.fgo, o.fgu, o.fgd]
        whole = [w.reshape(-1, w.shape[-1]).astype(F32) for w in whole]
        parts = [o.ov[i] for i in range(5)] + [o.ov[8:12].reshape(FF)]
        *mats, v0, v1, v2, v3, v4, up_vec = [
            lax.psum_scatter(w, both, scatter_dimension=0, tiled=True) for w in whole + parts
        ]
        vec = [v0, v1, v2, v3, v4]
        loss = lax.psum(jnp.sum(o.ov[5]), both) / (tokens * D)
    return (
        o.py,
        o.cy,
        loss,
        o.pdx,
        o.cdx,
        vec[0],
        vec[1],
        mats[0],
        mats[1],
        mats[2],
        mats[3],
        vec[2],
        vec[3],
        mats[4],
        up_vec,
        mats[5],
        vec[4],
    )


def solution(mesh):
    rows = P("dp", "cont", None)
    conts = P("dp", "cont", None, None)
    vector = P(("dp", "cont"))
    matrix = P(("dp", "cont"), None)
    return jax.shard_map(
        functools.partial(layer, mesh),
        mesh=mesh,
        in_specs=(rows, conts, rows, conts, conts, P("dp", "cont"), P())
        + (vector, vector, matrix, matrix, matrix, matrix, vector, vector, matrix, vector, matrix, vector),
        out_specs=(rows, conts, P(), rows, conts)
        + (vector, vector, matrix, matrix, matrix, matrix, vector, vector, matrix, vector, matrix, vector),
        check_vma=False,
    )
```

```python
import functools
import types

import jax
import jax.numpy as jnp
from jax import lax
from jax.experimental import pallas as pl
from jax.experimental.pallas import tpu as pltpu
from jax.sharding import PartitionSpec as P

D = 512
HEADS = 8
HEAD_DIM = 64
FF = 2048
BLOCK = 16
CONT_LEN = 128
COARSE = CONT_LEN // BLOCK
PAIRS = HEADS // 2
EPS = 1e-5
SCORE = HEAD_DIM**-0.5
LOG2E = 1.4426950408889634
AWAY = -1e30
F32 = jnp.float32
BF16 = jnp.bfloat16
MESH = pl.DeviceIdType.MESH
LANES = 128
SENDS = 24
EARLY = 2


def nn(a, b):
    return jnp.dot(a, b, preferred_element_type=F32)


def nt(a, b):
    return lax.dot_general(a, b, (((1,), (1,)), ((), ())), preferred_element_type=F32)


def tn(a, b):
    return lax.dot_general(a, b, (((0,), (0,)), ((), ())), preferred_element_type=F32)


def iota(shape, dim):
    return lax.broadcasted_iota(jnp.int32, shape, dim)


def norm_stats(x):
    center = x - jnp.mean(x, -1, keepdims=True)
    rstd = lax.rsqrt(jnp.mean(center * center, -1, keepdims=True) + EPS)
    return center * rstd, rstd


def norm_back(xhat, rstd, gain, dn):
    dxhat = dn * gain
    mean_one = jnp.mean(dxhat, -1, keepdims=True)
    mean_two = jnp.mean(dxhat * xhat, -1, keepdims=True)
    return rstd * (dxhat - mean_one - xhat * mean_two)


def colsum(x):
    return jnp.sum(x, 0, keepdims=True)


class Sizes:
    def __init__(self, groups, prompt, conts, nz, exchange, ndev):
        self.groups = groups
        self.prompt = prompt
        self.conts = conts
        self.nz = nz
        self.exchange = exchange
        self.ndev = ndev
        self.nb = prompt // CONT_LEN
        self.tb = self.nb + conts
        self.rows_g = self.tb * CONT_LEN
        self.rows = groups * self.rows_g
        self.nl = 48 * self.tb
        self.blocks = groups * self.tb
        self.far_own = prompt // COARSE
        self.far = self.far_own * nz
        self.r = D // ndev
        self.rf = FF // ndev


def kernel(s, names, *refs):
    r = types.SimpleNamespace(**dict(zip(names, refs)))
    z = lax.axis_index("cont")
    dp = lax.axis_index("dp")
    zs = [lax.rem(z + d, s.nz) for d in range(1, s.nz)]
    pending = {}
    sent = [0]

    def remote(src, dst, ssem, rsem, dev):
        return pltpu.make_async_remote_copy(
            src_ref=src, dst_ref=dst, send_sem=ssem, recv_sem=rsem, device_id=dev, device_id_type=MESH
        )

    def send(src, dst, rsem, dev, cond=None):
        slot = sent[0] % SENDS
        sent[0] += 1
        if slot in pending:
            left(slot)
        copy = remote(src, dst, r.ss.at[slot], rsem, dev)
        on(cond, copy.start)
        pending[slot] = (cond, copy)

    def on(cond, act):
        if cond is None:
            act()
        else:
            pl.when(cond)(act)

    def left(slot):
        cond, copy = pending[slot]
        on(cond, copy.wait_send)

    def line_send(src, dst, rsem):
        for d, zz in enumerate(zs):
            cond = None
            if s.exchange and d != 1:
                cond = z != (s.nz - 1 if d == 0 else 0)
            send(src, dst, rsem, (dp, zz), cond)

    middle = (z == 1) | (z == 2)
    far_end = jnp.clip(3 * (z - 1), 0, s.nz - 1)

    def line_relay(piece, rsem):
        if s.exchange:
            ref = piece(3 - far_end)
            send(ref, ref, rsem, (dp, far_end), middle)

    def wait_recv(ref, rsem):
        pltpu.make_async_copy(ref, ref, rsem).wait()

    local_count = [0]
    outs = []

    def local(pairs, whole=None):
        sem = r.lsem.at[local_count[0]]
        local_count[0] += 1
        copies = [pltpu.make_async_copy(src, dst, sem) for src, dst in pairs]
        for copy in copies:
            copy.start()
        return copies[0] if whole is None else pltpu.make_async_copy(whole, whole, sem)

    def row_pairs(prompt, cont, rows):
        out = []
        for g in range(s.groups):
            base = g * s.rows_g
            out.append((prompt.at[g], rows.at[pl.ds(base, s.prompt)]))
            for c in range(s.conts):
                out.append((cont.at[g, c], rows.at[pl.ds(base + s.prompt + c * CONT_LEN, CONT_LEN)]))
        return out

    if s.exchange:
        core = lax.rem(dp, 2)
        ix = lax.rem(dp // 2, 2)
        iy = dp // 4
        sib = dp + 1 - 2 * core
        xn = dp + 2 - 4 * ix
        yn = dp + 4 - 8 * iy
        cell = dp // 2
        cell_x = cell + 1 - 2 * ix
        cell_y = cell + 2 - 4 * iy
        cell_d = cell_x + cell_y - cell
        sibcore = 1 - core
        me = dp * s.nz + z

        def view(k, a, n, part=None):
            if k == 0:
                return r.tiles.at[pl.ds(a, n)]
            ref, rows = (r.w4, s.r) if k < 5 else (r.wu, s.r) if k == 5 else (r.wd, s.rf)
            place = pl.ds(pl.multiple_of(a * rows, rows), n * rows)
            width = ref.shape[-1]
            cols = pl.ds(0, width) if part is None else pl.ds(part * (width // 2), width // 2)
            if k < 5:
                return ref.at[(1, 2, 0, 3)[k - 1], place, cols]
            return ref.at[place, cols]

        def shard(c, co, zz):
            return (c * 2 + co) * s.nz + zz

        def ag_sem(k, kind, wave):
            return r.agw.at[kind - 1] if wave and 0 < kind < 5 else r.agr.at[k, kind]

        def ag_move(k, kind, a, n, dev, part=None, wave=0):
            v = view(k, a, n, part)
            send(v, v, ag_sem(k, kind, wave), dev)

        def ag_got(k, kind, n, part=None, wave=0):
            wait_recv(view(k, 0, n, part), ag_sem(k, kind, wave))

        def ag_z(k):
            own = view(k, me, 1)
            line_send(own, own, ag_sem(k, 0, 0))

        def ag_out(k, wave, starts, n):
            if wave == 1 or n > 1:
                ag_got(k, 0, s.nz - 1)
                line_relay(lambda zz: view(k, dp * s.nz + zz, 1), ag_sem(k, 0, 0))
            for zz in starts:
                a = shard(cell, core, zz)
                ag_move(k, 1, a, n, (xn, z), None, wave)
                ag_move(k, 2, a, n, (yn, z), None, wave)
            for zz in starts:
                ag_move(k, 5, shard(cell, core, zz), n, (sib, z))

        def ag_pass(k, wave, starts, n):
            total = len(starts) * n
            ag_got(k, 1, total, None, wave)
            for zz in starts:
                ag_move(k, 3, shard(cell_x, core, zz), n, (yn, z), 0, wave)
            ag_got(k, 2, total, None, wave)
            if k > 0:
                for zz in starts:
                    ag_move(k, 4, shard(cell_y, core, zz), n, (xn, z), 1, wave)
            for zz in starts:
                ag_move(k, 5, shard(cell_x, core, zz), n, (sib, z))
                ag_move(k, 5, shard(cell_y, core, zz), n, (sib, z))

        def ag_last(k, wave, starts, n):
            total = len(starts) * n
            ag_got(k, 3, total, 0, wave)
            if k > 0:
                ag_got(k, 4, total, 1, wave)
            for zz in starts:
                ag_move(k, 5, shard(cell_d, core, zz), n, (sib, z))

        def ag1(k):
            ag_out(k, 0, [0], s.nz)

        def ag2(k):
            ag_pass(k, 0, [0], s.nz)

        def ag3(k):
            ag_last(k, 0, [0], s.nz)

        def ag4(k):
            ag_got(k, 5, 4 * s.nz)

        grads = [(r.gd.at[...], r.rcd, r.rdd, r.rxd, r.rzd), (r.gu.at[...], r.rcu, r.rdu, r.rxu, r.rzu),
                 (r.go.at[...], r.rco, r.rdo, r.rxo, r.rzo)]
        for p in range(PAIRS):
            grads.append((r.gq.at[p], r.rcq.at[p], r.rdq.at[p], r.rxq.at[p], r.rzq.at[p]))

        def rs0(k):
            g, rc, _, _, _ = grads[k]
            send(g.at[:, sibcore], rc, r.rsr.at[k, 0], (sib, z))

        def add_to(g, c, lo, n, term):
            place = (c, core, pl.ds(lo, n))
            g[place] = (g[place].astype(F32) + term.astype(F32)).astype(BF16) if term.dtype == F32 else g[place] + term

        def rs1(k):
            g, rc, rd, _, _ = grads[k]
            m = g.shape[2]
            wait_recv(rc, r.rsr.at[k, 0])
            add_to(g, cell_d, 0, m, rc[cell_d])
            mh = m // 2
            send(g.at[cell_d, core, pl.ds(0, mh)], rd.at[0], r.rsr.at[k, 1], (yn, z))
            send(g.at[cell_d, core, pl.ds(mh, mh)], rd.at[1], r.rsr.at[k, 2], (xn, z))
            for c in (cell_x, cell_y, cell):
                add_to(g, c, 0, m, rc[c])

        def rs2(k):
            g, _, rd, rx, _ = grads[k]
            mh = g.shape[2] // 2
            wait_recv(rd.at[0], r.rsr.at[k, 1])
            add_to(g, cell_x, 0, mh, rd[0])
            send(g.at[cell_x, core], rx.at[0], r.rsr.at[k, 3], (xn, z))
            wait_recv(rd.at[1], r.rsr.at[k, 2])
            add_to(g, cell_y, mh, mh, rd[1])
            send(g.at[cell_y, core], rx.at[1], r.rsr.at[k, 3], (yn, z))

        def piece(g, zz):
            n = g.shape[2] // s.nz
            return pl.ds(pl.multiple_of(zz * n, n), n)

        def rs3(k):
            g, _, _, rx, rz = grads[k]
            wait_recv(rx, r.rsr.at[k, 3])
            add_to(g, cell, 0, g.shape[2], rx[0].astype(F32) + rx[1].astype(F32))
            for d, zz in enumerate(zs):
                send(g.at[cell, core, piece(g, zz)], rz.at[d], r.rsr.at[k, 4], (dp, zz))

        def rs4(k):
            g, _, _, _, rz = grads[k]
            wait_recv(rz, r.rsr.at[k, 4])
            total = g[cell, core, piece(g, z)].astype(F32)
            for d in range(s.nz - 1):
                total = total + rz[d].astype(F32)
            if k < 3:
                held, out = ((r.hgd, r.ogd), (r.hgu, r.ogu), (r.hgo, r.ogo))[k]
                held[...] = total
                outs.append(local([(held, out)]))
            else:
                lanes = pl.ds((k - 3) * LANES, LANES)
                for j, (held, out) in enumerate(((r.hgq, r.ogq), (r.hgk, r.ogk), (r.hgv, r.ogv))):
                    held[:, lanes] = total[:, j * LANES : (j + 1) * LANES]
                    if k == 2 + PAIRS:
                        outs.append(local([(held, out)]))
    else:

        def nothing(*_):
            return None

        ag1 = ag2 = ag3 = ag4 = ag_z = ag_out = ag_pass = ag_last = nothing
        rs0 = rs1 = rs2 = rs3 = rs4 = nothing

    scalars_in = [local([(r.lens_in, r.lens)]), local([(r.ls_in, r.ls)])]
    if s.exchange:
        vectors_in = (r.v1g, r.v1b, r.v2g, r.v2b, r.vdb)
        scalars_in.append(local([(v, r.small.at[i]) for i, v in enumerate(vectors_in)], r.small))
        scalars_in.append(local([(r.vub, r.smallup)]))
        own_rows = pl.ds(pl.multiple_of(me * s.r, s.r), s.r)
        weights_in = [
            local([(w, r.w4.at[j, own_rows]) for j, w in enumerate((r.wq, r.wk, r.wv, r.wo))], r.w4.at[:, own_rows]),
            local([(r.wup, view(5, me, 1))]),
            local([(r.wdn, view(6, me, 1))]),
        ]
    else:
        weights_in = [local([(w, r.w4.at[j]) for j, w in enumerate((r.wq, r.wk, r.wv, r.wo))], r.w4)]
        weights_in += [local([(r.wup, r.wu)]), local([(r.wdn, r.wd)])]
    barrier = pltpu.get_barrier_semaphore()
    partners = [(dp, zz) for zz in zs]
    if s.exchange:
        partners += [(sib, z), (xn, z), (yn, z)]
    for dev in partners:
        pl.semaphore_signal(barrier, inc=1, device_id=dev, device_id_type=MESH)
    x_in = [local(row_pairs(r.px, r.cx, r.x), r.x)]
    teach_pairs = [(r.te.at[g, c], r.teach.at[g * s.conts + c]) for g in range(s.groups) for c in range(s.conts)]
    later_in = [local(row_pairs(r.pdy, r.cdy, r.dy), r.dy), local(teach_pairs, r.teach)]

    for copy in scalars_in:
        copy.wait()
    if s.exchange:
        r.build[...] = jnp.zeros_like(r.build)
        for i in range(5):
            r.build[pl.ds(i, 1), pl.ds(0, s.r)] = r.small[i].astype(F32)
        r.build[pl.ds(5, 1), pl.ds(0, s.rf)] = r.smallup[...].astype(F32)
        own_tokens = 0
        for g in range(s.groups):
            for c in range(s.conts):
                own_tokens = own_tokens + r.lens[c, g]
        tile = r.build[...]
        row = iota((8, LANES), 0)
        placed = jnp.where(
            row < 5,
            pltpu.roll(tile, lax.rem(me, LANES // s.r) * s.r, 1),
            pltpu.roll(tile, lax.rem(me, LANES // s.rf) * s.rf, 1),
        )
        r.tiles[me] = jnp.where(row == 6, own_tokens.astype(F32), placed)

    for copy in weights_in:
        copy.wait()
    pl.semaphore_wait(barrier, len(partners))
    first, rest = [z], zs
    ag_z(0)
    ag_z(1)
    ag_out(1, 0, first, 1)
    ag_z(2)

    ri = iota((64, CONT_LEN), 0)
    ci = iota((64, CONT_LEN), 1)
    coarse_ci = jnp.where(ri < 32, ci >> 1, jnp.where(ri < 48, ci >> 2, ci >> 3))
    position = jnp.where(ri < 16, ri, jnp.where(ri < 32, ri + 16, jnp.where(ri < 48, ri - 32, ri - 48)))
    r.poolk[...] = jnp.where(coarse_ci == position, 1.0, 0.0).astype(BF16)
    position = jnp.where(ri < 48, position + 16, position)
    r.poolq[...] = jnp.where(coarse_ci == position, 1.0, 0.0).astype(BF16)
    r.pq3[...] = jnp.zeros_like(r.pq3)
    r.pk3[...] = jnp.zeros_like(r.pk3)
    for b in range(s.tb):
        cols = pl.ds(b * CONT_LEN, CONT_LEN)
        for first_row in (0, s.nl):
            r.pq3[pl.ds(first_row + b * 48, 48), cols] = r.poolq[pl.ds(0, 48)]
        r.pq3[pl.ds(2 * s.nl + b * BLOCK, BLOCK), cols] = r.poolq[pl.ds(48, BLOCK)]
        r.pk3[pl.ds(b * 48, 48), cols] = r.poolk[pl.ds(0, 48)]
    ri = iota((CONT_LEN, CONT_LEN), 0)
    ci = iota((CONT_LEN, CONT_LEN), 1)
    bi, bj = ri >> 4, ci >> 4
    near = ((bi == bj) & (ci <= ri)) | (((bi & 1) == 1) & (bj == bi - 1))
    near = jnp.where(near, 0.0, AWAY)
    r.bias0[pl.ds(0, CONT_LEN)] = near
    r.bias0[pl.ds(CONT_LEN, CONT_LEN)] = near
    ri = iota((2 * s.nl, s.nl), 0)
    ri = jnp.where(ri >= s.nl, ri - s.nl, ri)
    r.bias1[...] = jnp.where((ri >> 4) == (iota((2 * s.nl, s.nl), 1) >> 4), 0.0, AWAY)
    nq = s.tb * BLOCK
    blk = lax.rem(iota((2 * nq, s.far), 0), nq) >> 4
    limit = jnp.where(blk >= s.nb, s.far, BLOCK * (z * s.nb + blk))
    r.biasf[...] = jnp.where(iota((2 * nq, s.far), 1) < limit, 0.0, AWAY)
    scale_rows = iota((64, D), 0)
    mean_scale = jnp.where(scale_rows < 32, 0.5, jnp.where(scale_rows < 48, 0.25, 0.125))
    r.vg[...] = jnp.zeros_like(r.vg)

    ag_pass(1, 0, first, 1)
    ag1(0)
    ag_out(1, 1, rest, 1)
    ag_z(3)
    ag_last(1, 0, first, 1)
    ag1(2)
    ag_z(4)
    ag_z(5)
    ag2(0)
    ag_pass(1, 1, rest, 1)
    ag1(3)
    ag3(0)
    ag_z(6)
    ag_last(1, 1, rest, 1)
    ag2(2)
    ag4(0)
    if s.exchange:
        count = 8
        for k in range(s.ndev // count):
            part = jnp.sum(r.tiles[pl.ds(k * count, count)], 0)
            r.vec[:, pl.ds(k * LANES, LANES)] = part
        for k in range(s.ndev // 2):
            part = r.tiles[2 * k] + r.tiles[2 * k + 1]
            r.upb[:, pl.ds(k * LANES, LANES)] = part[5:6]
    else:
        r.vec[...] = r.vecs[...]
        r.upb[...] = r.upbs[...]

    def vec(i):
        return r.vec[pl.ds(i, 1), :]

    token_row = r.vec[pl.ds(6, 1), pl.ds(0, LANES)]
    for k in range(1, D // LANES):
        token_row = token_row + r.vec[pl.ds(6, 1), pl.ds(k * LANES, LANES)]
    token_row = jnp.concatenate([token_row] * (D // LANES), 1)

    def length_of(g, b):
        if isinstance(b, int):
            return CONT_LEN if b < s.nb else r.lens[b - s.nb, g]
        c = jnp.clip(b - s.nb, 0, s.conts - 1)
        return jnp.where(b >= s.nb, r.lens[c, g], CONT_LEN)

    def block_rows(t):
        if isinstance(t, int):
            return pl.ds(t * CONT_LEN, CONT_LEN)
        return pl.ds(pl.multiple_of(t * CONT_LEN, CONT_LEN), CONT_LEN)

    for copy in x_in:
        copy.wait()

    def norm_one(i, carry):
        rows = block_rows(i)
        xhat, _ = norm_stats(r.x[rows].astype(F32))
        r.n1[rows] = (xhat * vec(0) + vec(1)).astype(BF16)
        return carry

    lax.fori_loop(0, s.blocks, norm_one, 0)
    ag2(3)
    ag4(1)

    def project(j, out, pools):
        for g in range(s.groups):
            rows = pl.ds(g * s.rows_g, s.rows_g)
            value = nn(r.n1[rows], r.w4[j])
            parts = [value[: s.prompt]]
            for c in range(s.conts):
                lo = s.prompt + c * CONT_LEN
                part = value[lo : lo + CONT_LEN]
                if j > 0:
                    part = jnp.where(iota((CONT_LEN, D), 0) < r.lens[c, g], part, 0.0)
                parts.append(part)
            value = jnp.concatenate(parts, 0).astype(BF16)
            out[rows] = value
            pool, pooled, scale = pools
            for b in range(s.tb):
                pooled[g * s.tb + b] = (nn(pool[...], value[b * CONT_LEN : (b + 1) * CONT_LEN]) * scale).astype(BF16)

    project(1, r.k, (r.poolk, r.kl, mean_scale))
    ag3(2)
    ag1(4)
    ag1(5)
    ag4(2)
    project(2, r.v, (r.poolk, r.vl, 1.0))
    for g in range(s.groups):
        for b in range(s.nb):
            place = pl.ds(pl.multiple_of(z * s.far_own + b * BLOCK, BLOCK), BLOCK)
            r.fkv[0, g, place] = r.kl[g * s.tb + b, pl.ds(48, BLOCK)]
            r.fkv[1, g, place] = r.vl[g * s.tb + b, pl.ds(48, BLOCK)]

    def far_rows(zz):
        return r.fkv.at[:, :, pl.ds(pl.multiple_of(zz * s.far_own, s.far_own), s.far_own)]

    line_send(far_rows(z), far_rows(z), r.fr.at[0])

    def far_got():
        wait_recv(r.fkv.at[:, :, pl.ds(0, s.far - s.far_own)], r.fr.at[0])

    ag3(3)
    ag2(4)
    ag1(6)
    ag4(3)
    project(0, r.q, (r.poolq, r.ql, mean_scale))

    def two(a):
        low = iota(a.shape, 1) < HEAD_DIM
        zero = jnp.zeros_like(a)
        return jnp.concatenate([jnp.where(low, a, zero), jnp.where(low, zero, a)], 0)

    def pick(a):
        n = a.shape[0] // 2
        return jnp.where(iota((n, LANES), 1) < HEAD_DIM, a[:n], a[n:])

    def counts(length):
        i0 = iota((CONT_LEN, LANES), 0)
        counts0 = jnp.where(i0 < length, 1.0, 0.0).astype(BF16)
        i1 = iota((48, LANES), 0)
        first = jnp.where(i1 < 16, 2 * i1, jnp.where(i1 < 32, 2 * (i1 + 16), 4 * (i1 - 32)))
        width = jnp.where(i1 < 32, 2, 4)
        counts1 = jnp.clip(length - first, 0, width).astype(F32).astype(BF16)
        return counts0, counts1

    def pair_lanes(p):
        return pl.ds(p * LANES, LANES)

    low48 = pl.ds(0, 48)
    far16 = pl.ds(48, BLOCK)

    def near(t, carry):
        g, b = t // s.tb, lax.rem(t, s.tb)
        rows = block_rows(t)
        counts0, _ = counts(length_of(g, b))
        for p in range(PAIRS):
            lanes = pair_lanes(p)
            e0 = jnp.exp2(nt(two(r.q[rows, lanes]), r.k[rows, lanes]) * (SCORE * LOG2E) + r.bias0[...])
            e0 = e0.astype(BF16)
            r.e0[t * PAIRS + p] = e0
            t0 = nn(e0, jnp.concatenate([r.v[rows, lanes], counts0], 1))
            r.num[rows, lanes] = pick(t0[:, :LANES])
            r.den[rows, lanes] = pick(t0[:, LANES:])
        return carry

    eight = jnp.full((s.far, LANES), float(COARSE), BF16)

    def gathered(ref, g, lanes, part=None):
        part = far16 if part is None else part
        return jnp.concatenate([ref[g * s.tb + b, part, lanes] for b in range(s.tb)], 0)

    def coarse_values(g, lanes):
        widths = jnp.concatenate([counts(length_of(g, b))[1] for b in range(s.tb)], 0)
        return jnp.concatenate([gathered(r.vl, g, lanes, low48), widths], 1)

    def group_rows(g):
        if isinstance(g, int):
            return pl.ds(g * s.rows_g, s.rows_g)
        return pl.ds(pl.multiple_of(g * s.rows_g, CONT_LEN), s.rows_g)

    def coarse_forward(g):
        rows = group_rows(g)
        for p in range(PAIRS):
            lanes = pair_lanes(p)
            e1 = nt(two(gathered(r.ql, g, lanes, low48)), gathered(r.kl, g, lanes, low48))
            e1 = jnp.exp2(e1 * (SCORE * LOG2E) + r.bias1[...]).astype(BF16)
            r.e1[g, p] = e1
            t1 = nn(e1, coarse_values(g, lanes))
            t1 = jnp.concatenate([pick(t1[:, :LANES]), pick(t1[:, LANES:])], 1)
            high = t1.astype(BF16)
            both = jnp.concatenate([high, (t1 - high.astype(F32)).astype(BF16)], 0)
            t1 = tn(r.pq3[pl.ds(0, 2 * s.nl)], both)
            r.num[rows, lanes] += t1[:, :LANES]
            r.den[rows, lanes] += t1[:, LANES:]

    def repeat_rows(a):
        n = a.shape[0]
        return jnp.broadcast_to(a[:, None, :], (n, COARSE, LANES)).reshape(n * COARSE, LANES)

    def far_forward(g):
        rows = pl.ds(g * s.rows_g, s.rows_g)
        for p in range(PAIRS):
            lanes = pair_lanes(p)
            ef = nt(two(gathered(r.ql, g, lanes)), r.fkv[0, g, :, lanes]) * (SCORE * LOG2E) + r.biasf[...]
            ef = jnp.exp2(ef).astype(BF16)
            r.ef[g, p] = ef
            total = nn(ef, jnp.concatenate([r.fkv[1, g, :, lanes], eight], 1))
            denominator = r.den[rows, lanes] + repeat_rows(pick(total[:, LANES:]))
            numerator = r.num[rows, lanes] + repeat_rows(pick(total[:, :LANES]))
            r.den[rows, lanes] = denominator
            r.att[rows, lanes] = (numerator / denominator).astype(BF16)

    lax.fori_loop(0, s.tb, near, 0)
    ag2(5)
    ag3(4)
    ag2(6)
    if s.exchange:
        on(middle, far_got)
    line_relay(far_rows, r.fr.at[0])
    coarse_forward(0)
    lax.fori_loop(s.tb, s.blocks, near, 0)
    for g in range(1, s.groups):
        coarse_forward(g)
    ag3(5)
    on(jnp.logical_not(middle) if s.exchange else None, far_got)
    for g in range(s.groups):
        far_forward(g)
    ag4(4)
    ag3(6)

    for copy in later_in:
        copy.wait()
    for g in range(s.groups):
        rows = pl.ds(g * s.rows_g, s.rows_g)
        mixed = r.x[rows].astype(F32) + nn(r.att[rows], r.w4[3])
        r.mix[rows] = mixed
        xhat, _ = norm_stats(mixed)
        r.n2[rows] = (xhat * vec(2) + vec(3)).astype(BF16)
    ag4(5)
    for g in range(s.groups):
        rows = pl.ds(g * s.rows_g, s.rows_g)
        for n in range(FF // D):
            cols = pl.ds(n * D, D)
            pre = nn(r.n2[rows], r.wu[:, cols]) + r.upb[:, cols]
            r.h[rows, cols] = jnp.maximum(pre, 0.0).astype(BF16)
    ag4(6)
    extra = 2.0 * r.ls[0, 0] / (token_row * float(D))
    for g in range(s.groups):
        base = g * s.rows_g
        rows = pl.ds(base, s.rows_g)
        y = r.mix[rows] + nn(r.h[rows], r.wd[...]) + vec(4)
        r.y[rows] = y.astype(BF16)
        gy = r.dy[rows].astype(F32)
        parts = [gy[: s.prompt]]
        for c in range(s.conts):
            lo = s.prompt + c * CONT_LEN
            keep = iota((CONT_LEN, D), 0) < r.lens[c, g]
            diff = jnp.where(keep, y[lo : lo + CONT_LEN] - r.teach[g * s.conts + c].astype(F32), 0.0)
            r.vg[pl.ds(5, 1), :] += colsum(diff * diff)
            parts.append(gy[lo : lo + CONT_LEN] + extra * diff)
        gy = jnp.concatenate(parts, 0)
        r.gy[rows] = gy
        r.gyb[rows] = gy.astype(BF16)
        r.vg[pl.ds(4, 1), :] += colsum(gy)

    outs.append(local([(b, a) for a, b in row_pairs(r.py, r.cy, r.y)], r.y))

    for n in range(FF // D):
        cols = pl.ds(n * D, D)
        r.gd[n] = tn(r.h[:, cols], r.gyb[...]).astype(BF16).reshape(2, FF // 8, D)
    rs0(0)
    for n in range(FF // D):
        cols = pl.ds(n * D, D)
        for g in range(s.groups):
            rows = pl.ds(g * s.rows_g, s.rows_g)
            dh = nt(r.gyb[rows], r.wd[cols])
            dpre = jnp.where(r.h[rows, cols] > 0, dh, 0.0).astype(BF16)
            r.h[rows, cols] = dpre
            r.vg[pl.ds(8 + n, 1), :] += colsum(dpre.astype(F32))
    rs1(0)
    for g in range(s.groups):
        rows = pl.ds(g * s.rows_g, s.rows_g)
        dn2 = nt(r.h[rows], r.wu[...])
        xhat, rstd = norm_stats(r.mix[rows])
        r.vg[pl.ds(2, 1), :] += colsum(dn2 * xhat)
        r.vg[pl.ds(3, 1), :] += colsum(dn2)
        dmixed = r.gy[rows] + norm_back(xhat, rstd, vec(2), dn2)
        r.gy[rows] = dmixed
        r.gyb[rows] = dmixed.astype(BF16)
    for g in range(s.groups):
        rows = pl.ds(g * s.rows_g, s.rows_g)
        dnum = nt(r.gyb[rows], r.w4[3]) / r.den[rows]
        r.dnum[rows] = dnum.astype(BF16)
        r.xo[rows] = (-dnum * r.att[rows].astype(F32)).astype(BF16)
        for b in range(s.tb):
            t = g * s.tb + b
            for ref, fine in ((r.dnl, r.dnum), (r.xol, r.xo)):
                pooled = nn(r.poolq[...], fine[block_rows(t)])
                high = pooled.astype(BF16)
                ref[0, t] = high
                ref[1, t] = (pooled - high.astype(F32)).astype(BF16)

    for g in range(s.groups):
        for p in range(PAIRS):
            lanes = pair_lanes(p)
            d3, x3, d3_low, x3_low = [two(gathered(ref.at[i], g, lanes)) for i in range(2) for ref in (r.dnl, r.xol)]
            x = jnp.concatenate([d3, x3, d3_low, x3_low], 1)
            vn = jnp.concatenate([r.fkv[1, g, :, lanes], eight], 1)
            ef = r.ef[g, p]
            kf = r.fkv[0, g, :, lanes]
            ds = nt(x, jnp.concatenate([vn, vn], 1)) * ef.astype(F32)
            ds = ds.astype(BF16)
            dq3 = (pick(nn(ds, kf)) * 0.125).astype(BF16)
            for b in range(s.tb):
                r.dql[g * s.tb + b, :, lanes] = dq3[b * BLOCK : (b + 1) * BLOCK]
            dkf = tn(ds, two(gathered(r.ql, g, lanes)))
            dvf = tn(ef, d3)
            r.df[g, 0, :, lanes] = dkf
            r.df[g, 1, :, lanes] = dvf
            r.dfs[g, 0, :, lanes] = dkf.astype(BF16)
            r.dfs[g, 1, :, lanes] = dvf.astype(BF16)

    def far_part(zz):
        return r.dfs.at[:, :, pl.ds(pl.multiple_of(zz * s.far_own, s.far_own), s.far_own)]

    for d, zz in enumerate(zs):
        send(far_part(zz), r.rf.at[d], r.fr.at[1], (dp, zz))
    rs2(0)
    for n in range(FF // D):
        cols = pl.ds(n * D, D)
        r.gu[:, :, :, cols] = tn(r.n2[...], r.h[:, cols]).astype(BF16).reshape(4, 2, D // 8, D)
    rs0(1)
    r.go[...] = tn(r.att[...], r.gyb[...]).astype(BF16).reshape(4, 2, D // 8, D)
    rs0(2)

    def pair_back(p, g):
        lanes = pair_lanes(p)
        e1 = r.e1[g, p]
        q1 = two(gathered(r.ql, g, lanes, low48))
        k1 = gathered(r.kl, g, lanes, low48)
        d1, x1, d1_low, x1_low = [
            two(gathered(ref.at[i], g, lanes, low48)) for i in range(2) for ref in (r.dnl, r.xol)
        ]
        vn1 = coarse_values(g, lanes)
        ds1 = nt(jnp.concatenate([d1, x1, d1_low, x1_low], 1), jnp.concatenate([vn1, vn1], 1))
        ds1 = (ds1 * e1.astype(F32)).astype(BF16)
        lr = lax.rem(iota((s.nl, LANES), 0), 48)
        level_scale = jnp.where(lr < 32, 0.5, 0.25)
        dql = (pick(nn(ds1, k1)) * level_scale).astype(BF16)
        dql = jnp.concatenate([dql] + [r.dql[g * s.tb + b, :, lanes] for b in range(s.tb)], 0)
        fine_q = tn(r.pq3[pl.ds(s.nl, s.nl + s.tb * BLOCK)], dql)
        dkl = (tn(ds1, q1) * level_scale).astype(BF16)
        dvl = tn(e1, d1).astype(BF16)
        fine = tn(r.pk3[...], jnp.concatenate([dkl, dvl], 1))
        for b in range(s.tb):
            t = g * s.tb + b
            rows = block_rows(t)
            length = length_of(g, b)
            counts0, _ = counts(length)
            q2 = two(r.q[rows, lanes])
            e0 = r.e0[t * PAIRS + p]
            dn2 = two(r.dnum[rows, lanes])
            x0 = jnp.concatenate([dn2, two(r.xo[rows, lanes])], 1)
            ds0 = nt(x0, jnp.concatenate([r.v[rows, lanes], counts0], 1)) * e0.astype(F32)
            ds0 = ds0.astype(BF16)
            part = slice(b * CONT_LEN, (b + 1) * CONT_LEN)
            dq = pick(nn(ds0, r.k[rows, lanes])) + fine_q[part]
            dkv = tn(jnp.concatenate([ds0, e0], 1), jnp.concatenate([q2, dn2], 1))
            dk = (dkv[:CONT_LEN, :LANES] + fine[part, :LANES]) * SCORE
            dv = dkv[CONT_LEN:, LANES:] + fine[part, LANES:]
            r.dqkv[p, rows, pl.ds(0, LANES)] = (dq * SCORE).astype(BF16)
            if b >= s.nb:
                keep = iota((CONT_LEN, LANES), 0) < length
                dk = jnp.where(keep, dk, 0.0)
                dv = jnp.where(keep, dv, 0.0)
            elif p < EARLY:
                r.num[rows, pl.ds(2 * p * LANES, LANES)] = dk
                r.num[rows, pl.ds((2 * p + 1) * LANES, LANES)] = dv
                continue
            else:
                far_k, far_v = far_terms(p, g, b)
                dk = dk + far_k
                dv = dv + far_v
            r.dqkv[p, rows, pl.ds(LANES, LANES)] = dk.astype(BF16)
            r.dqkv[p, rows, pl.ds(2 * LANES, LANES)] = dv.astype(BF16)

    def far_terms(p, g, b):
        own = pl.ds(b * BLOCK, BLOCK)
        lanes = pair_lanes(p)
        return repeat_rows(r.ft[g, 0, own, lanes]), repeat_rows(r.ft[g, 1, own, lanes])

    def each_group(p):
        def body(g, carry):
            pair_back(p, g)
            return carry

        lax.fori_loop(0, s.groups, body, 0)

    rs1(1)
    each_group(0)
    rs1(2)
    each_group(1)
    rs3(0)
    wait_recv(r.rf, r.fr.at[1])
    own = pl.ds(pl.multiple_of(z * s.far_own, s.far_own), s.far_own)
    for g in range(s.groups):
        for i, scale in enumerate((SCORE / COARSE, 1.0)):
            total = r.df[g, i, own]
            for d in range(s.nz - 1):
                total = total + r.rf[d, g, i].astype(F32)
            r.ft[g, i] = total.astype(BF16).astype(F32) * scale
    def add_far(p):
        for g in range(s.groups):
            for b in range(s.nb):
                rows = block_rows(g * s.tb + b)
                far_k, far_v = far_terms(p, g, b)
                dk = r.num[rows, pl.ds(2 * p * LANES, LANES)] + far_k
                dv = r.num[rows, pl.ds((2 * p + 1) * LANES, LANES)] + far_v
                r.dqkv[p, rows, pl.ds(LANES, LANES)] = dk.astype(BF16)
                r.dqkv[p, rows, pl.ds(2 * LANES, LANES)] = dv.astype(BF16)

    def prompts_back(p):
        if p < EARLY:
            add_far(p)
        else:
            each_group(p)
        r.gq[p] = tn(r.n1[...], r.dqkv[p]).astype(BF16).reshape(4, 2, D // 8, 3 * LANES)

    def dn1_part(p, g):
        rows = pl.ds(g * s.rows_g, s.rows_g)
        w = jnp.concatenate([r.w4[j, :, pair_lanes(p)] for j in range(3)], 1)
        return nt(r.dqkv[p, rows], w)

    def dn1_add(p):
        for g in range(s.groups):
            rows = pl.ds(g * s.rows_g, s.rows_g)
            part = dn1_part(p, g)
            r.num[rows] = part if p == 0 else r.num[rows] + part

    prompts_back(0)
    rs0(3)
    rs2(1)
    prompts_back(1)
    rs0(4)
    rs2(2)
    rs1(3)
    dn1_add(0)
    dn1_add(1)
    rs1(4)
    prompts_back(2)
    rs0(5)
    rs4(0)
    dn1_add(2)
    rs1(5)
    prompts_back(3)
    rs0(6)
    rs3(1)
    rs2(3)
    rs3(2)
    rs2(4)

    for g in range(s.groups):
        rows = pl.ds(g * s.rows_g, s.rows_g)
        dn1 = r.num[rows] + dn1_part(PAIRS - 1, g)
        xhat, rstd = norm_stats(r.x[rows].astype(F32))
        r.vg[pl.ds(0, 1), :] += colsum(dn1 * xhat)
        r.vg[pl.ds(1, 1), :] += colsum(dn1)
        r.gy[rows] = r.gy[rows] + norm_back(xhat, rstd, vec(0), dn1)
        if g == 0:
            rs1(6)
            rs2(5)
            rs3(3)

    outs.append(local([(b, a) for a, b in row_pairs(r.pdx, r.cdx, r.gy)], r.gy))
    if s.exchange:

        def vsend(src, i, dev):
            send(src, r.rv.at[i], r.vr.at[i], dev)

        vsend(r.vg, 0, (sib, z))
        rs3(4)
        rs2(6)
        wait_recv(r.rv.at[0], r.vr.at[0])
        r.vt[0] = r.vg[...] + r.rv[0]
        vsend(r.vt.at[0], 1, (xn, z))
        rs3(5)
        wait_recv(r.rv.at[1], r.vr.at[1])
        r.vt[1] = r.vt[0] + r.rv[1]
        vsend(r.vt.at[1], 2, (yn, z))
        rs3(6)
        rs4(1)
        wait_recv(r.rv.at[2], r.vr.at[2])
        r.vt[2] = r.vt[1] + r.rv[2]
        for zz in zs:
            send(r.vt.at[2], r.rv.at[3 + z], r.vr.at[3], (dp, zz))
        rs4(2)
        rs4(3)
        rs4(4)
        rs4(5)
        rs4(6)
        wait_recv(r.rv.at[pl.ds(3, s.nz - 1)], r.vr.at[3])
        r.rv[3 + z] = r.vt[2]
        total = r.rv[3]
        for i in range(1, s.nz):
            total = total + r.rv[3 + i]
        loss = jnp.sum(total[5:6], 1, keepdims=True) / (token_row[:, :1] * float(D))
        mine = jnp.zeros((8, LANES), F32)
        per = LANES // s.r
        for k in range(D // LANES):
            mine = jnp.where(me // per == k, total[:8, k * LANES : (k + 1) * LANES], mine)
        mine = pltpu.roll(mine, lax.rem(LANES - lax.rem(me, per) * s.r, LANES), 1)
        per = LANES // s.rf
        up = jnp.zeros((1, LANES), F32)
        for k in range(FF // LANES):
            i, j = divmod(k, D // LANES)
            up = jnp.where(me // per == k, total[8 + i : 9 + i, j * LANES : (j + 1) * LANES], up)
        up = jnp.broadcast_to(up, (8, LANES))
        up = pltpu.roll(up, lax.rem(LANES - lax.rem(me, per) * s.rf, LANES), 1)
        row = iota((8, LANES), 0)
        r.hv[...] = jnp.where(row < 5, mine, jnp.where(row == 5, loss, up))
        outs.append(local([(r.hv, r.ov)]))
    else:
        r.ov[...] = r.vg[...]
        for src, dst in ((r.gq, r.fgq), (r.go, r.fgo), (r.gu, r.fgu), (r.gd, r.fgd)):
            outs.append(local([(src, dst)]))
    for copy in outs:
        copy.wait()
    for slot in pending:
        left(slot)


def finish(n_mats, *refs):
    ov = refs[0]
    srcs = refs[1 : 1 + n_mats]
    dsts = refs[1 + n_mats : 1 + 2 * n_mats]
    vectors = refs[1 + 2 * n_mats : -1 - n_mats]
    held = refs[-1 - n_mats : -1]
    sems = refs[-1]
    reads = [pltpu.make_async_copy(a, b, sems.at[0, i]) for i, (a, b) in enumerate(zip(srcs, held))]
    writes = [pltpu.make_async_copy(a, b, sems.at[1, i]) for i, (a, b) in enumerate(zip(held, dsts))]
    for copy in reads:
        copy.start()
    for i, out in enumerate(vectors):
        out[...] = ov[pl.ds(i, 1), pl.ds(0, out.shape[1])]
    for read, write in zip(reads, writes):
        read.wait()
        write.start()
    for copy in writes:
        copy.wait()


def layer(
    mesh,
    prompt_x,
    cont_x,
    prompt_dy,
    cont_dy,
    teacher,
    cont_lengths,
    loss_scale,
    norm1_gain,
    norm1_bias,
    w_query,
    w_key,
    w_value,
    w_out,
    norm2_gain,
    norm2_bias,
    w_up,
    up_bias,
    w_down,
    down_bias,
):
    nz, ndp = mesh.shape["cont"], mesh.shape["dp"]
    ndev = nz * ndp
    exchange = ndp == 8 and nz == 4
    groups, prompt = prompt_x.shape[:2]
    conts = cont_x.shape[1]
    s = Sizes(groups, prompt, conts, nz, exchange, ndev)
    both = ("dp", "cont")
    any_spec = pl.BlockSpec(memory_space=pl.ANY)
    vmem = pl.BlockSpec(memory_space=pltpu.VMEM)

    inputs = {
        "px": (prompt_x, any_spec),
        "cx": (cont_x, any_spec),
        "pdy": (prompt_dy, any_spec),
        "cdy": (cont_dy, any_spec),
        "te": (teacher, any_spec),
        "lens_in": (cont_lengths.T, any_spec),
        "ls_in": (loss_scale.reshape(1, 1), any_spec),
    }
    weights = {"wq": w_query, "wk": w_key, "wv": w_value, "wo": w_out, "wup": w_up, "wdn": w_down}
    vectors = {"v1g": norm1_gain, "v1b": norm1_bias, "v2g": norm2_gain, "v2b": norm2_bias, "vdb": down_bias}
    if exchange:
        for name, w in weights.items():
            inputs[name] = (w, any_spec)
        for name, v in vectors.items():
            inputs[name] = (v.reshape(1, -1), any_spec)
        inputs["vub"] = (up_bias.reshape(1, -1), any_spec)
    else:
        for name, w in weights.items():
            inputs[name] = (lax.all_gather(w, both, axis=0, tiled=True), any_spec)
        tokens = lax.psum(jnp.sum(cont_lengths).astype(F32), both)
        full = [lax.all_gather(v, both, axis=0, tiled=True).astype(F32) for v in vectors.values()]
        zero = jnp.zeros((D,), F32)
        inputs["vecs"] = (jnp.stack(full + [zero, jnp.full((D,), tokens / (D // LANES)), zero]), vmem)
        up_full = lax.all_gather(up_bias, both, axis=0, tiled=True).astype(F32)
        inputs["upbs"] = (up_full.reshape(1, FF), vmem)

    m, mf = D // 8, FF // 8
    outputs = {
        "py": (prompt_x.shape, BF16, any_spec),
        "cy": (cont_x.shape, BF16, any_spec),
        "pdx": (prompt_x.shape, F32, any_spec),
        "cdx": (cont_x.shape, F32, any_spec),
    }
    if exchange:
        for name in ("ogq", "ogk", "ogv", "ogo"):
            outputs[name] = ((s.r, D), F32, any_spec)
        outputs["ogu"] = ((s.r, FF), F32, any_spec)
        outputs["ogd"] = ((s.rf, D), F32, any_spec)
        outputs["ov"] = ((8, LANES), F32, any_spec)
    else:
        outputs["fgq"] = ((PAIRS, 4, 2, m, 3 * LANES), BF16, any_spec)
        outputs["fgo"] = ((4, 2, m, D), BF16, any_spec)
        outputs["fgu"] = ((4, 2, m, FF), BF16, any_spec)
        outputs["fgd"] = ((4, 2, mf, D), BF16, any_spec)
        outputs["ov"] = ((16, D), F32, vmem)

    rows, blocks = s.rows, s.blocks
    dma = pltpu.SemaphoreType.DMA
    scratch = {
        "w4": ((4, D, D), BF16),
        "wu": ((D, FF), BF16),
        "wd": ((FF, D), BF16),
        "vec": ((8, D), F32),
        "upb": ((1, FF), F32),
        "x": ((rows, D), BF16),
        "dy": ((rows, D), BF16),
        "teach": ((groups * conts, CONT_LEN, D), BF16),
        "y": ((rows, D), BF16),
        "n1": ((rows, D), BF16),
        "q": ((rows, D), BF16),
        "k": ((rows, D), BF16),
        "v": ((rows, D), BF16),
        "ql": ((blocks, 64, D), BF16),
        "kl": ((blocks, 64, D), BF16),
        "vl": ((blocks, 64, D), BF16),
        "fkv": ((2, groups, s.far, D), BF16),
        "poolk": ((64, CONT_LEN), BF16),
        "poolq": ((64, CONT_LEN), BF16),
        "pq3": ((2 * s.nl + s.tb * BLOCK, s.rows_g), BF16),
        "pk3": ((s.nl, s.rows_g), BF16),
        "bias0": ((2 * CONT_LEN, CONT_LEN), F32),
        "bias1": ((2 * s.nl, s.nl), F32),
        "biasf": ((2 * s.tb * BLOCK, s.far), F32),
        "e0": ((blocks * PAIRS, 2 * CONT_LEN, CONT_LEN), BF16),
        "e1": ((groups, PAIRS, 2 * s.nl, s.nl), BF16),
        "ef": ((groups, PAIRS, 2 * s.tb * BLOCK, s.far), BF16),
        "num": ((rows, D), F32),
        "att": ((rows, D), BF16),
        "den": ((rows, D), F32),
        "mix": ((rows, D), F32),
        "n2": ((rows, D), BF16),
        "h": ((rows, FF), BF16),
        "gy": ((rows, D), F32),
        "gyb": ((rows, D), BF16),
        "dnum": ((rows, D), BF16),
        "xo": ((rows, D), BF16),
        "dnl": ((2, blocks, 64, D), BF16),
        "xol": ((2, blocks, 64, D), BF16),
        "dql": ((blocks, BLOCK, D), BF16),
        "dqkv": ((PAIRS, rows, 3 * LANES), BF16),
        "df": ((groups, 2, s.far, D), F32),
        "dfs": ((groups, 2, s.far, D), BF16),
        "rf": ((nz - 1, groups, 2, s.far_own, D), BF16),
        "ft": ((groups, 2, s.far_own, D), F32),
        "vg": ((16, D), F32),
        "gq": ((PAIRS, 4, 2, m, 3 * LANES), BF16),
        "go": ((4, 2, m, D), BF16),
        "gu": ((4, 2, m, FF), BF16),
        "gd": ((4, 2, mf, D), BF16),
        "lens": pltpu.SMEM((conts, groups), jnp.int32),
        "ls": pltpu.SMEM((1, 1), F32),
        "lsem": dma((20,)),
        "ss": dma((SENDS,)),
        "fr": dma((2,)),
    }
    if exchange:
        scratch["tiles"] = ((ndev, 8, LANES), F32)
        scratch["build"] = ((8, LANES), F32)
        scratch["small"] = ((5, 1, s.r), BF16)
        scratch["smallup"] = ((1, s.rf), BF16)
        for name in ("q", "k", "v", "o"):
            scratch["hg" + name] = ((s.r, D), F32)
        scratch["hgu"] = ((s.r, FF), F32)
        scratch["hgd"] = ((s.rf, D), F32)
        scratch["hv"] = ((8, LANES), F32)
        for name, lead, rr, cc in (("q", (PAIRS,), m, 3 * LANES), ("o", (), m, D), ("u", (), m, FF), ("d", (), mf, D)):
            scratch["rc" + name] = (lead + (4, rr, cc), BF16)
            scratch["rd" + name] = (lead + (2, rr // 2, cc), BF16)
            scratch["rx" + name] = (lead + (2, rr, cc), BF16)
            scratch["rz" + name] = (lead + (nz - 1, rr // nz, cc), BF16)
        scratch["rv"] = ((3 + nz, 16, D), F32)
        scratch["vt"] = ((3, 16, D), F32)
        scratch["agr"] = dma((7, 6))
        scratch["agw"] = dma((4,))
        scratch["rsr"] = dma((3 + PAIRS, 5))
        scratch["vr"] = dma((4,))

    names = list(inputs) + list(outputs) + list(scratch)
    results = pl.pallas_call(
        functools.partial(kernel, s, names),
        out_shape=[jax.ShapeDtypeStruct(shape, dtype) for shape, dtype, _ in outputs.values()],
        in_specs=[spec for _, spec in inputs.values()],
        out_specs=[spec for _, _, spec in outputs.values()],
        scratch_shapes=[pltpu.VMEM(*v) if isinstance(v, tuple) else v for v in scratch.values()],
        compiler_params=pltpu.CompilerParams(
            collective_id=0, has_side_effects=True, vmem_limit_bytes=64 * 1024 * 1024 - 65536
        ),
        name="layer",
    )(*[a for a, _ in inputs.values()])
    o = types.SimpleNamespace(**dict(zip(outputs, results)))
    if exchange:
        bulk = ["py", "cy", "pdx", "cdx", "ogq", "ogk", "ogv", "ogo", "ogu", "ogd"]
        shapes = [jax.ShapeDtypeStruct(outputs[k][0], outputs[k][1]) for k in bulk]
        vectors = [jax.ShapeDtypeStruct((1, n), F32) for n in [s.r] * 5 + [1, s.rf]]
        done = pl.pallas_call(
            functools.partial(finish, len(bulk)),
            out_shape=shapes + vectors,
            in_specs=[vmem] + [any_spec] * len(bulk),
            out_specs=[any_spec] * len(bulk) + [vmem] * len(vectors),
            scratch_shapes=[pltpu.VMEM(v.shape, v.dtype) for v in shapes] + [dma((2, len(bulk)))],
            name="finish",
        )(o.ov, *[getattr(o, k) for k in bulk])
        for k, v in zip(bulk, done):
            setattr(o, k, v)
        *vec, loss, up_vec = [v.reshape(-1) for v in done[len(bulk) :]]
        loss = loss.reshape(())
        mats = [o.ogq, o.ogk, o.ogv, o.ogo, o.ogu, o.ogd]
    else:
        three = o.fgq.reshape(PAIRS, D, 3, LANES).transpose(2, 1, 0, 3).reshape(3, D, D)
        whole = [three[0], three[1], three[2], o.fgo, o.fgu, o.fgd]
        whole = [w.reshape(-1, w.shape[-1]).astype(F32) for w in whole]
        parts = [o.ov[i] for i in range(5)] + [o.ov[8:12].reshape(FF)]
        *mats, v0, v1, v2, v3, v4, up_vec = [
            lax.psum_scatter(w, both, scatter_dimension=0, tiled=True) for w in whole + parts
        ]
        vec = [v0, v1, v2, v3, v4]
        loss = lax.psum(jnp.sum(o.ov[5]), both) / (tokens * D)
    return (
        o.py,
        o.cy,
        loss,
        o.pdx,
        o.cdx,
        vec[0],
        vec[1],
        mats[0],
        mats[1],
        mats[2],
        mats[3],
        vec[2],
        vec[3],
        mats[4],
        up_vec,
        mats[5],
        vec[4],
    )


def solution(mesh):
    rows = P("dp", "cont", None)
    conts = P("dp", "cont", None, None)
    vector = P(("dp", "cont"))
    matrix = P(("dp", "cont"), None)
    return jax.shard_map(
        functools.partial(layer, mesh),
        mesh=mesh,
        in_specs=(rows, conts, rows, conts, conts, P("dp", "cont"), P())
        + (vector, vector, matrix, matrix, matrix, matrix, vector, vector, matrix, vector, matrix, vector),
        out_specs=(rows, conts, P(), rows, conts)
        + (vector, vector, matrix, matrix, matrix, matrix, vector, vector, matrix, vector, matrix, vector),
        check_vma=False,
    )
```

```python
import functools
import types

import jax
import jax.numpy as jnp
from jax import lax
from jax.experimental import pallas as pl
from jax.experimental.pallas import tpu as pltpu
from jax.sharding import PartitionSpec as P

D = 512
HEADS = 8
HEAD_DIM = 64
FF = 2048
BLOCK = 16
CONT_LEN = 128
COARSE = CONT_LEN // BLOCK
PAIRS = HEADS // 2
EPS = 1e-5
SCORE = HEAD_DIM**-0.5
LOG2E = 1.4426950408889634
AWAY = -1e30
F32 = jnp.float32
BF16 = jnp.bfloat16
MESH = pl.DeviceIdType.MESH
LANES = 128
SENDS = 24
EARLY = 2


def nn(a, b):
    return jnp.dot(a, b, preferred_element_type=F32)


def nt(a, b):
    return lax.dot_general(a, b, (((1,), (1,)), ((), ())), preferred_element_type=F32)


def tn(a, b):
    return lax.dot_general(a, b, (((0,), (0,)), ((), ())), preferred_element_type=F32)


def iota(shape, dim):
    return lax.broadcasted_iota(jnp.int32, shape, dim)


def norm_stats(x):
    center = x - jnp.mean(x, -1, keepdims=True)
    rstd = lax.rsqrt(jnp.mean(center * center, -1, keepdims=True) + EPS)
    return center * rstd, rstd


def norm_back(xhat, rstd, gain, dn):
    dxhat = dn * gain
    mean_one = jnp.mean(dxhat, -1, keepdims=True)
    mean_two = jnp.mean(dxhat * xhat, -1, keepdims=True)
    return rstd * (dxhat - mean_one - xhat * mean_two)


def colsum(x):
    return jnp.sum(x, 0, keepdims=True)


class Sizes:
    def __init__(self, groups, prompt, conts, nz, exchange, ndev):
        self.groups = groups
        self.prompt = prompt
        self.conts = conts
        self.nz = nz
        self.exchange = exchange
        self.ndev = ndev
        self.nb = prompt // CONT_LEN
        self.tb = self.nb + conts
        self.rows_g = self.tb * CONT_LEN
        self.rows = groups * self.rows_g
        self.nl = 48 * self.tb
        self.blocks = groups * self.tb
        self.far_own = prompt // COARSE
        self.far = self.far_own * nz
        self.r = D // ndev
        self.rf = FF // ndev


def kernel(s, names, *refs):
    r = types.SimpleNamespace(**dict(zip(names, refs)))
    z = lax.axis_index("cont")
    dp = lax.axis_index("dp")
    zs = [lax.rem(z + d, s.nz) for d in range(1, s.nz)]
    pending = {}
    sent = [0]

    def remote(src, dst, ssem, rsem, dev):
        return pltpu.make_async_remote_copy(
            src_ref=src, dst_ref=dst, send_sem=ssem, recv_sem=rsem, device_id=dev, device_id_type=MESH
        )

    def send(src, dst, rsem, dev, cond=None):
        slot = sent[0] % SENDS
        sent[0] += 1
        if slot in pending:
            left(slot)
        copy = remote(src, dst, r.ss.at[slot], rsem, dev)
        on(cond, copy.start)
        pending[slot] = (cond, copy)

    def on(cond, act):
        if cond is None:
            act()
        else:
            pl.when(cond)(act)

    def left(slot):
        cond, copy = pending[slot]
        on(cond, copy.wait_send)

    def line_send(src, dst, rsem):
        for d, zz in enumerate(zs):
            cond = None
            if s.exchange and d != 1:
                cond = z != (s.nz - 1 if d == 0 else 0)
            send(src, dst, rsem, (dp, zz), cond)

    middle = (z == 1) | (z == 2)
    far_end = jnp.clip(3 * (z - 1), 0, s.nz - 1)

    def line_relay(piece, rsem):
        if s.exchange:
            ref = piece(3 - far_end)
            send(ref, ref, rsem, (dp, far_end), middle)

    def wait_recv(ref, rsem):
        pltpu.make_async_copy(ref, ref, rsem).wait()

    local_count = [0]
    outs = []

    def local(pairs, whole=None):
        sem = r.lsem.at[local_count[0]]
        local_count[0] += 1
        copies = [pltpu.make_async_copy(src, dst, sem) for src, dst in pairs]
        for copy in copies:
            copy.start()
        return copies[0] if whole is None else pltpu.make_async_copy(whole, whole, sem)

    def row_pairs(prompt, cont, rows):
        out = []
        for g in range(s.groups):
            base = g * s.rows_g
            out.append((prompt.at[g], rows.at[pl.ds(base, s.prompt)]))
            for c in range(s.conts):
                out.append((cont.at[g, c], rows.at[pl.ds(base + s.prompt + c * CONT_LEN, CONT_LEN)]))
        return out

    if s.exchange:
        core = lax.rem(dp, 2)
        ix = lax.rem(dp // 2, 2)
        iy = dp // 4
        sib = dp + 1 - 2 * core
        xn = dp + 2 - 4 * ix
        yn = dp + 4 - 8 * iy
        cell = dp // 2
        cell_x = cell + 1 - 2 * ix
        cell_y = cell + 2 - 4 * iy
        cell_d = cell_x + cell_y - cell
        sibcore = 1 - core
        me = dp * s.nz + z

        def view(k, a, n, part=None):
            if k == 0:
                return r.tiles.at[pl.ds(a, n)]
            ref, rows = (r.w4, s.r) if k < 5 else (r.wu, s.r) if k == 5 else (r.wd, s.rf)
            place = pl.ds(pl.multiple_of(a * rows, rows), n * rows)
            width = ref.shape[-1]
            cols = pl.ds(0, width) if part is None else pl.ds(part * (width // 2), width // 2)
            if k < 5:
                return ref.at[(1, 2, 0, 3)[k - 1], place, cols]
            return ref.at[place, cols]

        def shard(c, co, zz):
            return (c * 2 + co) * s.nz + zz

        def ag_sem(k, kind, wave):
            return r.agw.at[kind - 1] if wave and 0 < kind < 5 else r.agr.at[k, kind]

        def ag_move(k, kind, a, n, dev, part=None, wave=0):
            v = view(k, a, n, part)
            send(v, v, ag_sem(k, kind, wave), dev)

        def ag_got(k, kind, n, part=None, wave=0):
            wait_recv(view(k, 0, n, part), ag_sem(k, kind, wave))

        def ag_z(k):
            own = view(k, me, 1)
            line_send(own, own, ag_sem(k, 0, 0))

        def ag_out(k, wave, starts, n):
            if wave == 1 or n > 1:
                ag_got(k, 0, s.nz - 1)
                line_relay(lambda zz: view(k, dp * s.nz + zz, 1), ag_sem(k, 0, 0))
            for zz in starts:
                a = shard(cell, core, zz)
                ag_move(k, 1, a, n, (xn, z), None, wave)
                ag_move(k, 2, a, n, (yn, z), None, wave)
            for zz in starts:
                ag_move(k, 5, shard(cell, core, zz), n, (sib, z))

        def ag_pass(k, wave, starts, n):
            total = len(starts) * n
            ag_got(k, 1, total, None, wave)
            for zz in starts:
                ag_move(k, 3, shard(cell_x, core, zz), n, (yn, z), 0, wave)
            ag_got(k, 2, total, None, wave)
            if k > 0:
                for zz in starts:
                    ag_move(k, 4, shard(cell_y, core, zz), n, (xn, z), 1, wave)
            for zz in starts:
                ag_move(k, 5, shard(cell_x, core, zz), n, (sib, z))
                ag_move(k, 5, shard(cell_y, core, zz), n, (sib, z))

        def ag_last(k, wave, starts, n):
            total = len(starts) * n
            ag_got(k, 3, total, 0, wave)
            if k > 0:
                ag_got(k, 4, total, 1, wave)
            for zz in starts:
                ag_move(k, 5, shard(cell_d, core, zz), n, (sib, z))

        def ag1(k):
            ag_out(k, 0, [0], s.nz)

        def ag2(k):
            ag_pass(k, 0, [0], s.nz)

        def ag3(k):
            ag_last(k, 0, [0], s.nz)

        def ag4(k):
            ag_got(k, 5, 4 * s.nz)

        grads = [(r.gd.at[...], r.rcd, r.rdd, r.rxd, r.rzd), (r.gu.at[...], r.rcu, r.rdu, r.rxu, r.rzu),
                 (r.go.at[...], r.rco, r.rdo, r.rxo, r.rzo)]
        for p in range(PAIRS):
            grads.append((r.gq.at[p], r.rcq.at[p], r.rdq.at[p], r.rxq.at[p], r.rzq.at[p]))

        def rs0(k):
            g, rc, _, _, _ = grads[k]
            send(g.at[:, sibcore], rc, r.rsr.at[k, 0], (sib, z))

        def add_to(g, c, lo, n, term):
            place = (c, core, pl.ds(lo, n))
            g[place] = (g[place].astype(F32) + term.astype(F32)).astype(BF16) if term.dtype == F32 else g[place] + term

        def rs1(k):
            g, rc, rd, _, _ = grads[k]
            m = g.shape[2]
            wait_recv(rc, r.rsr.at[k, 0])
            add_to(g, cell_d, 0, m, rc[cell_d])
            mh = m // 2
            send(g.at[cell_d, core, pl.ds(0, mh)], rd.at[0], r.rsr.at[k, 1], (yn, z))
            send(g.at[cell_d, core, pl.ds(mh, mh)], rd.at[1], r.rsr.at[k, 2], (xn, z))
            for c in (cell_x, cell_y, cell):
                add_to(g, c, 0, m, rc[c])

        def rs2(k):
            g, _, rd, rx, _ = grads[k]
            mh = g.shape[2] // 2
            wait_recv(rd.at[0], r.rsr.at[k, 1])
            add_to(g, cell_x, 0, mh, rd[0])
            send(g.at[cell_x, core], rx.at[0], r.rsr.at[k, 3], (xn, z))
            wait_recv(rd.at[1], r.rsr.at[k, 2])
            add_to(g, cell_y, mh, mh, rd[1])
            send(g.at[cell_y, core], rx.at[1], r.rsr.at[k, 3], (yn, z))

        def piece(g, zz):
            n = g.shape[2] // s.nz
            return pl.ds(pl.multiple_of(zz * n, n), n)

        def rs3(k):
            g, _, _, rx, rz = grads[k]
            wait_recv(rx, r.rsr.at[k, 3])
            add_to(g, cell, 0, g.shape[2], rx[0].astype(F32) + rx[1].astype(F32))
            for d, zz in enumerate(zs):
                send(g.at[cell, core, piece(g, zz)], rz.at[d], r.rsr.at[k, 4], (dp, zz))

        def rs4(k):
            g, _, _, _, rz = grads[k]
            wait_recv(rz, r.rsr.at[k, 4])
            total = g[cell, core, piece(g, z)].astype(F32)
            for d in range(s.nz - 1):
                total = total + rz[d].astype(F32)
            if k < 3:
                held, out = ((r.hgd, r.ogd), (r.hgu, r.ogu), (r.hgo, r.ogo))[k]
                held[...] = total
                outs.append(local([(held, out)]))
            else:
                lanes = pl.ds((k - 3) * LANES, LANES)
                for j, (held, out) in enumerate(((r.hgq, r.ogq), (r.hgk, r.ogk), (r.hgv, r.ogv))):
                    held[:, lanes] = total[:, j * LANES : (j + 1) * LANES]
                    if k == 2 + PAIRS:
                        outs.append(local([(held, out)]))
    else:

        def nothing(*_):
            return None

        ag1 = ag2 = ag3 = ag4 = ag_z = ag_out = ag_pass = ag_last = nothing
        rs0 = rs1 = rs2 = rs3 = rs4 = nothing

    scalars_in = [local([(r.lens_in, r.lens)]), local([(r.ls_in, r.ls)])]
    if s.exchange:
        vectors_in = (r.v1g, r.v1b, r.v2g, r.v2b, r.vdb)
        scalars_in.append(local([(v, r.small.at[i]) for i, v in enumerate(vectors_in)], r.small))
        scalars_in.append(local([(r.vub, r.smallup)]))
        own_rows = pl.ds(pl.multiple_of(me * s.r, s.r), s.r)
        weights_in = [
            local([(w, r.w4.at[j, own_rows]) for j, w in enumerate((r.wq, r.wk, r.wv, r.wo))], r.w4.at[:, own_rows]),
            local([(r.wup, view(5, me, 1))]),
            local([(r.wdn, view(6, me, 1))]),
        ]
    else:
        weights_in = [local([(w, r.w4.at[j]) for j, w in enumerate((r.wq, r.wk, r.wv, r.wo))], r.w4)]
        weights_in += [local([(r.wup, r.wu)]), local([(r.wdn, r.wd)])]
    barrier = pltpu.get_barrier_semaphore()
    partners = [(dp, zz) for zz in zs]
    if s.exchange:
        partners += [(sib, z), (xn, z), (yn, z)]
    for dev in partners:
        pl.semaphore_signal(barrier, inc=1, device_id=dev, device_id_type=MESH)
    x_in = [local(row_pairs(r.px, r.cx, r.x), r.x)]
    teach_pairs = [(r.te.at[g, c], r.teach.at[g * s.conts + c]) for g in range(s.groups) for c in range(s.conts)]
    later_in = [local(row_pairs(r.pdy, r.cdy, r.dy), r.dy), local(teach_pairs, r.teach)]

    for copy in scalars_in:
        copy.wait()
    if s.exchange:
        r.build[...] = jnp.zeros_like(r.build)
        for i in range(5):
            r.build[pl.ds(i, 1), pl.ds(0, s.r)] = r.small[i].astype(F32)
        r.build[pl.ds(5, 1), pl.ds(0, s.rf)] = r.smallup[...].astype(F32)
        own_tokens = 0
        for g in range(s.groups):
            for c in range(s.conts):
                own_tokens = own_tokens + r.lens[c, g]
        tile = r.build[...]
        row = iota((8, LANES), 0)
        placed = jnp.where(
            row < 5,
            pltpu.roll(tile, lax.rem(me, LANES // s.r) * s.r, 1),
            pltpu.roll(tile, lax.rem(me, LANES // s.rf) * s.rf, 1),
        )
        r.tiles[me] = jnp.where(row == 6, own_tokens.astype(F32), placed)

    for copy in weights_in:
        copy.wait()
    pl.semaphore_wait(barrier, len(partners))
    first, rest = [z], zs
    ag_z(0)
    ag_z(1)
    ag_out(1, 0, first, 1)
    ag_z(2)

    ri = iota((64, CONT_LEN), 0)
    ci = iota((64, CONT_LEN), 1)
    coarse_ci = jnp.where(ri < 32, ci >> 1, jnp.where(ri < 48, ci >> 2, ci >> 3))
    position = jnp.where(ri < 16, ri, jnp.where(ri < 32, ri + 16, jnp.where(ri < 48, ri - 32, ri - 48)))
    r.poolk[...] = jnp.where(coarse_ci == position, 1.0, 0.0).astype(BF16)
    position = jnp.where(ri < 48, position + 16, position)
    r.poolq[...] = jnp.where(coarse_ci == position, 1.0, 0.0).astype(BF16)
    r.pq3[...] = jnp.zeros_like(r.pq3)
    r.pk3[...] = jnp.zeros_like(r.pk3)
    for b in range(s.tb):
        cols = pl.ds(b * CONT_LEN, CONT_LEN)
        for first_row in (0, s.nl):
            r.pq3[pl.ds(first_row + b * 48, 48), cols] = r.poolq[pl.ds(0, 48)]
        r.pq3[pl.ds(2 * s.nl + b * BLOCK, BLOCK), cols] = r.poolq[pl.ds(48, BLOCK)]
        r.pk3[pl.ds(b * 48, 48), cols] = r.poolk[pl.ds(0, 48)]
    ri = iota((CONT_LEN, CONT_LEN), 0)
    ci = iota((CONT_LEN, CONT_LEN), 1)
    bi, bj = ri >> 4, ci >> 4
    near = ((bi == bj) & (ci <= ri)) | (((bi & 1) == 1) & (bj == bi - 1))
    near = jnp.where(near, 0.0, AWAY)
    r.bias0[pl.ds(0, CONT_LEN)] = near
    r.bias0[pl.ds(CONT_LEN, CONT_LEN)] = near
    ri = iota((2 * s.nl, s.nl), 0)
    ri = jnp.where(ri >= s.nl, ri - s.nl, ri)
    r.bias1[...] = jnp.where((ri >> 4) == (iota((2 * s.nl, s.nl), 1) >> 4), 0.0, AWAY)
    nq = s.tb * BLOCK
    blk = lax.rem(iota((2 * nq, s.far), 0), nq) >> 4
    limit = jnp.where(blk >= s.nb, s.far, BLOCK * (z * s.nb + blk))
    r.biasf[...] = jnp.where(iota((2 * nq, s.far), 1) < limit, 0.0, AWAY)
    scale_rows = iota((64, D), 0)
    mean_scale = jnp.where(scale_rows < 32, 0.5, jnp.where(scale_rows < 48, 0.25, 0.125))
    r.vg[...] = jnp.zeros_like(r.vg)

    ag_pass(1, 0, first, 1)
    ag1(0)
    ag_out(1, 1, rest, 1)
    ag_z(3)
    ag_last(1, 0, first, 1)
    ag1(2)
    ag_z(4)
    ag_z(5)
    ag2(0)
    ag_pass(1, 1, rest, 1)
    ag1(3)
    ag3(0)
    ag_z(6)
    ag_last(1, 1, rest, 1)
    ag2(2)
    ag4(0)
    if s.exchange:
        count = 8
        for k in range(s.ndev // count):
            part = jnp.sum(r.tiles[pl.ds(k * count, count)], 0)
            r.vec[:, pl.ds(k * LANES, LANES)] = part
        for k in range(s.ndev // 2):
            part = r.tiles[2 * k] + r.tiles[2 * k + 1]
            r.upb[:, pl.ds(k * LANES, LANES)] = part[5:6]
    else:
        r.vec[...] = r.vecs[...]
        r.upb[...] = r.upbs[...]

    def vec(i):
        return r.vec[pl.ds(i, 1), :]

    token_row = r.vec[pl.ds(6, 1), pl.ds(0, LANES)]
    for k in range(1, D // LANES):
        token_row = token_row + r.vec[pl.ds(6, 1), pl.ds(k * LANES, LANES)]
    token_row = jnp.concatenate([token_row] * (D // LANES), 1)

    def length_of(g, b):
        if isinstance(b, int):
            return CONT_LEN if b < s.nb else r.lens[b - s.nb, g]
        c = jnp.clip(b - s.nb, 0, s.conts - 1)
        return jnp.where(b >= s.nb, r.lens[c, g], CONT_LEN)

    def block_rows(t):
        if isinstance(t, int):
            return pl.ds(t * CONT_LEN, CONT_LEN)
        return pl.ds(pl.multiple_of(t * CONT_LEN, CONT_LEN), CONT_LEN)

    for copy in x_in:
        copy.wait()

    def norm_one(i, carry):
        rows = block_rows(i)
        xhat, _ = norm_stats(r.x[rows].astype(F32))
        r.n1[rows] = (xhat * vec(0) + vec(1)).astype(BF16)
        return carry

    lax.fori_loop(0, s.blocks, norm_one, 0)
    ag2(3)
    ag4(1)

    def project(j, out, pools):
        for g in range(s.groups):
            rows = pl.ds(g * s.rows_g, s.rows_g)
            value = nn(r.n1[rows], r.w4[j])
            parts = [value[: s.prompt]]
            for c in range(s.conts):
                lo = s.prompt + c * CONT_LEN
                part = value[lo : lo + CONT_LEN]
                if j > 0:
                    part = jnp.where(iota((CONT_LEN, D), 0) < r.lens[c, g], part, 0.0)
                parts.append(part)
            value = jnp.concatenate(parts, 0).astype(BF16)
            out[rows] = value
            pool, pooled, scale = pools
            for b in range(s.tb):
                pooled[g * s.tb + b] = (nn(pool[...], value[b * CONT_LEN : (b + 1) * CONT_LEN]) * scale).astype(BF16)

    project(1, r.k, (r.poolk, r.kl, mean_scale))
    ag3(2)
    ag1(4)
    ag1(5)
    ag4(2)
    project(2, r.v, (r.poolk, r.vl, 1.0))
    for g in range(s.groups):
        for b in range(s.nb):
            place = pl.ds(pl.multiple_of(z * s.far_own + b * BLOCK, BLOCK), BLOCK)
            r.fkv[0, g, place] = r.kl[g * s.tb + b, pl.ds(48, BLOCK)]
            r.fkv[1, g, place] = r.vl[g * s.tb + b, pl.ds(48, BLOCK)]

    def far_rows(zz):
        return r.fkv.at[:, :, pl.ds(pl.multiple_of(zz * s.far_own, s.far_own), s.far_own)]

    line_send(far_rows(z), far_rows(z), r.fr.at[0])

    def far_got():
        wait_recv(r.fkv.at[:, :, pl.ds(0, s.far - s.far_own)], r.fr.at[0])

    ag3(3)
    ag2(4)
    ag1(6)
    ag4(3)
    project(0, r.q, (r.poolq, r.ql, mean_scale))

    def two(a):
        low = iota(a.shape, 1) < HEAD_DIM
        zero = jnp.zeros_like(a)
        return jnp.concatenate([jnp.where(low, a, zero), jnp.where(low, zero, a)], 0)

    def pick(a):
        n = a.shape[0] // 2
        return jnp.where(iota((n, LANES), 1) < HEAD_DIM, a[:n], a[n:])

    def counts(length):
        i0 = iota((CONT_LEN, LANES), 0)
        counts0 = jnp.where(i0 < length, 1.0, 0.0).astype(BF16)
        i1 = iota((48, LANES), 0)
        first = jnp.where(i1 < 16, 2 * i1, jnp.where(i1 < 32, 2 * (i1 + 16), 4 * (i1 - 32)))
        width = jnp.where(i1 < 32, 2, 4)
        counts1 = jnp.clip(length - first, 0, width).astype(F32).astype(BF16)
        return counts0, counts1

    def pair_lanes(p):
        return pl.ds(p * LANES, LANES)

    low48 = pl.ds(0, 48)
    far16 = pl.ds(48, BLOCK)

    def near(t, carry):
        g, b = t // s.tb, lax.rem(t, s.tb)
        rows = block_rows(t)
        counts0, _ = counts(length_of(g, b))
        for p in range(PAIRS):
            lanes = pair_lanes(p)
            e0 = jnp.exp2(nt(two(r.q[rows, lanes]), r.k[rows, lanes]) * (SCORE * LOG2E) + r.bias0[...])
            e0 = e0.astype(BF16)
            r.e0[t * PAIRS + p] = e0
            t0 = nn(e0, jnp.concatenate([r.v[rows, lanes], counts0], 1))
            r.num[rows, lanes] = pick(t0[:, :LANES])
            r.den[rows, lanes] = pick(t0[:, LANES:])
        return carry

    eight = jnp.full((s.far, LANES), float(COARSE), BF16)

    def gathered(ref, g, lanes, part=None):
        part = far16 if part is None else part
        return jnp.concatenate([ref[g * s.tb + b, part, lanes] for b in range(s.tb)], 0)

    def coarse_values(g, lanes):
        widths = jnp.concatenate([counts(length_of(g, b))[1] for b in range(s.tb)], 0)
        return jnp.concatenate([gathered(r.vl, g, lanes, low48), widths], 1)

    def group_rows(g):
        if isinstance(g, int):
            return pl.ds(g * s.rows_g, s.rows_g)
        return pl.ds(pl.multiple_of(g * s.rows_g, CONT_LEN), s.rows_g)

    def coarse_forward(g):
        rows = group_rows(g)
        for p in range(PAIRS):
            lanes = pair_lanes(p)
            e1 = nt(two(gathered(r.ql, g, lanes, low48)), gathered(r.kl, g, lanes, low48))
            e1 = jnp.exp2(e1 * (SCORE * LOG2E) + r.bias1[...]).astype(BF16)
            r.e1[g, p] = e1
            t1 = nn(e1, coarse_values(g, lanes))
            t1 = jnp.concatenate([pick(t1[:, :LANES]), pick(t1[:, LANES:])], 1)
            high = t1.astype(BF16)
            both = jnp.concatenate([high, (t1 - high.astype(F32)).astype(BF16)], 0)
            t1 = tn(r.pq3[pl.ds(0, 2 * s.nl)], both)
            r.num[rows, lanes] += t1[:, :LANES]
            r.den[rows, lanes] += t1[:, LANES:]

    def repeat_rows(a):
        n = a.shape[0]
        return jnp.broadcast_to(a[:, None, :], (n, COARSE, LANES)).reshape(n * COARSE, LANES)

    def far_forward(g):
        rows = pl.ds(g * s.rows_g, s.rows_g)
        for p in range(PAIRS):
            lanes = pair_lanes(p)
            ef = nt(two(gathered(r.ql, g, lanes)), r.fkv[0, g, :, lanes]) * (SCORE * LOG2E) + r.biasf[...]
            ef = jnp.exp2(ef).astype(BF16)
            r.ef[g, p] = ef
            total = nn(ef, jnp.concatenate([r.fkv[1, g, :, lanes], eight], 1))
            denominator = r.den[rows, lanes] + repeat_rows(pick(total[:, LANES:]))
            numerator = r.num[rows, lanes] + repeat_rows(pick(total[:, :LANES]))
            r.den[rows, lanes] = denominator
            r.att[rows, lanes] = (numerator / denominator).astype(BF16)

    lax.fori_loop(0, s.tb, near, 0)
    ag2(5)
    ag3(4)
    ag2(6)
    if s.exchange:
        on(middle, far_got)
    line_relay(far_rows, r.fr.at[0])
    coarse_forward(0)
    lax.fori_loop(s.tb, s.blocks, near, 0)
    for g in range(1, s.groups):
        coarse_forward(g)
    ag3(5)
    on(jnp.logical_not(middle) if s.exchange else None, far_got)
    for g in range(s.groups):
        far_forward(g)
    ag4(4)
    ag3(6)

    for copy in later_in:
        copy.wait()
    for g in range(s.groups):
        rows = pl.ds(g * s.rows_g, s.rows_g)
        mixed = r.x[rows].astype(F32) + nn(r.att[rows], r.w4[3])
        r.mix[rows] = mixed
        xhat, _ = norm_stats(mixed)
        r.n2[rows] = (xhat * vec(2) + vec(3)).astype(BF16)
    ag4(5)
    for g in range(s.groups):
        rows = pl.ds(g * s.rows_g, s.rows_g)
        for n in range(FF // D):
            cols = pl.ds(n * D, D)
            pre = nn(r.n2[rows], r.wu[:, cols]) + r.upb[:, cols]
            r.h[rows, cols] = jnp.maximum(pre, 0.0).astype(BF16)
    ag4(6)
    extra = 2.0 * r.ls[0, 0] / (token_row * float(D))
    for g in range(s.groups):
        base = g * s.rows_g
        rows = pl.ds(base, s.rows_g)
        y = r.mix[rows] + nn(r.h[rows], r.wd[...]) + vec(4)
        r.y[rows] = y.astype(BF16)
        gy = r.dy[rows].astype(F32)
        parts = [gy[: s.prompt]]
        for c in range(s.conts):
            lo = s.prompt + c * CONT_LEN
            keep = iota((CONT_LEN, D), 0) < r.lens[c, g]
            diff = jnp.where(keep, y[lo : lo + CONT_LEN] - r.teach[g * s.conts + c].astype(F32), 0.0)
            r.vg[pl.ds(5, 1), :] += colsum(diff * diff)
            parts.append(gy[lo : lo + CONT_LEN] + extra * diff)
        gy = jnp.concatenate(parts, 0)
        r.gy[rows] = gy
        r.gyb[rows] = gy.astype(BF16)
        r.vg[pl.ds(4, 1), :] += colsum(gy)

    outs.append(local([(b, a) for a, b in row_pairs(r.py, r.cy, r.y)], r.y))

    for n in range(FF // D):
        cols = pl.ds(n * D, D)
        r.gd[n] = tn(r.h[:, cols], r.gyb[...]).astype(BF16).reshape(2, FF // 8, D)
    rs0(0)
    for n in range(FF // D):
        cols = pl.ds(n * D, D)
        for g in range(s.groups):
            rows = pl.ds(g * s.rows_g, s.rows_g)
            dh = nt(r.gyb[rows], r.wd[cols])
            dpre = jnp.where(r.h[rows, cols] > 0, dh, 0.0).astype(BF16)
            r.h[rows, cols] = dpre
            r.vg[pl.ds(8 + n, 1), :] += colsum(dpre.astype(F32))
    rs1(0)
    for g in range(s.groups):
        rows = pl.ds(g * s.rows_g, s.rows_g)
        dn2 = nt(r.h[rows], r.wu[...])
        xhat, rstd = norm_stats(r.mix[rows])
        r.vg[pl.ds(2, 1), :] += colsum(dn2 * xhat)
        r.vg[pl.ds(3, 1), :] += colsum(dn2)
        dmixed = r.gy[rows] + norm_back(xhat, rstd, vec(2), dn2)
        r.gy[rows] = dmixed
        r.gyb[rows] = dmixed.astype(BF16)
    for g in range(s.groups):
        rows = pl.ds(g * s.rows_g, s.rows_g)
        dnum = nt(r.gyb[rows], r.w4[3]) / r.den[rows]
        r.dnum[rows] = dnum.astype(BF16)
        r.xo[rows] = (-dnum * r.att[rows].astype(F32)).astype(BF16)
        for b in range(s.tb):
            t = g * s.tb + b
            for ref, fine in ((r.dnl, r.dnum), (r.xol, r.xo)):
                pooled = nn(r.poolq[...], fine[block_rows(t)])
                high = pooled.astype(BF16)
                ref[0, t] = high
                ref[1, t] = (pooled - high.astype(F32)).astype(BF16)

    for g in range(s.groups):
        for p in range(PAIRS):
            lanes = pair_lanes(p)
            d3, x3, d3_low, x3_low = [two(gathered(ref.at[i], g, lanes)) for i in range(2) for ref in (r.dnl, r.xol)]
            x = jnp.concatenate([d3, x3, d3_low, x3_low], 1)
            vn = jnp.concatenate([r.fkv[1, g, :, lanes], eight], 1)
            ef = r.ef[g, p]
            kf = r.fkv[0, g, :, lanes]
            ds = nt(x, jnp.concatenate([vn, vn], 1)) * ef.astype(F32)
            ds = ds.astype(BF16)
            dq3 = (pick(nn(ds, kf)) * 0.125).astype(BF16)
            for b in range(s.tb):
                r.dql[g * s.tb + b, :, lanes] = dq3[b * BLOCK : (b + 1) * BLOCK]
            dkf = tn(ds, two(gathered(r.ql, g, lanes)))
            dvf = tn(ef, d3)
            r.df[g, 0, :, lanes] = dkf
            r.df[g, 1, :, lanes] = dvf
            r.dfs[g, 0, :, lanes] = dkf.astype(BF16)
            r.dfs[g, 1, :, lanes] = dvf.astype(BF16)

    def far_part(zz):
        return r.dfs.at[:, :, pl.ds(pl.multiple_of(zz * s.far_own, s.far_own), s.far_own)]

    for d, zz in enumerate(zs):
        send(far_part(zz), r.rf.at[d], r.fr.at[1], (dp, zz))
    rs2(0)
    for n in range(FF // D):
        cols = pl.ds(n * D, D)
        r.gu[:, :, :, cols] = tn(r.n2[...], r.h[:, cols]).astype(BF16).reshape(4, 2, D // 8, D)
    rs0(1)
    r.go[...] = tn(r.att[...], r.gyb[...]).astype(BF16).reshape(4, 2, D // 8, D)
    rs0(2)

    def pair_back(p, g):
        lanes = pair_lanes(p)
        e1 = r.e1[g, p]
        q1 = two(gathered(r.ql, g, lanes, low48))
        k1 = gathered(r.kl, g, lanes, low48)
        d1, x1, d1_low, x1_low = [
            two(gathered(ref.at[i], g, lanes, low48)) for i in range(2) for ref in (r.dnl, r.xol)
        ]
        vn1 = coarse_values(g, lanes)
        ds1 = nt(jnp.concatenate([d1, x1, d1_low, x1_low], 1), jnp.concatenate([vn1, vn1], 1))
        ds1 = (ds1 * e1.astype(F32)).astype(BF16)
        lr = lax.rem(iota((s.nl, LANES), 0), 48)
        level_scale = jnp.where(lr < 32, 0.5, 0.25)
        dql = (pick(nn(ds1, k1)) * level_scale).astype(BF16)
        dql = jnp.concatenate([dql] + [r.dql[g * s.tb + b, :, lanes] for b in range(s.tb)], 0)
        fine_q = tn(r.pq3[pl.ds(s.nl, s.nl + s.tb * BLOCK)], dql)
        dkl = (tn(ds1, q1) * level_scale).astype(BF16)
        dvl = tn(e1, d1).astype(BF16)
        fine = tn(r.pk3[...], jnp.concatenate([dkl, dvl], 1))
        for b in range(s.tb):
            t = g * s.tb + b
            rows = block_rows(t)
            length = length_of(g, b)
            counts0, _ = counts(length)
            q2 = two(r.q[rows, lanes])
            e0 = r.e0[t * PAIRS + p]
            dn2 = two(r.dnum[rows, lanes])
            x0 = jnp.concatenate([dn2, two(r.xo[rows, lanes])], 1)
            ds0 = nt(x0, jnp.concatenate([r.v[rows, lanes], counts0], 1)) * e0.astype(F32)
            ds0 = ds0.astype(BF16)
            part = slice(b * CONT_LEN, (b + 1) * CONT_LEN)
            dq = pick(nn(ds0, r.k[rows, lanes])) + fine_q[part]
            dkv = tn(jnp.concatenate([ds0, e0], 1), jnp.concatenate([q2, dn2], 1))
            dk = (dkv[:CONT_LEN, :LANES] + fine[part, :LANES]) * SCORE
            dv = dkv[CONT_LEN:, LANES:] + fine[part, LANES:]
            r.dqkv[p, rows, pl.ds(0, LANES)] = (dq * SCORE).astype(BF16)
            if b >= s.nb:
                keep = iota((CONT_LEN, LANES), 0) < length
                dk = jnp.where(keep, dk, 0.0)
                dv = jnp.where(keep, dv, 0.0)
            elif p < EARLY:
                r.num[rows, pl.ds(2 * p * LANES, LANES)] = dk
                r.num[rows, pl.ds((2 * p + 1) * LANES, LANES)] = dv
                continue
            else:
                far_k, far_v = far_terms(p, g, b)
                dk = dk + far_k
                dv = dv + far_v
            r.dqkv[p, rows, pl.ds(LANES, LANES)] = dk.astype(BF16)
            r.dqkv[p, rows, pl.ds(2 * LANES, LANES)] = dv.astype(BF16)

    def far_terms(p, g, b):
        own = pl.ds(b * BLOCK, BLOCK)
        lanes = pair_lanes(p)
        return repeat_rows(r.ft[g, 0, own, lanes]), repeat_rows(r.ft[g, 1, own, lanes])

    def each_group(p):
        def body(g, carry):
            pair_back(p, g)
            return carry

        lax.fori_loop(0, s.groups, body, 0)

    rs1(1)
    each_group(0)
    rs1(2)
    each_group(1)
    rs3(0)
    wait_recv(r.rf, r.fr.at[1])
    own = pl.ds(pl.multiple_of(z * s.far_own, s.far_own), s.far_own)
    for g in range(s.groups):
        for i, scale in enumerate((SCORE / COARSE, 1.0)):
            total = r.df[g, i, own]
            for d in range(s.nz - 1):
                total = total + r.rf[d, g, i].astype(F32)
            r.ft[g, i] = total.astype(BF16).astype(F32) * scale
    def add_far(p):
        for g in range(s.groups):
            for b in range(s.nb):
                rows = block_rows(g * s.tb + b)
                far_k, far_v = far_terms(p, g, b)
                dk = r.num[rows, pl.ds(2 * p * LANES, LANES)] + far_k
                dv = r.num[rows, pl.ds((2 * p + 1) * LANES, LANES)] + far_v
                r.dqkv[p, rows, pl.ds(LANES, LANES)] = dk.astype(BF16)
                r.dqkv[p, rows, pl.ds(2 * LANES, LANES)] = dv.astype(BF16)

    def prompts_back(p):
        if p < EARLY:
            add_far(p)
        else:
            each_group(p)
        r.gq[p] = tn(r.n1[...], r.dqkv[p]).astype(BF16).reshape(4, 2, D // 8, 3 * LANES)

    def dn1_part(p, g):
        rows = pl.ds(g * s.rows_g, s.rows_g)
        w = jnp.concatenate([r.w4[j, :, pair_lanes(p)] for j in range(3)], 1)
        return nt(r.dqkv[p, rows], w)

    def dn1_add(p):
        for g in range(s.groups):
            rows = pl.ds(g * s.rows_g, s.rows_g)
            part = dn1_part(p, g)
            r.num[rows] = part if p == 0 else r.num[rows] + part

    prompts_back(0)
    rs0(3)
    rs2(1)
    prompts_back(1)
    rs0(4)
    rs2(2)
    rs1(3)
    dn1_add(0)
    dn1_add(1)
    rs1(4)
    prompts_back(2)
    rs0(5)
    rs4(0)
    dn1_add(2)
    rs1(5)
    prompts_back(3)
    rs0(6)
    rs3(1)
    rs2(3)
    rs3(2)
    rs2(4)

    for g in range(s.groups):
        rows = pl.ds(g * s.rows_g, s.rows_g)
        dn1 = r.num[rows] + dn1_part(PAIRS - 1, g)
        xhat, rstd = norm_stats(r.x[rows].astype(F32))
        r.vg[pl.ds(0, 1), :] += colsum(dn1 * xhat)
        r.vg[pl.ds(1, 1), :] += colsum(dn1)
        r.gy[rows] = r.gy[rows] + norm_back(xhat, rstd, vec(0), dn1)
        if g == 0:
            rs1(6)
            rs2(5)
            rs3(3)

    outs.append(local([(b, a) for a, b in row_pairs(r.pdx, r.cdx, r.gy)], r.gy))
    if s.exchange:

        def vsend(src, i, dev):
            send(src, r.rv.at[i], r.vr.at[i], dev)

        vsend(r.vg, 0, (sib, z))
        rs3(4)
        rs2(6)
        wait_recv(r.rv.at[0], r.vr.at[0])
        r.vt[0] = r.vg[...] + r.rv[0]
        vsend(r.vt.at[0], 1, (xn, z))
        rs3(5)
        wait_recv(r.rv.at[1], r.vr.at[1])
        r.vt[1] = r.vt[0] + r.rv[1]
        vsend(r.vt.at[1], 2, (yn, z))
        rs3(6)
        rs4(1)
        wait_recv(r.rv.at[2], r.vr.at[2])
        r.vt[2] = r.vt[1] + r.rv[2]
        for zz in zs:
            send(r.vt.at[2], r.rv.at[3 + z], r.vr.at[3], (dp, zz))
        rs4(2)
        rs4(3)
        rs4(4)
        rs4(5)
        rs4(6)
        wait_recv(r.rv.at[pl.ds(3, s.nz - 1)], r.vr.at[3])
        r.rv[3 + z] = r.vt[2]
        total = r.rv[3]
        for i in range(1, s.nz):
            total = total + r.rv[3 + i]
        loss = jnp.sum(total[5:6], 1, keepdims=True) / (token_row[:, :1] * float(D))
        mine = jnp.zeros((8, LANES), F32)
        per = LANES // s.r
        for k in range(D // LANES):
            mine = jnp.where(me // per == k, total[:8, k * LANES : (k + 1) * LANES], mine)
        mine = pltpu.roll(mine, lax.rem(LANES - lax.rem(me, per) * s.r, LANES), 1)
        per = LANES // s.rf
        up = jnp.zeros((1, LANES), F32)
        for k in range(FF // LANES):
            i, j = divmod(k, D // LANES)
            up = jnp.where(me // per == k, total[8 + i : 9 + i, j * LANES : (j + 1) * LANES], up)
        up = jnp.broadcast_to(up, (8, LANES))
        up = pltpu.roll(up, lax.rem(LANES - lax.rem(me, per) * s.rf, LANES), 1)
        row = iota((8, LANES), 0)
        r.hv[...] = jnp.where(row < 5, mine, jnp.where(row == 5, loss, up))
        outs.append(local([(r.hv, r.ov)]))
    else:
        r.ov[...] = r.vg[...]
        for src, dst in ((r.gq, r.fgq), (r.go, r.fgo), (r.gu, r.fgu), (r.gd, r.fgd)):
            outs.append(local([(src, dst)]))
    for copy in outs:
        copy.wait()
    for slot in pending:
        left(slot)


def finish(n_mats, n_vecs, *refs):
    ov = refs[0]
    srcs = refs[1 : 1 + n_mats]
    dsts = refs[1 + n_mats : 1 + 2 * n_mats + n_vecs]
    held = refs[1 + 2 * n_mats + n_vecs : -2]
    hov, sems = refs[-2:]
    first = pltpu.make_async_copy(ov, hov, sems.at[0, n_mats])
    first.start()
    reads = [pltpu.make_async_copy(a, b, sems.at[0, i]) for i, (a, b) in enumerate(zip(srcs, held))]
    writes = [pltpu.make_async_copy(a, b, sems.at[1, i]) for i, (a, b) in enumerate(zip(held, dsts))]
    for copy in reads:
        copy.start()
    first.wait()
    for i in range(n_vecs):
        out = held[n_mats + i]
        out[...] = hov[pl.ds(i, 1), pl.ds(0, out.shape[1])]
        writes[n_mats + i].start()
    for read, write in zip(reads, writes):
        read.wait()
        write.start()
    for copy in writes:
        copy.wait()


def layer(
    mesh,
    prompt_x,
    cont_x,
    prompt_dy,
    cont_dy,
    teacher,
    cont_lengths,
    loss_scale,
    norm1_gain,
    norm1_bias,
    w_query,
    w_key,
    w_value,
    w_out,
    norm2_gain,
    norm2_bias,
    w_up,
    up_bias,
    w_down,
    down_bias,
):
    nz, ndp = mesh.shape["cont"], mesh.shape["dp"]
    ndev = nz * ndp
    exchange = ndp == 8 and nz == 4
    groups, prompt = prompt_x.shape[:2]
    conts = cont_x.shape[1]
    s = Sizes(groups, prompt, conts, nz, exchange, ndev)
    both = ("dp", "cont")
    any_spec = pl.BlockSpec(memory_space=pl.ANY)
    vmem = pl.BlockSpec(memory_space=pltpu.VMEM)

    inputs = {
        "px": (prompt_x, any_spec),
        "cx": (cont_x, any_spec),
        "pdy": (prompt_dy, any_spec),
        "cdy": (cont_dy, any_spec),
        "te": (teacher, any_spec),
        "lens_in": (cont_lengths.T, any_spec),
        "ls_in": (loss_scale.reshape(1, 1), any_spec),
    }
    weights = {"wq": w_query, "wk": w_key, "wv": w_value, "wo": w_out, "wup": w_up, "wdn": w_down}
    vectors = {"v1g": norm1_gain, "v1b": norm1_bias, "v2g": norm2_gain, "v2b": norm2_bias, "vdb": down_bias}
    if exchange:
        for name, w in weights.items():
            inputs[name] = (w, any_spec)
        for name, v in vectors.items():
            inputs[name] = (v.reshape(1, -1), any_spec)
        inputs["vub"] = (up_bias.reshape(1, -1), any_spec)
    else:
        for name, w in weights.items():
            inputs[name] = (lax.all_gather(w, both, axis=0, tiled=True), any_spec)
        tokens = lax.psum(jnp.sum(cont_lengths).astype(F32), both)
        full = [lax.all_gather(v, both, axis=0, tiled=True).astype(F32) for v in vectors.values()]
        zero = jnp.zeros((D,), F32)
        inputs["vecs"] = (jnp.stack(full + [zero, jnp.full((D,), tokens / (D // LANES)), zero]), vmem)
        up_full = lax.all_gather(up_bias, both, axis=0, tiled=True).astype(F32)
        inputs["upbs"] = (up_full.reshape(1, FF), vmem)

    m, mf = D // 8, FF // 8
    outputs = {
        "py": (prompt_x.shape, BF16, any_spec),
        "cy": (cont_x.shape, BF16, any_spec),
        "pdx": (prompt_x.shape, F32, any_spec),
        "cdx": (cont_x.shape, F32, any_spec),
    }
    if exchange:
        for name in ("ogq", "ogk", "ogv", "ogo"):
            outputs[name] = ((s.r, D), F32, any_spec)
        outputs["ogu"] = ((s.r, FF), F32, any_spec)
        outputs["ogd"] = ((s.rf, D), F32, any_spec)
        outputs["ov"] = ((8, LANES), F32, any_spec)
    else:
        outputs["fgq"] = ((PAIRS, 4, 2, m, 3 * LANES), BF16, any_spec)
        outputs["fgo"] = ((4, 2, m, D), BF16, any_spec)
        outputs["fgu"] = ((4, 2, m, FF), BF16, any_spec)
        outputs["fgd"] = ((4, 2, mf, D), BF16, any_spec)
        outputs["ov"] = ((16, D), F32, vmem)

    rows, blocks = s.rows, s.blocks
    dma = pltpu.SemaphoreType.DMA
    scratch = {
        "w4": ((4, D, D), BF16),
        "wu": ((D, FF), BF16),
        "wd": ((FF, D), BF16),
        "vec": ((8, D), F32),
        "upb": ((1, FF), F32),
        "x": ((rows, D), BF16),
        "dy": ((rows, D), BF16),
        "teach": ((groups * conts, CONT_LEN, D), BF16),
        "y": ((rows, D), BF16),
        "n1": ((rows, D), BF16),
        "q": ((rows, D), BF16),
        "k": ((rows, D), BF16),
        "v": ((rows, D), BF16),
        "ql": ((blocks, 64, D), BF16),
        "kl": ((blocks, 64, D), BF16),
        "vl": ((blocks, 64, D), BF16),
        "fkv": ((2, groups, s.far, D), BF16),
        "poolk": ((64, CONT_LEN), BF16),
        "poolq": ((64, CONT_LEN), BF16),
        "pq3": ((2 * s.nl + s.tb * BLOCK, s.rows_g), BF16),
        "pk3": ((s.nl, s.rows_g), BF16),
        "bias0": ((2 * CONT_LEN, CONT_LEN), F32),
        "bias1": ((2 * s.nl, s.nl), F32),
        "biasf": ((2 * s.tb * BLOCK, s.far), F32),
        "e0": ((blocks * PAIRS, 2 * CONT_LEN, CONT_LEN), BF16),
        "e1": ((groups, PAIRS, 2 * s.nl, s.nl), BF16),
        "ef": ((groups, PAIRS, 2 * s.tb * BLOCK, s.far), BF16),
        "num": ((rows, D), F32),
        "att": ((rows, D), BF16),
        "den": ((rows, D), F32),
        "mix": ((rows, D), F32),
        "n2": ((rows, D), BF16),
        "h": ((rows, FF), BF16),
        "gy": ((rows, D), F32),
        "gyb": ((rows, D), BF16),
        "dnum": ((rows, D), BF16),
        "xo": ((rows, D), BF16),
        "dnl": ((2, blocks, 64, D), BF16),
        "xol": ((2, blocks, 64, D), BF16),
        "dql": ((blocks, BLOCK, D), BF16),
        "dqkv": ((PAIRS, rows, 3 * LANES), BF16),
        "df": ((groups, 2, s.far, D), F32),
        "dfs": ((groups, 2, s.far, D), BF16),
        "rf": ((nz - 1, groups, 2, s.far_own, D), BF16),
        "ft": ((groups, 2, s.far_own, D), F32),
        "vg": ((16, D), F32),
        "gq": ((PAIRS, 4, 2, m, 3 * LANES), BF16),
        "go": ((4, 2, m, D), BF16),
        "gu": ((4, 2, m, FF), BF16),
        "gd": ((4, 2, mf, D), BF16),
        "lens": pltpu.SMEM((conts, groups), jnp.int32),
        "ls": pltpu.SMEM((1, 1), F32),
        "lsem": dma((20,)),
        "ss": dma((SENDS,)),
        "fr": dma((2,)),
    }
    if exchange:
        scratch["tiles"] = ((ndev, 8, LANES), F32)
        scratch["build"] = ((8, LANES), F32)
        scratch["small"] = ((5, 1, s.r), BF16)
        scratch["smallup"] = ((1, s.rf), BF16)
        for name in ("q", "k", "v", "o"):
            scratch["hg" + name] = ((s.r, D), F32)
        scratch["hgu"] = ((s.r, FF), F32)
        scratch["hgd"] = ((s.rf, D), F32)
        scratch["hv"] = ((8, LANES), F32)
        for name, lead, rr, cc in (("q", (PAIRS,), m, 3 * LANES), ("o", (), m, D), ("u", (), m, FF), ("d", (), mf, D)):
            scratch["rc" + name] = (lead + (4, rr, cc), BF16)
            scratch["rd" + name] = (lead + (2, rr // 2, cc), BF16)
            scratch["rx" + name] = (lead + (2, rr, cc), BF16)
            scratch["rz" + name] = (lead + (nz - 1, rr // nz, cc), BF16)
        scratch["rv"] = ((3 + nz, 16, D), F32)
        scratch["vt"] = ((3, 16, D), F32)
        scratch["agr"] = dma((7, 6))
        scratch["agw"] = dma((4,))
        scratch["rsr"] = dma((3 + PAIRS, 5))
        scratch["vr"] = dma((4,))

    names = list(inputs) + list(outputs) + list(scratch)
    results = pl.pallas_call(
        functools.partial(kernel, s, names),
        out_shape=[jax.ShapeDtypeStruct(shape, dtype) for shape, dtype, _ in outputs.values()],
        in_specs=[spec for _, spec in inputs.values()],
        out_specs=[spec for _, _, spec in outputs.values()],
        scratch_shapes=[pltpu.VMEM(*v) if isinstance(v, tuple) else v for v in scratch.values()],
        compiler_params=pltpu.CompilerParams(
            collective_id=0, has_side_effects=True, vmem_limit_bytes=64 * 1024 * 1024 - 65536
        ),
        name="layer",
    )(*[a for a, _ in inputs.values()])
    o = types.SimpleNamespace(**dict(zip(outputs, results)))
    if exchange:
        bulk = ["py", "cy", "pdx", "cdx", "ogq", "ogk", "ogv", "ogo", "ogu", "ogd"]
        shapes = [jax.ShapeDtypeStruct(outputs[k][0], outputs[k][1]) for k in bulk]
        vectors = [jax.ShapeDtypeStruct((1, n), F32) for n in [s.r] * 5 + [1, s.rf]]
        done = pl.pallas_call(
            functools.partial(finish, len(bulk), len(vectors)),
            out_shape=shapes + vectors,
            in_specs=[any_spec] * (1 + len(bulk)),
            out_specs=[any_spec] * (len(bulk) + len(vectors)),
            scratch_shapes=[pltpu.VMEM(v.shape, v.dtype) for v in shapes + vectors]
            + [pltpu.VMEM((8, LANES), F32), dma((2, len(bulk) + len(vectors)))],
            name="finish",
        )(o.ov, *[getattr(o, k) for k in bulk])
        for k, v in zip(bulk, done):
            setattr(o, k, v)
        *vec, loss, up_vec = [v.reshape(-1) for v in done[len(bulk) :]]
        loss = loss.reshape(())
        mats = [o.ogq, o.ogk, o.ogv, o.ogo, o.ogu, o.ogd]
    else:
        three = o.fgq.reshape(PAIRS, D, 3, LANES).transpose(2, 1, 0, 3).reshape(3, D, D)
        whole = [three[0], three[1], three[2], o.fgo, o.fgu, o.fgd]
        whole = [w.reshape(-1, w.shape[-1]).astype(F32) for w in whole]
        parts = [o.ov[i] for i in range(5)] + [o.ov[8:12].reshape(FF)]
        *mats, v0, v1, v2, v3, v4, up_vec = [
            lax.psum_scatter(w, both, scatter_dimension=0, tiled=True) for w in whole + parts
        ]
        vec = [v0, v1, v2, v3, v4]
        loss = lax.psum(jnp.sum(o.ov[5]), both) / (tokens * D)
    return (
        o.py,
        o.cy,
        loss,
        o.pdx,
        o.cdx,
        vec[0],
        vec[1],
        mats[0],
        mats[1],
        mats[2],
        mats[3],
        vec[2],
        vec[3],
        mats[4],
        up_vec,
        mats[5],
        vec[4],
    )


def solution(mesh):
    rows = P("dp", "cont", None)
    conts = P("dp", "cont", None, None)
    vector = P(("dp", "cont"))
    matrix = P(("dp", "cont"), None)
    return jax.shard_map(
        functools.partial(layer, mesh),
        mesh=mesh,
        in_specs=(rows, conts, rows, conts, conts, P("dp", "cont"), P())
        + (vector, vector, matrix, matrix, matrix, matrix, vector, vector, matrix, vector, matrix, vector),
        out_specs=(rows, conts, P(), rows, conts)
        + (vector, vector, matrix, matrix, matrix, matrix, vector, vector, matrix, vector, matrix, vector),
        check_vma=False,
    )
```
